256 devices in a mesh: cnec: 8 (over y_lo, x), bus: 16 (over z, y_hi), act: 2 (over core).
Axes of the slice: x: 4, y: 4 (y_hi: 2, y_lo: 2; y = y_hi * 2 + y_lo), z: 8, core: 2. Of those that a mesh axis runs over, the one named last changes fastest.
Arguments:
- nodal_sensitivity: bfloat16 [4096, 131072], P('cnec', 'bus'), may hold values from -1 to 1, as said below
- shift_weight: float32 [131072], P('bus'), may hold values from 0 to 48, as said below
- bus_zone: int32 [131072], P('bus'), may hold values from 0 to 63, as said below
- branch_buses: int32 [2, 4096], replicated, may hold values from 0 to 131071, as said below
- switched_rows: int32 [64, 8], P('act'), may hold values from 0 to 4095, as said below
- net_position: float32 [64], replicated, may hold values from -4 to 4
- flow_limit: float32 [4096], P(('cnec', 'bus')), may hold values from 1 to 4
Outputs:
- zonal_after: float32 [64, 4096, 64], P('act', ('cnec', 'bus'))
- loading: float32 [64, 4096], P('act', ('cnec', 'bus'))
- remaining_margin: float32 [64, 4096], P('act', ('cnec', 'bus'))
The draws below stay inside these ranges and needn't reach their ends.
Inputs may be any that keep to these rules, and one draw needn't show every extreme that they name: For each CNEC c with branch ends f and t, nodal_sensitivity[c, f] - nodal_sensitivity[c, t] lies between 0.2 and 0.45; every action's coupling has a dominant diagonal. `bus_zone`: every zone holds at least one bus. `branch_buses`: the two buses of a branch differ and lie in one zone; no bus ends two CNEC branches. `switched_rows`: the 8 branches of one action differ. `shift_weight`: every zone holds a bus of positive weight; each weight is 0 or at least 0.5.
All inputs are finite; a program needn't handle non-finite values.
Results may differ from the reference program's by a relative error of at most 0.0016.
Values sent between devices are 32-bit elements; how exact they have to be, the bound alone decides.
No kernel may reach another device: no remote copies, remote signals or barrier semaphores. Data moves between devices by JAX's collectives and lax.ppermute only.
A program may use at most 64 MiB of HBM per device.

```python
import math
import jax
import jax.numpy as jnp
from jax import lax

C_DEV = 512
Z = 64
RANK = 8
CNECS = 4096
BUSES = 131072
ACTIONS = 64
N_CNEC = 8


def layout(key):
    first, second, third = jax.random.split(key, 3)
    order = jax.random.permutation(first, BUSES)
    pairs = BUSES // 2
    offset = jax.random.randint(second, (), 0, Z)
    spread = jax.random.randint(third, (pairs,), 0, Z)
    pair_ids = jnp.arange(pairs)
    pair_zone = jnp.where(pair_ids < Z, (pair_ids + offset) % Z, spread).astype(jnp.int32)
    slot_pair = (jnp.arange(BUSES) // 2).astype(jnp.int32)
    zone_of_bus = jnp.zeros((BUSES,), jnp.int32).at[order].set(pair_zone[slot_pair])
    pair_of_bus = jnp.zeros((BUSES,), jnp.int32).at[order].set(slot_pair)
    return (order, zone_of_bus, pair_of_bus)


def draw_nodal_sensitivity(key, part):
    order, zone_of_bus, pair_of_bus = layout(key)
    key = jax.random.fold_in(key, 15)
    key_zone, key_slope, key_place, key_half, key_noise = jax.random.split(key, 5)
    place = jax.random.uniform(key_place, (BUSES // 2,), jnp.float32, -1.0, 1.0)
    bus_place = place[pair_of_bus]
    zone_part = jax.random.uniform(key_zone, (CNECS, Z), jnp.float32, -0.45, 0.45)
    slope = jax.random.uniform(key_slope, (CNECS, Z), jnp.float32, -0.3, 0.3)
    half = jax.random.uniform(key_half, (CNECS,), jnp.float32, 0.1, 0.225)
    from_bus = order[0:2 * CNECS:2]
    to_bus = order[1:2 * CNECS:2]
    own_zone = zone_of_bus[from_bus]
    rows = jnp.arange(C_DEV)

    def block(index):
        start = index * C_DEV
        zone_rows = lax.dynamic_slice_in_dim(zone_part, start, C_DEV, 0)
        slope_rows = lax.dynamic_slice_in_dim(slope, start, C_DEV, 0)
        half_rows = lax.dynamic_slice_in_dim(half, start, C_DEV, 0)
        from_rows = lax.dynamic_slice_in_dim(from_bus, start, C_DEV, 0)
        to_rows = lax.dynamic_slice_in_dim(to_bus, start, C_DEV, 0)
        zone_own = lax.dynamic_slice_in_dim(own_zone, start, C_DEV, 0)
        raw = jax.random.uniform(jax.random.fold_in(key_noise, index), (C_DEV, BUSES), jnp.float32, -1.0, 1.0)
        noise = 0.03 * raw
        values = zone_rows[:, zone_of_bus] + slope_rows[:, zone_of_bus] * bus_place[None, :] + noise
        base_own = zone_rows[rows, zone_own] + slope_rows[rows, zone_own] * bus_place[from_rows]
        values = values.at[rows, from_rows].set(base_own + half_rows)
        values = values.at[rows, to_rows].set(base_own - half_rows)
        return values.astype(jnp.bfloat16)
    blocks = lax.map(block, jnp.arange(CNECS // C_DEV))
    return blocks.reshape(CNECS, BUSES)


def draw_shift_weight(key, part):
    order, zone_of_bus, pair_of_bus = layout(key)
    key = jax.random.fold_in(key, 11)
    key_base, key_pick = jax.random.split(key)
    positions = jnp.arange(BUSES).astype(jnp.float32) / BUSES
    rising = jnp.exp(jnp.log(3.0) * positions)
    rate = max(1, BUSES // (8 * Z))
    picked = (jax.random.randint(key_pick, (BUSES,), 0, rate) == 0) | (pair_of_bus < Z)
    base = jnp.exp(jax.random.uniform(key_base, (BUSES,), jnp.float32, 0.0, jnp.log(10.0)))
    return jnp.where(picked, base * rising, 0.0)


def draw_bus_zone(key, part):
    order, zone_of_bus, pair_of_bus = layout(key)
    return zone_of_bus


def draw_branch_buses(key, part):
    order, zone_of_bus, pair_of_bus = layout(key)
    start_bus = order[0:2 * CNECS:2]
    end_bus = order[1:2 * CNECS:2]
    return jnp.stack([start_bus, end_bus]).astype(jnp.int32)


def draw_switched_rows(key, part):
    key = jax.random.fold_in(key, 14)
    keys = jax.random.split(key, ACTIONS)
    chosen = jax.vmap(lambda single: jax.random.permutation(single, CNECS)[:RANK])(keys)
    return chosen.astype(jnp.int32)


def steps_of(stream_key, extent, cuts, least, high):
    factor_of = 1.0
    for axis_at, blocks in cuts:
        draws = jax.random.uniform(jax.random.fold_in(jax.random.fold_in(stream_key, 6), axis_at), (blocks,), jnp.float32, least / len(cuts), high / len(cuts))
        factor_of = factor_of * jnp.repeat(jnp.exp(draws), extent[axis_at] // blocks).reshape((-1,) + (1,) * (len(extent) - 1 - axis_at))
    return factor_of


def scatter_about(stream_key, extent, scale, limit, kind=jnp.bfloat16):
    entries = scale * jax.random.normal(stream_key, extent, jnp.float32)
    return jnp.clip(entries, min=-limit, max=limit).astype(kind)


def setup_inputs(seed: int = 0) -> dict:
    seeds = jax.random.split(jax.random.key(seed), 8)
    return {
        "nodal_sensitivity": draw_nodal_sensitivity(jax.random.fold_in(seeds[7], 71), 0),
        "shift_weight": draw_shift_weight(jax.random.fold_in(seeds[7], 71), 0),
        "bus_zone": draw_bus_zone(jax.random.fold_in(seeds[7], 71), 0),
        "branch_buses": draw_branch_buses(jax.random.fold_in(seeds[7], 71), 0),
        "switched_rows": draw_switched_rows(jax.random.fold_in(seeds[7], 71), 0),
        "net_position": scatter_about(seeds[5], (Z,), 0.5, 4.0, jnp.float32),
        "flow_limit": jnp.clip(jnp.exp(math.log(4.0) - 1.3862944 * jax.random.uniform(seeds[6], (CNECS,), jnp.float32) ** steps_of(seeds[6], (CNECS,), ((0, 128),), -0.2, 0.2)), 1.0, 4.0),
    }


def eliminate(coupling, right):
    size = coupling.shape[1]
    positions = jnp.arange(size)
    for pivot in range(size):
        diagonal = coupling[:, pivot, pivot]
        row_now = coupling[:, pivot, :] / diagonal[:, None]
        right_now = right[:, pivot, :] / diagonal[:, None]
        factor = jnp.where(positions[None, :] == pivot, 0.0, coupling[:, :, pivot])
        coupling = coupling - factor[:, :, None] * row_now[:, None, :]
        right = right - factor[:, :, None] * right_now[:, None, :]
        is_pivot = (positions == pivot)[None, :, None]
        coupling = jnp.where(is_pivot, row_now[:, None, :], coupling)
        right = jnp.where(is_pivot, right_now[:, None, :], right)
    return right


def reference(nodal_sensitivity, shift_weight, bus_zone, branch_buses, switched_rows, net_position, flow_limit):
    onehot = (bus_zone[:, None] == jnp.arange(Z)[None, :]).astype(jnp.float32)
    zone_total = jnp.sum(onehot * shift_weight[:, None], axis=0)
    shift_key = (onehot * shift_weight[:, None] / zone_total[None, :]).astype(jnp.bfloat16)
    blocks = nodal_sensitivity.reshape(N_CNEC, C_DEV, BUSES)
    zonal = lax.map(lambda block: jnp.dot(block, shift_key, preferred_element_type=jnp.float32), blocks)
    zonal = zonal.reshape(CNECS, Z)
    from_bus = branch_buses[0][switched_rows]
    to_bus = branch_buses[1][switched_rows]
    column_diff = nodal_sensitivity[:, from_bus].astype(jnp.float32) - nodal_sensitivity[:, to_bus].astype(jnp.float32)
    action_ids = jnp.arange(ACTIONS)[:, None]
    coupled = column_diff[switched_rows, action_ids, :]
    coupling = jnp.eye(RANK, dtype=jnp.float32)[None, :, :] - coupled
    solved = eliminate(coupling, zonal[switched_rows])
    zonal_after = zonal[None, :, :] + jnp.einsum('caj,ajz->acz', column_diff, solved, precision=lax.Precision.HIGHEST)
    flow = jnp.einsum('acz,z->ac', zonal_after, net_position, precision=lax.Precision.HIGHEST)
    loading = flow / flow_limit[None, :]
    remaining_margin = flow_limit[None, :] - jnp.abs(flow)
    return zonal_after, loading, remaining_margin
```

```python
import functools

import jax
import jax.numpy as jnp
from jax import lax
from jax.experimental import pallas as pl
from jax.experimental.pallas import tpu as pltpu
from jax.sharding import PartitionSpec as P

HIGHEST = lax.Precision.HIGHEST
LANES = 128
HALF = 64
SUB = 8
BLOCK = 1024


def iota(shape, dim):
    return lax.broadcasted_iota(jnp.int32, shape, dim)


def dot_nt(x, y, precision=None):
    return lax.dot_general(
        x, y, (((1,), (1,)), ((), ())), precision=precision, preferred_element_type=jnp.float32
    )


def dot(x, y):
    return jnp.dot(x, y, preferred_element_type=jnp.float32)


def pick_rows(local, values):
    pick = jnp.where(iota((local.shape[0], values.shape[0]), 1) == local, 1.0, 0.0)
    pick = pick.astype(jnp.bfloat16)
    high = values.astype(jnp.bfloat16)
    rest = values - high.astype(jnp.float32)
    middle = rest.astype(jnp.bfloat16)
    low = (rest - middle.astype(jnp.float32)).astype(jnp.bfloat16)
    return dot(pick, high) + dot(pick, middle) + dot(pick, low)


def pack_actions(rows):
    return rows.reshape(rows.shape[0] // (2 * SUB), 2, SUB, rows.shape[1])


def total_kernel(zones, weight_ref, zone_ref, out_ref):
    cols = weight_ref.shape[1]
    acc = jnp.zeros((zones, LANES), jnp.float32)
    ids = iota((zones, LANES), 0)
    for start in range(0, cols, LANES):
        weight = weight_ref[:, pl.ds(start, LANES)]
        zone = zone_ref[:, pl.ds(start, LANES)]
        acc += jnp.where(zone == ids, weight, 0.0)
    column = jnp.sum(acc, axis=1, keepdims=True)
    row = jnp.sum(jnp.where(ids == iota((zones, LANES), 1), column, 0.0), axis=0, keepdims=True)
    out_ref[...] = jnp.broadcast_to(row, out_ref.shape)


def column_kernel(
    starts_ref, s_row_ref, s_col_ref, branch_ref, sens_hbm, diff_ref, coup_ref, sens_ref, sems
):
    rows, cols = sens_ref.shape
    picks = s_row_ref.shape[1]
    rank = SUB
    copies = []
    for step in range(cols // BLOCK):
        at = pl.ds(step * BLOCK, BLOCK)
        copies.append(
            pltpu.make_async_copy(sens_hbm.at[:, at], sens_ref.at[:, at], sems.at[step])
        )
        copies[-1].start()

    branches = branch_ref.shape[1]
    s_row = s_row_ref[...]
    found = jnp.zeros((SUB, picks), jnp.float32)
    for start in range(0, branches, BLOCK):
        ends = branch_ref[:, pl.ds(start, BLOCK)]
        pieces = jnp.concatenate(
            [ends >> 12, (ends >> 6) & 63, ends & 63, jnp.zeros_like(ends)], axis=0
        ).astype(jnp.bfloat16)
        onehot = jnp.where(iota((BLOCK, picks), 0) + start == s_row, 1.0, 0.0)
        found += dot(pieces, onehot.astype(jnp.bfloat16))
    ends = found[0:2] * 4096.0 + found[2:4] * 64.0 + found[4:6]
    ends = ends.astype(jnp.int32) - starts_ref[0]

    for step in range(cols // BLOCK):
        at = iota((BLOCK, picks), 0) + step * BLOCK
        select = jnp.where(at == ends[0:1], 1.0, jnp.where(at == ends[1:2], -1.0, 0.0))
        select = select.astype(jnp.bfloat16)
        copies[step].wait()
        part = dot(sens_ref[:, pl.ds(step * BLOCK, BLOCK)], select)
        if step:
            diff_ref[...] += part
        else:
            diff_ref[...] = part

    found = pick_rows(s_col_ref[...] - starts_ref[1], diff_ref[...])
    same = iota((picks, picks), 0) // rank == iota((picks, picks), 1) // rank
    found = jnp.where(same, found, 0.0)
    folded = found[:, 0:LANES]
    for start in range(LANES, picks, LANES):
        folded = folded + found[:, start:start + LANES]
    shift = HALF
    while shift >= rank:
        folded = folded + pltpu.roll(folded, shift, 1)
        shift //= 2
    folded = pack_actions(folded)
    first = iota((1, SUB, LANES), 2) < HALF
    coup_ref[...] = jnp.where(first, folded[:, 0], folded[:, 1])


def zonal_kernel(
    zones, starts_ref, total_ref, weight_ref, zone_ref, s_col_ref, coup_ref, sens_ref, out_ref
):
    rows, cols = sens_ref.shape
    parts = out_ref.shape[0]
    total = total_ref[0:1, :]
    eye = iota((zones, LANES), 0) == iota((zones, LANES), 1)
    column = jnp.sum(jnp.where(eye, total, 0.0), axis=1, keepdims=True)
    zonal = jnp.zeros((rows, zones), jnp.float32)
    for start in range(0, cols, BLOCK):
        at = pl.ds(start, BLOCK)
        key = jnp.where(zone_ref[:, at] == iota((zones, BLOCK), 0), weight_ref[:, at] / column, 0.0)
        zonal += dot_nt(sens_ref[:, at], key.astype(jnp.bfloat16))
    switched = pack_actions(pick_rows(s_col_ref[...] - starts_ref[1], zonal))
    share = zonal.reshape(parts, rows // parts // SUB, SUB, zones)
    lower = starts_ref[2] == 0
    share = [jnp.where(lower, share[:, at], share[:, at + 2]) for at in (0, 1)]
    out_ref[:, 0:SUB, :] = jnp.concatenate(share, axis=2)
    out_ref[:, SUB:2 * SUB, :] = jnp.concatenate([switched[:, 0], switched[:, 1]], axis=2)
    out_ref[:, 2 * SUB:, :] = coup_ref[...]


def solve_kernel(rank, parts_ref, diff_ref, out_ref, sum_ref):
    sum_ref[...] = jnp.sum(diff_ref[...], axis=0)
    right = parts_ref[0:SUB]
    row_id = iota((SUB, LANES), 0)
    lane = iota((SUB, LANES), 1)
    first = lane < HALF
    left = jnp.where(lane % rank == row_id, 1.0, 0.0) - parts_ref[SUB:]
    for pivot in range(rank):
        factor = jnp.where(first, left[:, pivot:pivot + 1], left[:, HALF + pivot:HALF + pivot + 1])
        diagonal = factor[pivot:pivot + 1]
        left_now = left[pivot:pivot + 1] / diagonal
        right_now = right[pivot:pivot + 1] / diagonal
        left = jnp.where(row_id == pivot, left_now, left - factor * left_now)
        right = jnp.where(row_id == pivot, right_now, right - factor * right_now)
    out_ref[...] = jnp.broadcast_to(right[None], out_ref.shape)


def final_kernel(
    rank, starts_ref, mine_ref, other_ref, diff_ref, solved_ref, position_ref, limit_ref,
    after_ref, loading_ref, margin_ref
):
    actions, share, zones = after_ref.shape
    picks = actions * rank
    lower = starts_ref[2] == 0
    mine, other = mine_ref[...], other_ref[...]
    low, high = jnp.where(lower, mine, other), jnp.where(lower, other, mine)
    zonal = jnp.concatenate(
        [low[:, :HALF], low[:, HALF:], high[:, :HALF], high[:, HALF:]], axis=0
    )
    zonal_twice = jnp.concatenate([zonal, zonal], axis=1)
    diff = diff_ref[...]
    first = iota((share, LANES), 1) < HALF
    for pair in range(actions // 2):
        total = zonal_twice
        for j in range(rank):
            at = pair * 2 * rank + j
            factor = jnp.where(first, diff[:, at:at + 1], diff[:, at + rank:at + rank + 1])
            total = total + factor * solved_ref[pair, j:j + 1, :]
        after_ref[2 * pair] = total[:, :HALF]
        after_ref[2 * pair + 1] = total[:, HALF:]
    position = position_ref[...]
    solved = solved_ref[...].reshape(actions // 2 * rank, LANES)
    moved = [
        dot_nt(position, solved[:, at:at + HALF], HIGHEST) for at in (0, HALF)
    ]
    flow = dot_nt(position, zonal, HIGHEST)
    half = picks // 2
    mask = iota((actions, half), 1) // rank == iota((actions, half), 0) // 2
    side = iota((actions, half), 0) % 2 == 0
    diff_pairs = diff.reshape(share, picks)
    spread = [
        jnp.concatenate(
            [diff_pairs[:, (2 * pair + at) * rank:(2 * pair + at + 1) * rank] for pair in range(actions // 2)],
            axis=1,
        )
        for at in (0, 1)
    ]
    flow = (
        flow
        + dot_nt(jnp.where(mask & side, moved[0], 0.0), spread[0], HIGHEST)
        + dot_nt(jnp.where(mask & ~side, moved[1], 0.0), spread[1], HIGHEST)
    )
    limit = limit_ref[...]
    loading_ref[...] = flow / limit
    margin_ref[...] = limit - jnp.abs(flow)


def params():
    return pltpu.CompilerParams(vmem_limit_bytes=48 * 1024 * 1024)


def sum_over(x, axis, size, group, stride):
    total = x
    for offset in range(1, group):
        pairs = []
        for source in range(size):
            place = source // stride % group
            target = source + ((place + offset) % group - place) * stride
            pairs.append((source, target))
        total = total + lax.ppermute(x, axis, pairs)
    return total


def body(
    nodal_sensitivity, shift_weight, bus_zone, branch_buses, switched_rows, net_position, flow_limit
):
    rows, cols = nodal_sensitivity.shape
    zones = net_position.shape[0]
    actions, rank = switched_rows.shape
    picks = actions * rank
    n_bus, n_cnec = lax.axis_size("bus"), lax.axis_size("cnec")
    share = rows // n_bus
    f32 = jnp.float32

    starts = jnp.stack(
        [lax.axis_index("bus") * cols, lax.axis_index("cnec") * rows, lax.axis_index("act")]
    ).astype(jnp.int32)
    weight = shift_weight.reshape(1, cols)
    zone = bus_zone.reshape(1, cols)
    s_row = switched_rows.reshape(1, picks)
    s_col = switched_rows.reshape(picks, 1)
    smem = pl.BlockSpec(memory_space=pltpu.SMEM)
    vmem = pl.BlockSpec(memory_space=pltpu.VMEM)
    hbm = pl.BlockSpec(memory_space=pltpu.HBM)

    total = pl.pallas_call(
        functools.partial(total_kernel, zones),
        out_shape=jax.ShapeDtypeStruct((SUB, LANES), f32),
        in_specs=[vmem, vmem],
        out_specs=vmem,
        compiler_params=params(),
        name="zone_totals",
    )(weight, zone)
    total = sum_over(total, "bus", n_bus, 4, 1)
    total = sum_over(total, "bus", n_bus, n_bus // 4, 4)

    diff, coupled, sens = pl.pallas_call(
        column_kernel,
        out_shape=(
            jax.ShapeDtypeStruct((rows, picks), f32),
            jax.ShapeDtypeStruct((n_bus, SUB, LANES), f32),
            pltpu.VMEM((rows, cols), jnp.bfloat16),
        ),
        in_specs=[smem, vmem, vmem, vmem, hbm],
        out_specs=(vmem, vmem, vmem),
        scratch_shapes=[pltpu.SemaphoreType.DMA((cols // BLOCK,))],
        compiler_params=params(),
        name="columns",
    )(starts, s_row, s_col, branch_buses, nodal_sensitivity)
    sens = pltpu.with_memory_space_constraint(sens, pltpu.VMEM)
    diff = lax.all_to_all(diff.reshape(n_bus, share, picks), "bus", 0, 0, tiled=True)

    partial = pl.pallas_call(
        functools.partial(zonal_kernel, zones),
        out_shape=jax.ShapeDtypeStruct((n_bus, 3 * SUB, LANES), f32),
        in_specs=[smem] + [vmem] * 6,
        out_specs=vmem,
        compiler_params=params(),
        name="zonal",
    )(starts, total, weight, zone, s_col, coupled, sens)
    local = jnp.sum(lax.all_to_all(partial, "bus", 0, 0, tiled=True), axis=0)

    mine = local[0:SUB]
    other = lax.ppermute(mine, "act", [(0, 1), (1, 0)])
    joined = sum_over(local[SUB:], "cnec", n_cnec, n_cnec, 1)
    solved, diff = pl.pallas_call(
        functools.partial(solve_kernel, rank),
        out_shape=(
            jax.ShapeDtypeStruct((n_bus, SUB, LANES), f32),
            jax.ShapeDtypeStruct((share, picks), f32),
        ),
        in_specs=[vmem, vmem],
        out_specs=(vmem, vmem),
        compiler_params=params(),
        name="solve",
    )(joined, diff)
    solved = lax.all_to_all(solved, "bus", 0, 0, tiled=True)

    return pl.pallas_call(
        functools.partial(final_kernel, rank),
        out_shape=(
            jax.ShapeDtypeStruct((actions, share, zones), f32),
            jax.ShapeDtypeStruct((actions, share), f32),
            jax.ShapeDtypeStruct((actions, share), f32),
        ),
        in_specs=[smem] + [vmem] * 6,
        out_specs=(vmem, vmem, vmem),
        compiler_params=params(),
        name="update",
    )(starts, mine, other, diff, solved, net_position.reshape(1, zones), flow_limit.reshape(1, share))


def solution(mesh):
    return jax.shard_map(
        body,
        mesh=mesh,
        in_specs=(
            P("cnec", "bus"),
            P("bus"),
            P("bus"),
            P(),
            P("act", None),
            P(),
            P(("cnec", "bus")),
        ),
        out_specs=(
            P("act", ("cnec", "bus"), None),
            P("act", ("cnec", "bus")),
            P("act", ("cnec", "bus")),
        ),
        check_vma=False,
    )
```

```python
import jax
import jax.numpy as jnp
from jax import lax
from jax.experimental import pallas as pl
from jax.experimental.pallas import tpu as pltpu
from jax.sharding import Mesh
from jax.sharding import PartitionSpec as P

HIGHEST = lax.Precision.HIGHEST
LANES = 128
HALF = 64
SUB = 8
BLOCK = 1024
CNEC, BUS = ("yl", "x"), ("z", "yh")
PLANE = ("yl", "x", "yh")


def iota(shape, dim):
    return lax.broadcasted_iota(jnp.int32, shape, dim)


def dot_nt(x, y, precision=None):
    return lax.dot_general(
        x, y, (((1,), (1,)), ((), ())), precision=precision, preferred_element_type=jnp.float32
    )


def dot(x, y, precision=None):
    return jnp.dot(x, y, precision=precision, preferred_element_type=jnp.float32)


def three_parts(values):
    high = values.astype(jnp.bfloat16)
    rest = values - high.astype(jnp.float32)
    middle = rest.astype(jnp.bfloat16)
    return high, middle, (rest - middle.astype(jnp.float32)).astype(jnp.bfloat16)


def digits(values, base, count):
    return [((values >> (base * at)) & ((1 << base) - 1)).astype(jnp.float32).astype(jnp.bfloat16)
            for at in reversed(range(count))]


def partial_kernel(
    swt_hbm, branch_hbm, weight_hbm, zone_hbm, sens_hbm, pay_ref,
    swt_ref, branch_ref, weight_ref, zone_ref, sens_ref, acc_ref, zonal_ref, total_ref, sems
):
    rows, cols = sens_ref.shape
    rank, actions = swt_ref.shape
    picks = rank * actions
    zones = HALF
    steps = cols // BLOCK
    small = [
        pltpu.make_async_copy(source, target, sems.at[steps + at])
        for at, (source, target) in enumerate(
            [(swt_hbm, swt_ref), (branch_hbm, branch_ref), (weight_hbm, weight_ref), (zone_hbm, zone_ref)]
        )
    ]
    for copy in small:
        copy.start()

    def block_copy(step):
        at = pl.ds(pl.multiple_of(step * BLOCK, BLOCK), BLOCK)
        return pltpu.make_async_copy(sens_hbm.at[:, at], sens_ref.at[:, at], sems.at[step])

    for step in range(steps):
        block_copy(step).start()

    bus_start = lax.axis_index(BUS) * cols
    row_start = lax.axis_index(CNEC) * rows
    acc_ref[...] = jnp.zeros_like(acc_ref)
    zonal_ref[...] = jnp.zeros_like(zonal_ref)
    total_ref[...] = jnp.zeros_like(total_ref)

    for copy in small[:2]:
        copy.wait()
    swt = swt_ref[...]
    pick_id = iota((picks, actions), 0)
    of_action = pick_id % LANES // rank * 2 + pick_id // LANES == iota((picks, actions), 1)
    of_action = jnp.where(of_action, 1.0, 0.0).astype(jnp.bfloat16)
    high, low = digits(swt, 6, 2)
    column = dot_nt(of_action, high) * 64.0 + dot_nt(of_action, low)
    column = jnp.where(iota((picks, rank), 0) % rank == iota((picks, rank), 1), column, 0.0)
    column = jnp.sum(column, axis=1, keepdims=True).astype(jnp.int32)
    row = dot_nt(high, of_action) * 64.0 + dot_nt(low, of_action)
    row = jnp.where(iota((rank, picks), 1) % rank == iota((rank, picks), 0), row, 0.0)
    row = jnp.sum(row, axis=0, keepdims=True).astype(jnp.int32)

    tiles = branch_ref.shape[1] // LANES
    table = jnp.concatenate(
        [branch_ref[:, at * LANES:(at + 1) * LANES] for at in range(tiles)], axis=0
    )
    onehot = jnp.where(iota((LANES, picks), 0) == row % LANES, 1.0, 0.0).astype(jnp.bfloat16)
    high, middle, low = [dot(part, onehot) for part in digits(table, 6, 3)]
    found = high * 4096.0 + middle * 64.0 + low
    line = iota((2 * tiles, picks), 0) - row // LANES * 2
    ends = [
        jnp.sum(jnp.where(line == end, found, 0.0), axis=0, keepdims=True).astype(jnp.int32)
        - bus_start
        for end in (0, 1)
    ]
    for copy in small[2:]:
        copy.wait()

    def step_body(step, carry):
        at = pl.ds(pl.multiple_of(step * BLOCK, BLOCK), BLOCK)
        bus = iota((BLOCK, picks), 0)
        first, second = [end - step * BLOCK for end in ends]
        select = jnp.where(bus == first, 1.0, jnp.where(bus == second, -1.0, 0.0))
        select = select.astype(jnp.bfloat16)
        inside = zone_ref[:, at] == iota((zones, BLOCK), 0)
        weight = weight_ref[:, at]
        part = jnp.where(inside, weight, 0.0)
        total = part[:, 0:LANES]
        for start in range(LANES, BLOCK, LANES):
            total = total + part[:, start:start + LANES]
        total_ref[...] += total
        high = weight.astype(jnp.bfloat16).astype(jnp.float32)
        key = jnp.concatenate(
            [jnp.where(inside, high, 0.0), jnp.where(inside, weight - high, 0.0)], axis=0
        ).astype(jnp.bfloat16)
        block_copy(step).wait()
        sens = sens_ref[:, at]
        acc_ref[...] += dot(sens, select)
        zonal_ref[...] += dot_nt(sens, key)
        return carry

    lax.fori_loop(0, steps, step_body, 0)

    chunks = pay_ref.shape[0]
    diff = acc_ref[...]
    zonal = zonal_ref[:, 0:zones] + zonal_ref[:, zones:2 * zones]
    choose = jnp.where(iota((picks, rows), 1) == column - row_start, 1.0, 0.0).astype(jnp.bfloat16)
    switched = dot(choose, jnp.concatenate(three_parts(zonal), axis=1))
    switched = switched[:, 0:zones] + switched[:, zones:2 * zones] + switched[:, 2 * zones:]
    high, middle, low = [dot(choose, part) for part in three_parts(diff)]
    coupled = high + middle + low
    same = iota((picks, picks), 0) // rank == iota((picks, picks), 1) // rank
    coupled = jnp.where(same, coupled, 0.0)
    pick_id = iota((picks, LANES), 0)
    lane = (pick_id // rank % 2 * 2 + pick_id // LANES) * rank + pick_id % rank
    fold = jnp.where(lane == iota((picks, LANES), 1), 1.0, 0.0).astype(jnp.bfloat16)
    high, middle, low = [dot(part, fold) for part in three_parts(coupled)]
    coupled = jnp.sum((high + middle + low).reshape(2, chunks, 2, SUB, LANES), axis=(0, 2))
    total = jnp.sum(total_ref[...], axis=1, keepdims=True)
    eye = iota((zones, LANES), 0) == iota((zones, LANES), 1) - HALF
    total = jnp.sum(jnp.where(eye, total, 0.0), axis=0, keepdims=True)

    share = zonal.reshape(chunks, 2, 2, 2, SUB, zones)
    share = jnp.where(lax.axis_index("act") == 0, share[:, :, 0], share[:, :, 1])
    share = jnp.concatenate([share[:, :, 0], share[:, :, 1]], axis=-1)
    switched = switched.reshape(2, actions // 2, rank, zones)
    switched = jnp.concatenate([switched[0], switched[1]], axis=-1)
    half = rows // chunks // 2
    diff = diff.reshape(chunks, 2, half, picks)
    part = SUB + 2 * half
    for at in range(2):
        start = at * part
        pay_ref[:, start:start + SUB, :] = share[:, at]
        pay_ref[:, start + SUB:start + SUB + half, :] = diff[:, at, :, 0:LANES]
        pay_ref[:, start + SUB + half:start + part, :] = diff[:, at, :, LANES:]
    start = 2 * part
    pay_ref[:, start:start + 2 * SUB, :] = switched.reshape(chunks, 2 * SUB, LANES)
    pay_ref[:, start + 2 * SUB:, :] = coupled + total


def solve_kernel(parts_ref, out_ref, total_ref):
    full = jnp.sum(parts_ref[...], axis=0)
    extra = full[2 * SUB:]
    total = extra[0:1, HALF:] / lax.axis_size(CNEC)
    total = jnp.concatenate([total, total], axis=1)
    total_ref[...] = jnp.broadcast_to(total, total_ref.shape)
    row_id = iota((SUB, LANES), 0)
    lane = iota((SUB, LANES), 1)
    eye = jnp.where(lane % SUB == row_id, 1.0, 0.0)
    source = iota((LANES, LANES), 0)
    target = iota((LANES, LANES), 1)
    for tile in range(2):
        spread = (source // SUB == tile * 2 + target // HALF) & (source % SUB == target % SUB)
        left = eye - dot(extra, jnp.where(spread, 1.0, 0.0), HIGHEST)
        right = full[tile * SUB:(tile + 1) * SUB] / total
        for pivot in range(SUB):
            factor = jnp.where(
                lane < HALF, left[:, pivot:pivot + 1], left[:, HALF + pivot:HALF + pivot + 1]
            )
            diagonal = factor[pivot:pivot + 1]
            left_now = left[pivot:pivot + 1] / diagonal
            right_now = right[pivot:pivot + 1] / diagonal
            left = jnp.where(row_id == pivot, left_now, left - factor * left_now)
            right = jnp.where(row_id == pivot, right_now, right - factor * right_now)
        out_ref[:, tile * SUB:(tile + 1) * SUB, :] = jnp.broadcast_to(
            right[None], (out_ref.shape[0], SUB, LANES)
        )


def final_kernel(
    mine_ref, theirs_ref, other_ref, total_ref, solved_ref, position_ref, limit_ref,
    after_ref, loading_ref, margin_ref
):
    actions, share, zones = after_ref.shape
    pairs = actions // 2
    lower = lax.axis_index("act") == 0
    whole = mine_ref[...] + theirs_ref[...]
    mine, other = whole[0:SUB], other_ref[...]
    low, high = jnp.where(lower, mine, other), jnp.where(lower, other, mine)
    zonal = jnp.concatenate(
        [low[:, :HALF], low[:, HALF:], high[:, :HALF], high[:, HALF:]], axis=0
    ) / total_ref[0:1, :HALF]
    zonal_twice = jnp.concatenate([zonal, zonal], axis=1)
    even, odd = whole[SUB:SUB + share], whole[SUB + share:]
    first = iota((share, LANES), 1) < HALF
    for pair in range(pairs):
        total = zonal_twice
        for j in range(SUB):
            at = pair * SUB + j
            factor = jnp.where(first, even[:, at:at + 1], odd[:, at:at + 1])
            total = total + factor * solved_ref[pair, j:j + 1, :]
        after_ref[2 * pair] = total[:, :HALF]
        after_ref[2 * pair + 1] = total[:, HALF:]
    position = position_ref[...]
    solved = solved_ref[...].reshape(pairs * SUB, LANES)
    flow = dot_nt(position, zonal, HIGHEST)
    shape = (actions, pairs * SUB)
    same = iota(shape, 1) // SUB == iota(shape, 0) // 2
    for side, part in enumerate((even, odd)):
        moved = dot_nt(position, solved[:, side * HALF:(side + 1) * HALF], HIGHEST)
        mask = same & (iota(shape, 0) % 2 == side)
        flow = flow + dot_nt(jnp.where(mask, moved, 0.0), part, HIGHEST)
    limit = limit_ref[...]
    loading_ref[...] = flow / limit
    margin_ref[...] = limit - jnp.abs(flow)


def params():
    return pltpu.CompilerParams(vmem_limit_bytes=48 * 1024 * 1024)


def body(
    nodal_sensitivity, shift_weight, bus_zone, branch_buses, switched_rows, net_position, flow_limit
):
    rows, cols = nodal_sensitivity.shape
    zones = net_position.shape[0]
    actions, rank = switched_rows.shape
    picks = actions * rank
    n_z, n_yh, n_plane = lax.axis_size("z"), lax.axis_size("yh"), lax.axis_size(PLANE)
    share = rows // n_z // n_yh
    f32, i32 = jnp.float32, jnp.int32
    vmem = pl.BlockSpec(memory_space=pltpu.VMEM)
    hbm = pl.BlockSpec(memory_space=pltpu.HBM)

    part = SUB + 2 * share
    pay = pl.pallas_call(
        partial_kernel,
        out_shape=jax.ShapeDtypeStruct((n_z, n_yh * part + 3 * SUB, LANES), f32),
        in_specs=[hbm] * 5,
        out_specs=vmem,
        scratch_shapes=[
            pltpu.VMEM((rank, actions), i32),
            pltpu.VMEM(branch_buses.shape, i32),
            pltpu.VMEM((1, cols), f32),
            pltpu.VMEM((1, cols), i32),
            pltpu.VMEM((rows, cols), jnp.bfloat16),
            pltpu.VMEM((rows, picks), f32),
            pltpu.VMEM((rows, 2 * zones), f32),
            pltpu.VMEM((zones, LANES), f32),
            pltpu.SemaphoreType.DMA((cols // BLOCK + 4,)),
        ],
        compiler_params=params(),
        name="partials",
    )(
        *[
            pltpu.with_memory_space_constraint(x, pltpu.HBM)
            for x in (
                switched_rows.T, branch_buses, shift_weight.reshape(1, cols),
                bus_zone.reshape(1, cols), nodal_sensitivity,
            )
        ]
    )

    local = jnp.sum(lax.all_to_all(pay, "z", 0, 0, tiled=True), axis=0)
    spread = jnp.broadcast_to(local[n_yh * part:][None], (n_plane, 3 * SUB, LANES))
    spread = lax.all_to_all(spread, PLANE, 0, 0, tiled=True)

    swap = [(0, 1), (1, 0)]
    here = lax.axis_index("yh")
    mine = lax.dynamic_slice_in_dim(local, here * part, part)
    theirs = lax.ppermute(lax.dynamic_slice_in_dim(local, (1 - here) * part, part), "yh", swap)
    other = lax.ppermute(mine[:SUB] + theirs[:SUB], "act", swap)

    solved, total = pl.pallas_call(
        solve_kernel,
        out_shape=(
            jax.ShapeDtypeStruct((n_z, 2 * SUB, LANES), f32),
            jax.ShapeDtypeStruct((SUB, LANES), f32),
        ),
        in_specs=[vmem],
        out_specs=(vmem, vmem),
        compiler_params=params(),
        name="solve",
    )(spread)
    solved = lax.all_to_all(solved, "z", 0, 0, tiled=True).reshape(actions // 2, SUB, LANES)

    return pl.pallas_call(
        final_kernel,
        out_shape=(
            jax.ShapeDtypeStruct((actions, share, zones), f32),
            jax.ShapeDtypeStruct((actions, share), f32),
            jax.ShapeDtypeStruct((actions, share), f32),
        ),
        in_specs=[vmem] * 7,
        out_specs=(vmem, vmem, vmem),
        compiler_params=params(),
        name="update",
    )(
        mine, theirs, other, total, solved,
        net_position.reshape(1, zones), flow_limit.reshape(1, share),
    )


def solution(mesh):
    n_cnec, n_bus, n_act = mesh.devices.shape
    split = Mesh(
        mesh.devices.reshape(2, n_cnec // 2, n_bus // 2, 2, n_act), ("yl", "x", "z", "yh", "act")
    )
    return jax.shard_map(
        body,
        mesh=split,
        in_specs=(
            P(CNEC, BUS),
            P(BUS),
            P(BUS),
            P(),
            P("act", None),
            P(),
            P(CNEC + BUS),
        ),
        out_specs=(
            P("act", CNEC + BUS, None),
            P("act", CNEC + BUS),
            P("act", CNEC + BUS),
        ),
        check_vma=False,
    )
```

```python
import jax
import jax.numpy as jnp
from jax import lax
from jax.experimental import pallas as pl
from jax.experimental.pallas import tpu as pltpu
from jax.sharding import Mesh
from jax.sharding import PartitionSpec as P

HIGHEST = lax.Precision.HIGHEST
LANES = 128
HALF = 64
SUB = 8
BLOCK = 2048
CNEC, BUS = ("yl", "x"), ("z", "yh")


def iota(shape, dim):
    return lax.broadcasted_iota(jnp.int32, shape, dim)


def dot_nt(x, y, precision=None):
    return lax.dot_general(
        x, y, (((1,), (1,)), ((), ())), precision=precision, preferred_element_type=jnp.float32
    )


def dot(x, y, precision=None):
    return jnp.dot(x, y, precision=precision, preferred_element_type=jnp.float32)


def two_parts(values):
    high = values.astype(jnp.bfloat16)
    return high, (values - high.astype(jnp.float32)).astype(jnp.bfloat16)


def digits(values, base, count):
    return [((values >> (base * at)) & ((1 << base) - 1)).astype(jnp.float32).astype(jnp.bfloat16)
            for at in reversed(range(count))]


def partial_kernel(
    swt_hbm, branch_hbm, weight_hbm, zone_hbm, sens_hbm, pay_ref, diff_ref,
    swt_ref, branch_ref, weight_ref, zone_ref, sens_ref, select_ref, acc_ref, zonal_ref, sems
):
    cols = sens_ref.shape[1]
    rows = acc_ref.shape[0]
    rank, actions = swt_ref.shape
    picks = rank * actions
    zones = HALF
    steps = cols // BLOCK
    bf16 = jnp.bfloat16
    small = [
        pltpu.make_async_copy(source, target, sems.at[steps + at])
        for at, (source, target) in enumerate(
            [(swt_hbm, swt_ref), (branch_hbm, branch_ref), (weight_hbm, weight_ref), (zone_hbm, zone_ref)]
        )
    ]
    for copy in small:
        copy.start()

    def block_copy(step):
        at = pl.ds(pl.multiple_of(step * BLOCK, BLOCK), BLOCK)
        return pltpu.make_async_copy(sens_hbm.at[:, at], sens_ref.at[0:rows, at], sems.at[step])

    for step in range(steps):
        block_copy(step).start()

    bus_start = lax.axis_index(BUS) * cols
    row_start = lax.axis_index(CNEC) * rows
    acc_ref[...] = jnp.zeros_like(acc_ref)
    zonal_ref[...] = jnp.zeros_like(zonal_ref)
    sens_ref[rows:, :] = jnp.ones((sens_ref.shape[0] - rows, cols), bf16)

    for copy in small[:2]:
        copy.wait()
    swt = swt_ref[...]
    pick_id = iota((picks, actions), 0)
    of_action = pick_id % LANES // rank * 2 + pick_id // LANES == iota((picks, actions), 1)
    of_action = jnp.where(of_action, 1.0, 0.0).astype(bf16)
    high, low = digits(swt, 6, 2)
    column = dot_nt(of_action, high) * 64.0 + dot_nt(of_action, low)
    column = jnp.where(iota((picks, rank), 0) % rank == iota((picks, rank), 1), column, 0.0)
    column = jnp.sum(column, axis=1, keepdims=True).astype(jnp.int32)
    row = dot_nt(high, of_action) * 64.0 + dot_nt(low, of_action)
    row = jnp.where(iota((rank, picks), 1) % rank == iota((rank, picks), 0), row, 0.0)
    row = jnp.sum(row, axis=0, keepdims=True).astype(jnp.int32)

    tiles = branch_ref.shape[1] // LANES
    table = jnp.concatenate(
        [branch_ref[:, at * LANES:(at + 1) * LANES] for at in range(tiles)], axis=0
    )
    onehot = jnp.where(iota((LANES, picks), 0) == row % LANES, 1.0, 0.0).astype(bf16)
    high, middle, low = [dot(part, onehot) for part in digits(table, 6, 3)]
    found = high * 4096.0 + middle * 64.0 + low
    line = iota((2 * tiles, picks), 0) - row // LANES * 2
    ends = [
        jnp.sum(jnp.where(line == end, found, 0.0), axis=0, keepdims=True).astype(jnp.int32)
        - bus_start
        for end in (0, 1)
    ]
    group = [end >> 7 for end in ends]
    within = [(end & (LANES - 1)).astype(jnp.float32) for end in ends]
    bus = iota((LANES, picks), 0).astype(jnp.float32).astype(bf16)
    zone_id = iota((zones, BLOCK), 0).astype(jnp.float32).astype(bf16)
    for copy in small[2:]:
        copy.wait()

    def step_body(step, carry):
        at = pl.ds(pl.multiple_of(step * BLOCK, BLOCK), BLOCK)
        for part in range(BLOCK // LANES):
            here = step * (BLOCK // LANES) + part
            first, second = [
                jnp.where(g == here, w, -1.0).astype(bf16) for g, w in zip(group, within)
            ]
            select_ref[part * LANES:(part + 1) * LANES, :] = jnp.where(
                bus == first, bf16(1.0), jnp.where(bus == second, bf16(-1.0), bf16(0.0))
            )
        inside = zone_ref[:, at].astype(jnp.float32).astype(bf16) == zone_id
        high, low = two_parts(weight_ref[:, at])
        key = jnp.concatenate(
            [jnp.where(inside, high, bf16(0.0)), jnp.where(inside, low, bf16(0.0))], axis=0
        )
        block_copy(step).wait()
        acc_ref[...] += dot(sens_ref[0:rows, at], select_ref[...])
        zonal_ref[...] += dot_nt(sens_ref[:, at], key)
        return carry

    lax.fori_loop(0, steps, step_body, 0)

    chunks = pay_ref.shape[0]
    diff = acc_ref[...]
    zonal = zonal_ref[:, 0:zones] + zonal_ref[:, zones:2 * zones]
    total = zonal_ref[rows:rows + 1, :]
    total = total + pltpu.roll(total, HALF, 1)
    total = jnp.where(iota((1, LANES), 1) < HALF, 0.0, total)
    zonal = zonal[0:rows]
    choose = jnp.where(iota((picks, rows), 1) == column - row_start, 1.0, 0.0).astype(bf16)
    switched = dot(choose, jnp.concatenate(two_parts(zonal), axis=1))
    switched = switched[:, 0:zones] + switched[:, zones:]
    high, low = [dot(choose, part) for part in two_parts(diff)]
    coupled = high + low
    same = iota((picks, picks), 0) // rank == iota((picks, picks), 1) // rank
    coupled = jnp.where(same, coupled, 0.0)
    pick_id = iota((picks, LANES), 0)
    lane = (pick_id // rank % 2 * 2 + pick_id // LANES) * rank + pick_id % rank
    fold = jnp.where(lane == iota((picks, LANES), 1), 1.0, 0.0).astype(bf16)
    high, low = [dot(part, fold) for part in two_parts(coupled)]
    coupled = jnp.sum((high + low).reshape(2, chunks, 2, SUB, LANES), axis=(0, 2))

    share = zonal.reshape(chunks, 2, 2, 2, SUB, zones)
    share = jnp.where(lax.axis_index("act") == 0, share[:, :, 0], share[:, :, 1])
    share = jnp.concatenate([share[:, :, 0], share[:, :, 1]], axis=-1)
    switched = switched.reshape(2, actions // 2, rank, zones)
    switched = jnp.concatenate([switched[0], switched[1]], axis=-1)
    half = rows // chunks // 2
    diff = diff.reshape(chunks, 2, half, picks)
    for at in range(2):
        start = at * 2 * half
        pay_ref[:, at * SUB:(at + 1) * SUB, :] = share[:, at]
        diff_ref[:, start:start + half, :] = diff[:, at, :, 0:LANES]
        diff_ref[:, start + half:start + 2 * half, :] = diff[:, at, :, LANES:]
    pay_ref[:, 2 * SUB:4 * SUB, :] = switched.reshape(chunks, 2 * SUB, LANES)
    pay_ref[:, 4 * SUB:, :] = coupled + total


def solve_kernel(parts_ref, diff_ref, out_ref, total_ref, mine_ref, theirs_ref):
    half = mine_ref.shape[0]
    first, second = [
        jnp.sum(diff_ref[:, at * half:(at + 1) * half, :], axis=0) for at in (0, 1)
    ]
    lower = lax.axis_index("yh") == 0
    mine_ref[...] = jnp.where(lower, first, second)
    theirs_ref[...] = jnp.where(lower, second, first)
    full = parts_ref[...]
    extra = full[2 * SUB:]
    total = extra[0:1, HALF:] / lax.axis_size(CNEC)
    total = jnp.concatenate([total, total], axis=1)
    total_ref[...] = jnp.broadcast_to(total, total_ref.shape)
    row_id = iota((SUB, LANES), 0)
    lane = iota((SUB, LANES), 1)
    eye = jnp.where(lane % SUB == row_id, 1.0, 0.0)
    source = iota((LANES, LANES), 0)
    target = iota((LANES, LANES), 1)
    for tile in range(2):
        spread = (source // SUB == tile * 2 + target // HALF) & (source % SUB == target % SUB)
        left = eye - dot(extra, jnp.where(spread, 1.0, 0.0), HIGHEST)
        right = full[tile * SUB:(tile + 1) * SUB] / total
        for pivot in range(SUB):
            factor = jnp.where(
                lane < HALF, left[:, pivot:pivot + 1], left[:, HALF + pivot:HALF + pivot + 1]
            )
            diagonal = factor[pivot:pivot + 1]
            left_now = left[pivot:pivot + 1] / diagonal
            right_now = right[pivot:pivot + 1] / diagonal
            left = jnp.where(row_id == pivot, left_now, left - factor * left_now)
            right = jnp.where(row_id == pivot, right_now, right - factor * right_now)
        out_ref[:, tile * SUB:(tile + 1) * SUB, :] = jnp.broadcast_to(
            right[None], (out_ref.shape[0], SUB, LANES)
        )


def final_kernel(
    mine_ref, other_ref, diff_ref, diff_theirs_ref, total_ref, solved_ref, position_ref, limit_ref,
    after_ref, loading_ref, margin_ref
):
    actions, share, zones = after_ref.shape
    pairs = actions // 2
    lower = lax.axis_index("act") == 0
    diff = diff_ref[...] + diff_theirs_ref[...]
    mine, other = mine_ref[...], other_ref[...]
    low, high = jnp.where(lower, mine, other), jnp.where(lower, other, mine)
    zonal = jnp.concatenate(
        [low[:, :HALF], low[:, HALF:], high[:, :HALF], high[:, HALF:]], axis=0
    ) / total_ref[0:1, :HALF]
    zonal_twice = jnp.concatenate([zonal, zonal], axis=1)
    even, odd = diff[0:share], diff[share:]
    first = iota((share, LANES), 1) < HALF
    for pair in range(pairs):
        total = zonal_twice
        for j in range(SUB):
            at = pair * SUB + j
            factor = jnp.where(first, even[:, at:at + 1], odd[:, at:at + 1])
            total = total + factor * solved_ref[pair, j:j + 1, :]
        after_ref[2 * pair] = total[:, :HALF]
        after_ref[2 * pair + 1] = total[:, HALF:]
    position = position_ref[...]
    solved = solved_ref[...].reshape(pairs * SUB, LANES)
    flow = dot_nt(position, zonal, HIGHEST)
    shape = (actions, pairs * SUB)
    same = iota(shape, 1) // SUB == iota(shape, 0) // 2
    for side, part in enumerate((even, odd)):
        moved = dot_nt(position, solved[:, side * HALF:(side + 1) * HALF], HIGHEST)
        mask = same & (iota(shape, 0) % 2 == side)
        flow = flow + dot_nt(jnp.where(mask, moved, 0.0), part, HIGHEST)
    limit = limit_ref[...]
    loading_ref[...] = flow / limit
    margin_ref[...] = limit - jnp.abs(flow)


def params():
    return pltpu.CompilerParams(vmem_limit_bytes=48 * 1024 * 1024)


def body(
    nodal_sensitivity, shift_weight, bus_zone, branch_buses, switched_rows, net_position, flow_limit
):
    rows, cols = nodal_sensitivity.shape
    zones = net_position.shape[0]
    actions, rank = switched_rows.shape
    picks = actions * rank
    n_z, n_yh = lax.axis_size("z"), lax.axis_size("yh")
    share = rows // n_z // n_yh
    f32, i32 = jnp.float32, jnp.int32
    vmem = pl.BlockSpec(memory_space=pltpu.VMEM)
    hbm = pl.BlockSpec(memory_space=pltpu.HBM)

    pay, diff = pl.pallas_call(
        partial_kernel,
        out_shape=(
            jax.ShapeDtypeStruct((n_z, 5 * SUB, LANES), f32),
            jax.ShapeDtypeStruct((n_z, n_yh * 2 * share, LANES), f32),
        ),
        in_specs=[hbm] * 5,
        out_specs=(vmem, vmem),
        scratch_shapes=[
            pltpu.VMEM((rank, actions), i32),
            pltpu.VMEM(branch_buses.shape, i32),
            pltpu.VMEM((1, cols), f32),
            pltpu.VMEM((1, cols), i32),
            pltpu.VMEM((rows + 2 * SUB, cols), jnp.bfloat16),
            pltpu.VMEM((BLOCK, picks), jnp.bfloat16),
            pltpu.VMEM((rows, picks), f32),
            pltpu.VMEM((rows + 2 * SUB, 2 * zones), f32),
            pltpu.SemaphoreType.DMA((cols // BLOCK + 4,)),
        ],
        compiler_params=params(),
        name="partials",
    )(
        *[
            pltpu.with_memory_space_constraint(x, pltpu.HBM)
            for x in (
                switched_rows.T, branch_buses, shift_weight.reshape(1, cols),
                bus_zone.reshape(1, cols), nodal_sensitivity,
            )
        ]
    )

    swap = [(0, 1), (1, 0)]
    here = lax.axis_index("yh")

    local = jnp.sum(lax.all_to_all(pay, "z", 0, 0, tiled=True), axis=0)
    diff = lax.all_to_all(diff, "z", 0, 0, tiled=True)

    full = local[2 * SUB:]
    for axis, pairs in (
        ("x", [(0, 1), (1, 0), (2, 3), (3, 2)]),
        ("x", [(0, 3), (3, 0), (1, 2), (2, 1)]),
        ("yl", swap),
        (("yl", "yh"), [(0, 3), (3, 0), (1, 2), (2, 1)]),
    ):
        full = full + lax.ppermute(full, axis, pairs)

    theirs = lax.dynamic_slice_in_dim(local, (1 - here) * SUB, SUB)
    mine = lax.dynamic_slice_in_dim(local, here * SUB, SUB) + lax.ppermute(theirs, "yh", swap)
    other = lax.ppermute(mine, "act", swap)

    solved, total, diff, theirs = pl.pallas_call(
        solve_kernel,
        out_shape=(
            jax.ShapeDtypeStruct((n_z, 2 * SUB, LANES), f32),
            jax.ShapeDtypeStruct((SUB, LANES), f32),
            jax.ShapeDtypeStruct((2 * share, LANES), f32),
            jax.ShapeDtypeStruct((2 * share, LANES), f32),
        ),
        in_specs=[vmem, vmem],
        out_specs=(vmem,) * 4,
        compiler_params=params(),
        name="solve",
    )(full, diff)
    diff_theirs = lax.ppermute(theirs, "yh", swap)
    solved = lax.all_to_all(solved, "z", 0, 0, tiled=True).reshape(actions // 2, SUB, LANES)

    return pl.pallas_call(
        final_kernel,
        out_shape=(
            jax.ShapeDtypeStruct((actions, share, zones), f32),
            jax.ShapeDtypeStruct((actions, share), f32),
            jax.ShapeDtypeStruct((actions, share), f32),
        ),
        in_specs=[vmem] * 8,
        out_specs=(vmem, vmem, vmem),
        compiler_params=params(),
        name="update",
    )(
        mine, other, diff, diff_theirs, total, solved,
        net_position.reshape(1, zones), flow_limit.reshape(1, share),
    )


def solution(mesh):
    n_cnec, n_bus, n_act = mesh.devices.shape
    split = Mesh(
        mesh.devices.reshape(2, n_cnec // 2, n_bus // 2, 2, n_act), ("yl", "x", "z", "yh", "act")
    )
    return jax.shard_map(
        body,
        mesh=split,
        in_specs=(
            P(CNEC, BUS),
            P(BUS),
            P(BUS),
            P(),
            P("act", None),
            P(),
            P(CNEC + BUS),
        ),
        out_specs=(
            P("act", CNEC + BUS, None),
            P("act", CNEC + BUS),
            P("act", CNEC + BUS),
        ),
        check_vma=False,
    )
```

```python
import jax
import jax.numpy as jnp
from jax import lax
from jax.experimental import pallas as pl
from jax.experimental.pallas import tpu as pltpu
from jax.sharding import Mesh
from jax.sharding import PartitionSpec as P

HIGHEST = lax.Precision.HIGHEST
LANES = 128
HALF = 64
SUB = 8
BLOCK = 2048
SLOTS = 64
CNEC, BUS = ("yl", "x"), ("z", "yh")


def iota(shape, dim):
    return lax.broadcasted_iota(jnp.int32, shape, dim)


def dot_nt(x, y, precision=None):
    return lax.dot_general(
        x, y, (((1,), (1,)), ((), ())), precision=precision, preferred_element_type=jnp.float32
    )


def dot(x, y, precision=None):
    return jnp.dot(x, y, precision=precision, preferred_element_type=jnp.float32)


def two_parts(values):
    high = values.astype(jnp.bfloat16)
    return high, (values - high.astype(jnp.float32)).astype(jnp.bfloat16)


def digits(values, base, count):
    return [((values >> (base * at)) & ((1 << base) - 1)).astype(jnp.float32).astype(jnp.bfloat16)
            for at in reversed(range(count))]


def find_picks(swt, branch_ref):
    rank, actions = swt.shape
    picks = rank * actions
    pick_id = iota((picks, actions), 0)
    of_action = pick_id % LANES // rank * 2 + pick_id // LANES == iota((picks, actions), 1)
    of_action = jnp.where(of_action, 1.0, 0.0).astype(jnp.bfloat16)
    high, low = digits(swt, 6, 2)
    column = dot_nt(of_action, high) * 64.0 + dot_nt(of_action, low)
    column = jnp.where(iota((picks, rank), 0) % rank == iota((picks, rank), 1), column, 0.0)
    column = jnp.sum(column, axis=1, keepdims=True).astype(jnp.int32)
    row = dot_nt(high, of_action) * 64.0 + dot_nt(low, of_action)
    row = jnp.where(iota((rank, picks), 1) % rank == iota((rank, picks), 0), row, 0.0)
    row = jnp.sum(row, axis=0, keepdims=True).astype(jnp.int32)
    tiles = branch_ref.shape[1] // LANES
    table = jnp.concatenate(
        [branch_ref[:, at * LANES:(at + 1) * LANES] for at in range(tiles)], axis=0
    )
    onehot = jnp.where(iota((LANES, picks), 0) == row % LANES, 1.0, 0.0).astype(jnp.bfloat16)
    high, middle, low = [dot(part, onehot) for part in digits(table, 6, 3)]
    found = high * 4096.0 + middle * 64.0 + low
    line = iota((2 * tiles, picks), 0) - row // LANES * 2
    ends = [
        jnp.sum(jnp.where(line == end, found, 0.0), axis=0, keepdims=True).astype(jnp.int32)
        for end in (0, 1)
    ]
    return column, ends


def slot_matrix(slots, count):
    shape = (count, slots[0].shape[1])
    first, second = [jnp.where(iota(shape, 0) == slot, 1.0, 0.0) for slot in slots]
    return (first - second).astype(jnp.bfloat16)


def partial_kernel(
    swt_hbm, branch_hbm, weight_hbm, zone_hbm, sens_hbm, pay_ref, meta_ref,
    swt_ref, branch_ref, weight_ref, zone_ref, sens_ref, acc_ref, coupled_ref, sems
):
    cols = sens_ref.shape[1]
    rows = sens_ref.shape[0] - 2 * SUB
    rank, actions = swt_ref.shape
    picks = rank * actions
    zones = HALF
    steps = cols // BLOCK
    bf16 = jnp.bfloat16
    small = [
        pltpu.make_async_copy(source, target, sems.at[steps + at])
        for at, (source, target) in enumerate(
            [(swt_hbm, swt_ref), (branch_hbm, branch_ref), (weight_hbm, weight_ref), (zone_hbm, zone_ref)]
        )
    ]
    for copy in small:
        copy.start()

    def block_copy(step):
        at = pl.ds(pl.multiple_of(step * BLOCK, BLOCK), BLOCK)
        return pltpu.make_async_copy(sens_hbm.at[:, at], sens_ref.at[0:rows, at], sems.at[step])

    for step in range(steps):
        block_copy(step).start()

    shard = lax.axis_index(BUS)
    row_start = lax.axis_index(CNEC) * rows
    acc_ref[...] = jnp.zeros_like(acc_ref)
    sens_ref[rows:, :] = jnp.ones((sens_ref.shape[0] - rows, cols), bf16)

    for copy in small[:2]:
        copy.wait()
    column, ends = find_picks(swt_ref[...], branch_ref)

    bus = jnp.concatenate(ends, axis=1)
    held = bus // cols
    count = 2 * picks
    shards = lax.axis_size(BUS)
    inside = iota((shards, count), 0) == held
    before = jnp.where(iota((count, count), 0) < iota((count, count), 1), 1.0, 0.0).astype(bf16)
    place = dot(jnp.where(inside, 1.0, 0.0).astype(bf16), before)
    place = jnp.sum(jnp.where(inside, place, 0.0), axis=0, keepdims=True)
    over = jnp.where(jnp.max(place, axis=1, keepdims=True) >= SLOTS, 1.0, 0.0)
    meta = jnp.concatenate([held.astype(jnp.float32), place, jnp.broadcast_to(over, (1, count))], axis=0)
    meta_ref[...] = jnp.concatenate([meta, jnp.zeros((SUB - 3, count), jnp.float32)], axis=0)
    place = place.astype(jnp.int32)
    mine = held == shard
    slot = jnp.where(mine, place, -1)
    local = bus - shard * cols

    def buses_of(group):
        match = iota((SLOTS, count), 0) + group * SLOTS == slot
        return jnp.sum(jnp.where(match, (local + 1).astype(jnp.float32), 0.0), axis=1, keepdims=True).astype(jnp.int32) - 1

    first_buses = buses_of(0)
    zone_id = iota((zones, BLOCK), 0).astype(jnp.float32).astype(bf16)
    lane = iota((SLOTS, BLOCK), 1)
    for copy in small[2:]:
        copy.wait()

    def select(buses, step):
        return jnp.where(lane == buses - step * BLOCK, 1.0, 0.0).astype(bf16)

    def step_body(step, carry):
        at = pl.ds(pl.multiple_of(step * BLOCK, BLOCK), BLOCK)
        inside = zone_ref[:, at].astype(jnp.float32).astype(bf16) == zone_id
        high, low = two_parts(weight_ref[:, at])
        key = jnp.concatenate(
            [
                jnp.where(inside, high, bf16(0.0)),
                jnp.where(inside, low, bf16(0.0)),
                select(first_buses, step),
            ],
            axis=0,
        )
        block_copy(step).wait()
        acc_ref[...] += dot_nt(sens_ref[:, at], key)
        return carry

    lax.fori_loop(0, steps, step_body, 0)

    chunks = pay_ref.shape[0]
    zonal = acc_ref[0:rows, 0:zones] + acc_ref[0:rows, zones:2 * zones]
    total = acc_ref[rows:rows + 1, 0:2 * zones]
    total = total + pltpu.roll(total, HALF, 1)
    total = jnp.where(iota((1, LANES), 1) < HALF, 0.0, total)
    held_columns = acc_ref[0:rows, 2 * zones:]
    choose = jnp.where(iota((picks, rows), 1) == column - row_start, 1.0, 0.0).astype(bf16)
    chosen = dot(
        choose, jnp.concatenate([*two_parts(zonal), held_columns.astype(bf16)], axis=1)
    )
    switched = chosen[:, 0:zones] + chosen[:, zones:2 * zones]

    def coupled_of(chosen_columns, group):
        slots = [slot[:, at * picks:(at + 1) * picks] - group * SLOTS for at in (0, 1)]
        return dot(chosen_columns.astype(bf16), slot_matrix(slots, SLOTS))

    coupled_ref[...] = coupled_of(chosen[:, 2 * zones:], 0)

    def group_body(group, carry):
        buses = buses_of(group)
        columns = jnp.zeros((rows, SLOTS), jnp.float32)
        for step in range(steps):
            at = pl.ds(step * BLOCK, BLOCK)
            columns += dot_nt(sens_ref[0:rows, at], select(buses, step))
        coupled_ref[...] += coupled_of(dot(choose, columns.astype(bf16)), group)
        return carry

    groups = (jnp.sum(jnp.where(mine, 1.0, 0.0)).astype(jnp.int32) + SLOTS - 1) // SLOTS
    lax.fori_loop(1, groups, group_body, 0)

    same = iota((picks, picks), 0) // rank == iota((picks, picks), 1) // rank
    coupled = jnp.where(same, coupled_ref[...], 0.0)
    pick_id = iota((picks, LANES), 0)
    lane_of = (pick_id // rank % 2 * 2 + pick_id // LANES) * rank + pick_id % rank
    fold = jnp.where(lane_of == iota((picks, LANES), 1), 1.0, 0.0).astype(bf16)
    high, low = [dot(part, fold) for part in two_parts(coupled)]
    coupled = jnp.sum((high + low).reshape(2, chunks, 2, SUB, LANES), axis=(0, 2))

    share = zonal.reshape(chunks, 2, 2, 2, SUB, zones)
    share = jnp.where(lax.axis_index("act") == 0, share[:, :, 0], share[:, :, 1])
    share = jnp.concatenate([share[:, :, 0], share[:, :, 1]], axis=-1)
    switched = switched.reshape(2, actions // 2, rank, zones)
    switched = jnp.concatenate([switched[0], switched[1]], axis=-1)
    held_columns = held_columns.reshape(chunks, 2, rows // chunks // 2, SLOTS)
    pay_ref[:, 0:2 * SUB, :] = share.reshape(chunks, 2 * SUB, LANES)
    pay_ref[:, 2 * SUB:4 * SUB, :] = switched.reshape(chunks, 2 * SUB, LANES)
    pay_ref[:, 4 * SUB:5 * SUB, :] = coupled + total
    pay_ref[:, 5 * SUB:, :] = jnp.concatenate([held_columns[:, 0], held_columns[:, 1]], axis=-1)


def place_kernel(parts_ref, local_ref, meta_ref, mine_ref, theirs_ref):
    chunks = parts_ref.shape[0]
    picks = meta_ref.shape[1] // 2
    half = parts_ref.shape[1] - 5 * SUB
    y_here, y_size = lax.axis_index("yh"), lax.axis_size("yh")
    held = meta_ref[0:1, :].astype(jnp.int32)
    place = meta_ref[1:2, :].astype(jnp.int32)
    known = (held % y_size == y_here) & (place < SLOTS)
    slot = jnp.where(known, held // y_size * SLOTS + place, -1)
    spread = slot_matrix([slot[:, at * picks:(at + 1) * picks] for at in (0, 1)], chunks * SLOTS)
    columns = [
        jnp.concatenate(
            [parts_ref[z, 5 * SUB:, at * SLOTS:(at + 1) * SLOTS] for z in range(chunks)], axis=1
        )
        for at in (0, 1)
    ]
    diff = dot(jnp.concatenate(columns, axis=0).astype(jnp.bfloat16), spread)
    lower = y_here == 0
    for ref, first in ((mine_ref, lower), (theirs_ref, ~lower)):
        ref[0:SUB, :] = jnp.where(first, local_ref[0:SUB, :], local_ref[SUB:2 * SUB, :])
        part = jnp.where(first, diff[0:half], diff[half:])
        ref[SUB:SUB + half, :] = part[:, 0:LANES]
        ref[SUB + half:, :] = part[:, LANES:]


def dense_kernel(swt_ref, branch_ref, sens_ref, diff_ref):
    step = pl.program_id(0)
    rows, block = sens_ref.shape
    picks = swt_ref.shape[0] * swt_ref.shape[1]
    chunks = diff_ref.shape[0]
    half = rows // chunks // 2
    first, second = [
        end - lax.axis_index(BUS) * (block * pl.num_programs(0)) - step * block
        for end in find_picks(swt_ref[...], branch_ref)[1]
    ]

    @pl.when(step == 0)
    def _():
        diff_ref[...] = jnp.zeros_like(diff_ref)

    bus = iota((block, picks), 0)
    select = jnp.where(bus == first, 1.0, jnp.where(bus == second, -1.0, 0.0))
    diff = dot(sens_ref[...], select.astype(jnp.bfloat16)).reshape(chunks, 2, half, picks)
    for at in range(2):
        start = at * 2 * half
        diff_ref[:, start:start + half, :] += diff[:, at, :, 0:LANES]
        diff_ref[:, start + half:start + 2 * half, :] += diff[:, at, :, LANES:]


def solve_kernel(parts_ref, out_ref, total_ref):
    full = parts_ref[...]
    extra = full[2 * SUB:]
    total = extra[0:1, HALF:] / lax.axis_size(CNEC)
    total = jnp.concatenate([total, total], axis=1)
    total_ref[...] = jnp.broadcast_to(total, total_ref.shape)
    row_id = iota((SUB, LANES), 0)
    lane = iota((SUB, LANES), 1)
    eye = jnp.where(lane % SUB == row_id, 1.0, 0.0)
    source = iota((LANES, LANES), 0)
    target = iota((LANES, LANES), 1)
    for tile in range(2):
        spread = (source // SUB == tile * 2 + target // HALF) & (source % SUB == target % SUB)
        left = eye - dot(extra, jnp.where(spread, 1.0, 0.0), HIGHEST)
        right = full[tile * SUB:(tile + 1) * SUB] / total
        for pivot in range(SUB):
            factor = jnp.where(
                lane < HALF, left[:, pivot:pivot + 1], left[:, HALF + pivot:HALF + pivot + 1]
            )
            diagonal = factor[pivot:pivot + 1]
            left_now = left[pivot:pivot + 1] / diagonal
            right_now = right[pivot:pivot + 1] / diagonal
            left = jnp.where(row_id == pivot, left_now, left - factor * left_now)
            right = jnp.where(row_id == pivot, right_now, right - factor * right_now)
        out_ref[:, tile * SUB:(tile + 1) * SUB, :] = jnp.broadcast_to(
            right[None], (out_ref.shape[0], SUB, LANES)
        )


def final_kernel(
    mine_ref, theirs_ref, other_ref, total_ref, solved_ref, position_ref, limit_ref,
    after_ref, loading_ref, margin_ref
):
    actions, share, zones = after_ref.shape
    pairs = actions // 2
    lower = lax.axis_index("act") == 0
    whole = mine_ref[...] + theirs_ref[...]
    mine, other = whole[0:SUB], other_ref[0:SUB]
    low, high = jnp.where(lower, mine, other), jnp.where(lower, other, mine)
    zonal = jnp.concatenate(
        [low[:, :HALF], low[:, HALF:], high[:, :HALF], high[:, HALF:]], axis=0
    ) / total_ref[0:1, :HALF]
    zonal_twice = jnp.concatenate([zonal, zonal], axis=1)
    even, odd = whole[SUB:SUB + share], whole[SUB + share:]
    first = iota((share, LANES), 1) < HALF
    for pair in range(pairs):
        total = zonal_twice
        for j in range(SUB):
            at = pair * SUB + j
            factor = jnp.where(first, even[:, at:at + 1], odd[:, at:at + 1])
            total = total + factor * solved_ref[pair, j:j + 1, :]
        after_ref[2 * pair] = total[:, :HALF]
        after_ref[2 * pair + 1] = total[:, HALF:]
    position = position_ref[...]
    solved = solved_ref[...].reshape(pairs * SUB, LANES)
    flow = dot_nt(position, zonal, HIGHEST)
    shape = (actions, pairs * SUB)
    same = iota(shape, 1) // SUB == iota(shape, 0) // 2
    for side, part in enumerate((even, odd)):
        moved = dot_nt(position, solved[:, side * HALF:(side + 1) * HALF], HIGHEST)
        mask = same & (iota(shape, 0) % 2 == side)
        flow = flow + dot_nt(jnp.where(mask, moved, 0.0), part, HIGHEST)
    limit = limit_ref[...]
    loading_ref[...] = flow / limit
    margin_ref[...] = limit - jnp.abs(flow)


def in_hbm(x):
    return pltpu.with_memory_space_constraint(x, pltpu.HBM)


def params():
    return pltpu.CompilerParams(vmem_limit_bytes=48 * 1024 * 1024)


def body(
    nodal_sensitivity, shift_weight, bus_zone, branch_buses, switched_rows, net_position, flow_limit
):
    rows, cols = nodal_sensitivity.shape
    zones = net_position.shape[0]
    actions, rank = switched_rows.shape
    picks = actions * rank
    n_z, n_yh = lax.axis_size("z"), lax.axis_size("yh")
    share = rows // n_z // n_yh
    f32, i32 = jnp.float32, jnp.int32
    vmem = pl.BlockSpec(memory_space=pltpu.VMEM)
    hbm = pl.BlockSpec(memory_space=pltpu.HBM)

    weight, zone = shift_weight.reshape(1, cols), bus_zone.reshape(1, cols)
    pay, meta = pl.pallas_call(
        partial_kernel,
        out_shape=(
            jax.ShapeDtypeStruct((n_z, 5 * SUB + share, LANES), f32),
            jax.ShapeDtypeStruct((SUB, 2 * picks), f32),
        ),
        in_specs=[hbm] * 5,
        out_specs=(vmem, vmem),
        scratch_shapes=[
            pltpu.VMEM((rank, actions), i32),
            pltpu.VMEM(branch_buses.shape, i32),
            pltpu.VMEM((1, cols), f32),
            pltpu.VMEM((1, cols), i32),
            pltpu.VMEM((rows + 2 * SUB, cols), jnp.bfloat16),
            pltpu.VMEM((rows + 2 * SUB, 2 * zones + SLOTS), f32),
            pltpu.VMEM((picks, picks), f32),
            pltpu.SemaphoreType.DMA((cols // BLOCK + 4,)),
        ],
        compiler_params=params(),
        name="partials",
    )(
        *[in_hbm(x) for x in (switched_rows.T, branch_buses, weight, zone, nodal_sensitivity)]
    )

    swap = [(0, 1), (1, 0)]
    parts = lax.all_to_all(pay, "z", 0, 0, tiled=True)
    local = jnp.sum(parts[:, :5 * SUB], axis=0)

    full = local[2 * SUB:]
    for axis, pairs in (
        ("x", [(0, 1), (1, 0), (2, 3), (3, 2)]),
        ("x", [(0, 3), (3, 0), (1, 2), (2, 1)]),
        ("yl", swap),
        (("yl", "yh"), [(0, 3), (3, 0), (1, 2), (2, 1)]),
    ):
        full = full + lax.ppermute(full, axis, pairs)

    part = jax.ShapeDtypeStruct((SUB + 2 * share, LANES), f32)
    mine, theirs = pl.pallas_call(
        place_kernel,
        out_shape=(part, part),
        in_specs=[vmem] * 3,
        out_specs=(vmem, vmem),
        compiler_params=params(),
        name="place",
    )(parts, local, meta)
    theirs = lax.ppermute(theirs, "yh", swap)
    other = lax.ppermute(
        jnp.concatenate([mine[:SUB] + theirs[:SUB], meta[:, :LANES]], axis=0), "act", swap
    )

    solved, total = pl.pallas_call(
        solve_kernel,
        out_shape=(
            jax.ShapeDtypeStruct((n_z, 2 * SUB, LANES), f32),
            jax.ShapeDtypeStruct((SUB, LANES), f32),
        ),
        in_specs=[vmem],
        out_specs=(vmem, vmem),
        compiler_params=params(),
        name="solve",
    )(full)
    solved = lax.all_to_all(solved, "z", 0, 0, tiled=True).reshape(actions // 2, SUB, LANES)

    def finish(mine, theirs):
        return pl.pallas_call(
            final_kernel,
            out_shape=(
                jax.ShapeDtypeStruct((actions, share, zones), f32),
                jax.ShapeDtypeStruct((actions, share), f32),
                jax.ShapeDtypeStruct((actions, share), f32),
            ),
            in_specs=[vmem] * 7,
            out_specs=(vmem, vmem, vmem),
            compiler_params=params(),
            name="update",
        )(
            mine, theirs, other, total, solved,
            net_position.reshape(1, zones), flow_limit.reshape(1, share),
        )

    def dense():
        diff = pl.pallas_call(
            dense_kernel,
            grid=(cols // BLOCK,),
            out_shape=jax.ShapeDtypeStruct((n_z, n_yh * 2 * share, LANES), f32),
            in_specs=[
                pl.BlockSpec((rank, actions), lambda i: (0, 0)),
                pl.BlockSpec(branch_buses.shape, lambda i: (0, 0)),
                pl.BlockSpec((rows, BLOCK), lambda i: (0, i)),
            ],
            out_specs=pl.BlockSpec((n_z, n_yh * 2 * share, LANES), lambda i: (0, 0, 0)),
            compiler_params=params(),
            name="dense",
        )(*[in_hbm(x) for x in (switched_rows.T, branch_buses, nodal_sensitivity)])
        diff = jnp.sum(lax.all_to_all(diff, "z", 0, 0, tiled=True), axis=0)
        here, size = lax.axis_index("yh"), 2 * share
        own = lax.dynamic_slice_in_dim(diff, here * size, size)
        sent = lax.dynamic_slice_in_dim(diff, (1 - here) * size, size)
        sent = lax.ppermute(sent, "yh", swap)
        return finish(
            jnp.concatenate([mine[:SUB], own], axis=0),
            jnp.concatenate([theirs[:SUB], sent], axis=0),
        )

    over = jnp.maximum(meta[2, 0], other[SUB + 2, 0]) > 0.5
    return lax.cond(over, dense, lambda: finish(mine, theirs))


def solution(mesh):
    n_cnec, n_bus, n_act = mesh.devices.shape
    split = Mesh(
        mesh.devices.reshape(2, n_cnec // 2, n_bus // 2, 2, n_act), ("yl", "x", "z", "yh", "act")
    )
    return jax.shard_map(
        body,
        mesh=split,
        in_specs=(
            P(CNEC, BUS),
            P(BUS),
            P(BUS),
            P(),
            P("act", None),
            P(),
            P(CNEC + BUS),
        ),
        out_specs=(
            P("act", CNEC + BUS, None),
            P("act", CNEC + BUS),
            P("act", CNEC + BUS),
        ),
        check_vma=False,
    )
```

```python
import jax
import jax.numpy as jnp
from jax import lax
from jax.experimental import pallas as pl
from jax.experimental.pallas import tpu as pltpu
from jax.sharding import Mesh
from jax.sharding import PartitionSpec as P

HIGHEST = lax.Precision.HIGHEST
LANES = 128
HALF = 64
SUB = 8
BLOCK = 2048
SLOTS = 64
CNEC, BUS = ("yl", "x"), ("z", "yh")


def iota(shape, dim):
    return lax.broadcasted_iota(jnp.int32, shape, dim)


def dot_nt(x, y, precision=None):
    return lax.dot_general(
        x, y, (((1,), (1,)), ((), ())), precision=precision, preferred_element_type=jnp.float32
    )


def dot(x, y, precision=None):
    return jnp.dot(x, y, precision=precision, preferred_element_type=jnp.float32)


def two_parts(values):
    high = values.astype(jnp.bfloat16)
    return high, (values - high.astype(jnp.float32)).astype(jnp.bfloat16)


def by_parts(product, x, y):
    x_high, x_low = two_parts(x)
    y_high, y_low = two_parts(y)
    return product(x_high, y_high) + product(x_high, y_low) + product(x_low, y_high)


def digits(values, base, count):
    return [((values >> (base * at)) & ((1 << base) - 1)).astype(jnp.float32).astype(jnp.bfloat16)
            for at in reversed(range(count))]


def find_picks(swt, branch_ref):
    rank, actions = swt.shape
    picks = rank * actions
    pick_id = iota((picks, actions), 0)
    of_action = pick_id % LANES // rank * 2 + pick_id // LANES == iota((picks, actions), 1)
    of_action = jnp.where(of_action, 1.0, 0.0).astype(jnp.bfloat16)
    high, low = digits(swt, 6, 2)
    column = dot_nt(of_action, high) * 64.0 + dot_nt(of_action, low)
    column = jnp.where(iota((picks, rank), 0) % rank == iota((picks, rank), 1), column, 0.0)
    column = jnp.sum(column, axis=1, keepdims=True).astype(jnp.int32)
    row = dot_nt(high, of_action) * 64.0 + dot_nt(low, of_action)
    row = jnp.where(iota((rank, picks), 1) % rank == iota((rank, picks), 0), row, 0.0)
    row = jnp.sum(row, axis=0, keepdims=True).astype(jnp.int32)
    tiles = branch_ref.shape[1] // LANES
    table = jnp.concatenate(
        [branch_ref[:, at * LANES:(at + 1) * LANES] for at in range(tiles)], axis=0
    )
    onehot = jnp.where(iota((LANES, picks), 0) == row % LANES, 1.0, 0.0).astype(jnp.bfloat16)
    high, middle, low = [dot(part, onehot) for part in digits(table, 6, 3)]
    found = high * 4096.0 + middle * 64.0 + low
    line = iota((2 * tiles, picks), 0) - row // LANES * 2
    ends = [
        jnp.sum(jnp.where(line == end, found, 0.0), axis=0, keepdims=True).astype(jnp.int32)
        for end in (0, 1)
    ]
    return column, ends


def slot_matrix(slots, count):
    shape = (count, slots[0].shape[1])
    first, second = [jnp.where(iota(shape, 0) == slot, 1.0, 0.0) for slot in slots]
    return (first - second).astype(jnp.bfloat16)


def partial_kernel(
    swt_hbm, branch_hbm, weight_hbm, zone_hbm, sens_hbm, pay_ref, meta_ref,
    swt_ref, branch_ref, weight_ref, zone_ref, sens_ref, acc_ref, coupled_ref, sems
):
    cols = sens_ref.shape[1]
    rows = sens_ref.shape[0] - 2 * SUB
    rank, actions = swt_ref.shape
    picks = rank * actions
    zones = HALF
    steps = cols // BLOCK
    bf16 = jnp.bfloat16
    small = [
        pltpu.make_async_copy(source, target, sems.at[steps + at])
        for at, (source, target) in enumerate(
            [(swt_hbm, swt_ref), (branch_hbm, branch_ref), (weight_hbm, weight_ref), (zone_hbm, zone_ref)]
        )
    ]
    for copy in small:
        copy.start()

    def block_copy(step):
        at = pl.ds(pl.multiple_of(step * BLOCK, BLOCK), BLOCK)
        return pltpu.make_async_copy(sens_hbm.at[:, at], sens_ref.at[0:rows, at], sems.at[step])

    for step in range(steps):
        block_copy(step).start()

    shard = lax.axis_index(BUS)
    row_start = lax.axis_index(CNEC) * rows
    acc_ref[...] = jnp.zeros_like(acc_ref)
    sens_ref[rows:, :] = jnp.ones((sens_ref.shape[0] - rows, cols), bf16)

    for copy in small[:2]:
        copy.wait()
    column, ends = find_picks(swt_ref[...], branch_ref)

    bus = jnp.concatenate(ends, axis=1)
    held = bus // cols
    count = 2 * picks
    shards = lax.axis_size(BUS)
    inside = iota((shards, count), 0) == held
    before = jnp.where(iota((count, count), 0) < iota((count, count), 1), 1.0, 0.0).astype(bf16)
    place = dot(jnp.where(inside, 1.0, 0.0).astype(bf16), before)
    place = jnp.sum(jnp.where(inside, place, 0.0), axis=0, keepdims=True)
    over = jnp.where(jnp.max(place, axis=1, keepdims=True) >= SLOTS, 1.0, 0.0)
    meta = jnp.concatenate([held.astype(jnp.float32), place, jnp.broadcast_to(over, (1, count))], axis=0)
    meta_ref[...] = jnp.concatenate([meta, jnp.zeros((SUB - 3, count), jnp.float32)], axis=0)
    place = place.astype(jnp.int32)
    mine = held == shard
    slot = jnp.where(mine, place, -1)
    local = bus - shard * cols

    def buses_of(group):
        match = iota((SLOTS, count), 0) + group * SLOTS == slot
        return jnp.sum(jnp.where(match, (local + 1).astype(jnp.float32), 0.0), axis=1, keepdims=True).astype(jnp.int32) - 1

    first_buses = buses_of(0)
    zone_id = iota((zones, BLOCK), 0).astype(jnp.float32).astype(bf16)
    lane = iota((SLOTS, BLOCK), 1)
    for copy in small[2:]:
        copy.wait()

    def select(buses, step):
        return jnp.where(lane == buses - step * BLOCK, 1.0, 0.0).astype(bf16)

    def step_body(step, carry):
        at = pl.ds(pl.multiple_of(step * BLOCK, BLOCK), BLOCK)
        inside = zone_ref[:, at].astype(jnp.float32).astype(bf16) == zone_id
        high, low = two_parts(weight_ref[:, at])
        key = jnp.concatenate(
            [
                jnp.where(inside, high, bf16(0.0)),
                jnp.where(inside, low, bf16(0.0)),
                select(first_buses, step),
            ],
            axis=0,
        )
        block_copy(step).wait()
        acc_ref[...] += dot_nt(sens_ref[:, at], key)
        return carry

    for step in range(steps):
        step_body(step, 0)

    chunks = pay_ref.shape[0]
    zonal = acc_ref[0:rows, 0:zones] + acc_ref[0:rows, zones:2 * zones]
    total = acc_ref[rows:rows + 1, 0:2 * zones]
    total = total + pltpu.roll(total, HALF, 1)
    total = jnp.where(iota((1, LANES), 1) < HALF, 0.0, total)
    held_columns = acc_ref[0:rows, 2 * zones:]
    choose = jnp.where(iota((picks, rows), 1) == column - row_start, 1.0, 0.0).astype(bf16)
    chosen = dot(
        choose, jnp.concatenate([*two_parts(zonal), held_columns.astype(bf16)], axis=1)
    )
    switched = chosen[:, 0:zones] + chosen[:, zones:2 * zones]

    def coupled_of(chosen_columns, group):
        slots = [slot[:, at * picks:(at + 1) * picks] - group * SLOTS for at in (0, 1)]
        return dot(chosen_columns.astype(bf16), slot_matrix(slots, SLOTS))

    coupled_ref[...] = coupled_of(chosen[:, 2 * zones:], 0)

    def group_body(group, carry):
        buses = buses_of(group)
        columns = jnp.zeros((rows, SLOTS), jnp.float32)
        for step in range(steps):
            at = pl.ds(step * BLOCK, BLOCK)
            columns += dot_nt(sens_ref[0:rows, at], select(buses, step))
        coupled_ref[...] += coupled_of(dot(choose, columns.astype(bf16)), group)
        return carry

    groups = (jnp.sum(jnp.where(mine, 1.0, 0.0)).astype(jnp.int32) + SLOTS - 1) // SLOTS
    lax.fori_loop(1, groups, group_body, 0)

    same = iota((picks, picks), 0) // rank == iota((picks, picks), 1) // rank
    coupled = jnp.where(same, coupled_ref[...], 0.0)
    pick_id = iota((picks, LANES), 0)
    lane_of = (pick_id // rank % 2 * 2 + pick_id // LANES) * rank + pick_id % rank
    fold = jnp.where(lane_of == iota((picks, LANES), 1), 1.0, 0.0).astype(bf16)
    high, low = [dot(part, fold) for part in two_parts(coupled)]
    coupled = jnp.sum((high + low).reshape(2, chunks, 2, SUB, LANES), axis=(0, 2))

    share = zonal.reshape(chunks, 2, 2, 2, SUB, zones)
    share = jnp.where(lax.axis_index("act") == 0, share[:, :, 0], share[:, :, 1])
    share = jnp.concatenate([share[:, :, 0], share[:, :, 1]], axis=-1)
    switched = switched.reshape(2, actions // 2, rank, zones)
    switched = jnp.concatenate([switched[0], switched[1]], axis=-1)
    held_columns = held_columns.reshape(chunks, 2, rows // chunks // 2, SLOTS)
    pay_ref[:, 0:2 * SUB, :] = share.reshape(chunks, 2 * SUB, LANES)
    pay_ref[:, 2 * SUB:4 * SUB, :] = switched.reshape(chunks, 2 * SUB, LANES)
    pay_ref[:, 4 * SUB:5 * SUB, :] = coupled + total
    pay_ref[:, 5 * SUB:, :] = jnp.concatenate([held_columns[:, 0], held_columns[:, 1]], axis=-1)


def place_kernel(parts_ref, local_ref, meta_ref, mine_ref, theirs_ref):
    chunks = parts_ref.shape[0]
    picks = meta_ref.shape[1] // 2
    half = parts_ref.shape[1] - 5 * SUB
    y_here, y_size = lax.axis_index("yh"), lax.axis_size("yh")
    held = meta_ref[0:1, :].astype(jnp.int32)
    place = meta_ref[1:2, :].astype(jnp.int32)
    known = (held % y_size == y_here) & (place < SLOTS)
    slot = jnp.where(known, held // y_size * SLOTS + place, -1)
    spread = slot_matrix([slot[:, at * picks:(at + 1) * picks] for at in (0, 1)], chunks * SLOTS)
    columns = [
        jnp.concatenate(
            [parts_ref[z, 5 * SUB:, at * SLOTS:(at + 1) * SLOTS] for z in range(chunks)], axis=1
        )
        for at in (0, 1)
    ]
    columns = jnp.concatenate(columns, axis=0).astype(jnp.bfloat16)
    diff = lax.dot_general(
        spread, columns, (((0,), (1,)), ((), ())), preferred_element_type=jnp.float32
    )
    diff = diff.reshape(2, picks // (2 * SUB), SUB, 2 * half)
    diff = jnp.concatenate([diff[0], diff[1]], axis=1).reshape(4, picks // 4, 2 * half)
    lower = y_here == 0
    packed = [
        jnp.concatenate([diff[g, :, at * half:(at + 1) * half] for g in range(4)], axis=1)
        for at in (0, 1)
    ]
    for ref, first in ((mine_ref, lower), (theirs_ref, ~lower)):
        ref[0:SUB, :] = jnp.where(first, local_ref[0:SUB, :], local_ref[SUB:2 * SUB, :])
        ref[SUB:, :] = jnp.where(first, packed[0], packed[1])


def dense_kernel(swt_ref, branch_ref, sens_ref, diff_ref):
    step = pl.program_id(0)
    rows, block = sens_ref.shape
    picks = swt_ref.shape[0] * swt_ref.shape[1]
    chunks = diff_ref.shape[0]
    half = rows // chunks // 2
    first, second = [
        end - lax.axis_index(BUS) * (block * pl.num_programs(0)) - step * block
        for end in find_picks(swt_ref[...], branch_ref)[1]
    ]

    @pl.when(step == 0)
    def _():
        diff_ref[...] = jnp.zeros_like(diff_ref)

    bus = iota((block, picks), 0)
    select = jnp.where(bus == first, 1.0, jnp.where(bus == second, -1.0, 0.0))
    diff = dot(sens_ref[...], select.astype(jnp.bfloat16)).reshape(chunks, 2, half, picks)
    for at in range(2):
        start = at * 2 * half
        diff_ref[:, start:start + half, :] += diff[:, at, :, 0:LANES]
        diff_ref[:, start + half:start + 2 * half, :] += diff[:, at, :, LANES:]


def solve_kernel(parts_ref, out_ref, total_ref):
    full = parts_ref[...]
    extra = full[2 * SUB:]
    total = extra[0:1, HALF:] / lax.axis_size(CNEC)
    total = jnp.concatenate([total, total], axis=1)
    total_ref[...] = jnp.broadcast_to(total, total_ref.shape)
    row_id = iota((SUB, LANES), 0)
    lane = iota((SUB, LANES), 1)
    eye = jnp.where(lane % SUB == row_id, 1.0, 0.0)
    source = iota((LANES, LANES), 0)
    target = iota((LANES, LANES), 1)
    lefts, rights = [], []
    for tile in range(2):
        spread = (source // SUB == tile * 2 + target // HALF) & (source % SUB == target % SUB)
        lefts.append(eye - dot(extra, jnp.where(spread, 1.0, 0.0), HIGHEST))
        rights.append(full[tile * SUB:(tile + 1) * SUB] / total)
    for pivot in range(SUB):
        for tile in range(2):
            left, right = lefts[tile], rights[tile]
            factor = jnp.where(
                lane < HALF, left[:, pivot:pivot + 1], left[:, HALF + pivot:HALF + pivot + 1]
            )
            diagonal = factor[pivot:pivot + 1]
            left_now = left[pivot:pivot + 1] / diagonal
            right_now = right[pivot:pivot + 1] / diagonal
            lefts[tile] = jnp.where(row_id == pivot, left_now, left - factor * left_now)
            rights[tile] = jnp.where(row_id == pivot, right_now, right - factor * right_now)
    for tile in range(2):
        out_ref[:, tile * SUB:(tile + 1) * SUB, :] = jnp.broadcast_to(
            rights[tile][None], (out_ref.shape[0], SUB, LANES)
        )


def final_kernel(
    mine_ref, theirs_ref, other_ref, total_ref, solved_ref, position_ref, limit_ref,
    after_ref, loading_ref, margin_ref
):
    actions, share, zones = after_ref.shape
    pairs = actions // 2
    lower = lax.axis_index("act") == 0
    whole = mine_ref[...] + theirs_ref[...]
    mine, other = whole[0:SUB], other_ref[...]
    low, high = jnp.where(lower, mine, other), jnp.where(lower, other, mine)
    zonal = jnp.concatenate(
        [low[:, :HALF], low[:, HALF:], high[:, :HALF], high[:, HALF:]], axis=0
    ) / total_ref[0:1, :HALF]
    zonal_twice = jnp.concatenate([zonal, zonal], axis=1)
    groups = [whole[SUB:, g * share:(g + 1) * share] for g in range(LANES // share)]
    diff = jnp.concatenate(groups, axis=0)
    solved = solved_ref[...]
    first = iota(solved.shape, 2) < HALF
    solved = jnp.concatenate(
        [jnp.where(first, solved, 0.0), jnp.where(first, 0.0, solved)], axis=1
    )
    diff_high, diff_low = two_parts(diff)
    solved_high, solved_low = two_parts(solved)

    def product(x, y):
        return lax.dot_general(
            x, y, (((0,), (0,)), ((), ())), preferred_element_type=jnp.float32
        )

    size = 2 * SUB
    for pair in range(pairs):
        at = slice(pair * size, (pair + 1) * size)
        left = jnp.concatenate([diff_high[at], diff_high[at], diff_low[at]], axis=0)
        right = jnp.concatenate(
            [solved_high[pair], solved_low[pair], solved_high[pair]], axis=0
        )
        total = zonal_twice + product(left, right)
        after_ref[2 * pair] = total[:, :HALF]
        after_ref[2 * pair + 1] = total[:, HALF:]
    position = position_ref[...]
    twice = jnp.concatenate([position, position], axis=1)
    moved = by_parts(dot_nt, twice, solved.reshape(pairs * size, LANES))
    shape = (actions, pairs * size)
    same = iota(shape, 1) // SUB == iota(shape, 0)
    flow = by_parts(dot_nt, position, zonal) + by_parts(dot, jnp.where(same, moved, 0.0), diff)
    limit = limit_ref[...]
    loading_ref[...] = flow / limit
    margin_ref[...] = limit - jnp.abs(flow)


def in_hbm(x):
    return pltpu.with_memory_space_constraint(x, pltpu.HBM)


def params():
    return pltpu.CompilerParams(vmem_limit_bytes=48 * 1024 * 1024)


def body(
    nodal_sensitivity, shift_weight, bus_zone, branch_buses, switched_rows, net_position, flow_limit
):
    rows, cols = nodal_sensitivity.shape
    zones = net_position.shape[0]
    actions, rank = switched_rows.shape
    picks = actions * rank
    n_z, n_yh = lax.axis_size("z"), lax.axis_size("yh")
    share = rows // n_z // n_yh
    f32, i32 = jnp.float32, jnp.int32
    vmem = pl.BlockSpec(memory_space=pltpu.VMEM)
    hbm = pl.BlockSpec(memory_space=pltpu.HBM)

    weight, zone = shift_weight.reshape(1, cols), bus_zone.reshape(1, cols)
    pay, meta = pl.pallas_call(
        partial_kernel,
        out_shape=(
            jax.ShapeDtypeStruct((n_z, 5 * SUB + share, LANES), f32),
            jax.ShapeDtypeStruct((SUB, 2 * picks), f32),
        ),
        in_specs=[hbm] * 5,
        out_specs=(vmem, vmem),
        scratch_shapes=[
            pltpu.VMEM((rank, actions), i32),
            pltpu.VMEM(branch_buses.shape, i32),
            pltpu.VMEM((1, cols), f32),
            pltpu.VMEM((1, cols), i32),
            pltpu.VMEM((rows + 2 * SUB, cols), jnp.bfloat16),
            pltpu.VMEM((rows + 2 * SUB, 2 * zones + SLOTS), f32),
            pltpu.VMEM((picks, picks), f32),
            pltpu.SemaphoreType.DMA((cols // BLOCK + 4,)),
        ],
        compiler_params=params(),
        name="partials",
    )(
        *[in_hbm(x) for x in (switched_rows.T, branch_buses, weight, zone, nodal_sensitivity)]
    )

    swap = [(0, 1), (1, 0)]
    parts = lax.all_to_all(pay, "z", 0, 0, tiled=True)
    local = jnp.sum(parts[:, :5 * SUB], axis=0)

    full = local[2 * SUB:]
    for axis in ("x", ("yl", "yh")):
        size = lax.axis_size(axis)
        others = [
            lax.ppermute(full, axis, [(at, (at + by) % size) for at in range(size)])
            for by in range(1, size)
        ]
        full = sum(others, full)

    part = jax.ShapeDtypeStruct((SUB + 2 * share, LANES), f32)
    mine, theirs = pl.pallas_call(
        place_kernel,
        out_shape=(part, part),
        in_specs=[vmem] * 3,
        out_specs=(vmem, vmem),
        compiler_params=params(),
        name="place",
    )(parts, local, meta)
    theirs = lax.ppermute(theirs, "yh", swap)
    other = lax.ppermute(mine[:SUB] + theirs[:SUB], "act", swap)

    solved, total = pl.pallas_call(
        solve_kernel,
        out_shape=(
            jax.ShapeDtypeStruct((n_z, 2 * SUB, LANES), f32),
            jax.ShapeDtypeStruct((SUB, LANES), f32),
        ),
        in_specs=[vmem],
        out_specs=(vmem, vmem),
        compiler_params=params(),
        name="solve",
    )(full)
    solved = lax.all_to_all(solved, "z", 0, 0, tiled=True).reshape(actions // 2, SUB, LANES)

    def finish(mine, theirs):
        return pl.pallas_call(
            final_kernel,
            out_shape=(
                jax.ShapeDtypeStruct((actions, share, zones), f32),
                jax.ShapeDtypeStruct((actions, share), f32),
                jax.ShapeDtypeStruct((actions, share), f32),
            ),
            in_specs=[vmem] * 7,
            out_specs=(vmem, vmem, vmem),
            compiler_params=params(),
            name="update",
        )(
            mine, theirs, other, total, solved,
            net_position.reshape(1, zones), flow_limit.reshape(1, share),
        )

    def dense():
        diff = pl.pallas_call(
            dense_kernel,
            grid=(cols // BLOCK,),
            out_shape=jax.ShapeDtypeStruct((n_z, n_yh * 2 * share, LANES), f32),
            in_specs=[
                pl.BlockSpec((rank, actions), lambda i: (0, 0)),
                pl.BlockSpec(branch_buses.shape, lambda i: (0, 0)),
                pl.BlockSpec((rows, BLOCK), lambda i: (0, i)),
            ],
            out_specs=pl.BlockSpec((n_z, n_yh * 2 * share, LANES), lambda i: (0, 0, 0)),
            compiler_params=params(),
            name="dense",
        )(*[in_hbm(x) for x in (switched_rows.T, branch_buses, nodal_sensitivity)])
        diff = jnp.sum(lax.all_to_all(diff, "z", 0, 0, tiled=True), axis=0)
        here, size = lax.axis_index("yh"), 2 * share
        own = lax.dynamic_slice_in_dim(diff, here * size, size)
        sent = lax.dynamic_slice_in_dim(diff, (1 - here) * size, size)
        sent = lax.ppermute(sent, "yh", swap)

        def packed(x):
            x = x.reshape(2, share, 4, actions // 8, rank)
            return x.transpose(3, 0, 4, 2, 1).reshape(picks // 4, 4 * share)

        return finish(
            jnp.concatenate([mine[:SUB], packed(own)], axis=0),
            jnp.concatenate([theirs[:SUB], packed(sent)], axis=0),
        )

    return lax.cond(meta[2, 0] > 0.5, dense, lambda: finish(mine, theirs))


def solution(mesh):
    n_cnec, n_bus, n_act = mesh.devices.shape
    split = Mesh(
        mesh.devices.reshape(2, n_cnec // 2, n_bus // 2, 2, n_act), ("yl", "x", "z", "yh", "act")
    )
    return jax.shard_map(
        body,
        mesh=split,
        in_specs=(
            P(CNEC, BUS),
            P(BUS),
            P(BUS),
            P(),
            P("act", None),
            P(),
            P(CNEC + BUS),
        ),
        out_specs=(
            P("act", CNEC + BUS, None),
            P("act", CNEC + BUS),
            P("act", CNEC + BUS),
        ),
        check_vma=False,
    )
```

```python
import jax
import jax.numpy as jnp
from jax import lax
from jax.experimental import pallas as pl
from jax.experimental.pallas import tpu as pltpu
from jax.sharding import Mesh
from jax.sharding import PartitionSpec as P

HIGHEST = lax.Precision.HIGHEST
LANES = 128
HALF = 64
SUB = 8
BLOCK = 2048
SLOTS = 64
BLOCK_ROWS = SLOTS // 2 + SUB
SUMMED = 2 * SUB + BLOCK_ROWS
CNEC, BUS = ("yl", "x"), ("z", "yh")


def iota(shape, dim):
    return lax.broadcasted_iota(jnp.int32, shape, dim)


def dot_nt(x, y, precision=None):
    return lax.dot_general(
        x, y, (((1,), (1,)), ((), ())), precision=precision, preferred_element_type=jnp.float32
    )


def dot(x, y, precision=None):
    return jnp.dot(x, y, precision=precision, preferred_element_type=jnp.float32)


def two_parts(values):
    high = values.astype(jnp.bfloat16)
    return high, (values - high.astype(jnp.float32)).astype(jnp.bfloat16)


def by_parts(product, x, y):
    x_high, x_low = two_parts(x)
    y_high, y_low = two_parts(y)
    return product(x_high, y_high) + product(x_high, y_low) + product(x_low, y_high)


def digits(values, base, count):
    return [((values >> (base * at)) & ((1 << base) - 1)).astype(jnp.float32).astype(jnp.bfloat16)
            for at in reversed(range(count))]


def find_picks(swt, branch_ref):
    rank, actions = swt.shape
    picks = rank * actions
    pick_id = iota((picks, actions), 0)
    of_action = pick_id % LANES // rank * 2 + pick_id // LANES == iota((picks, actions), 1)
    of_action = jnp.where(of_action, 1.0, 0.0).astype(jnp.bfloat16)
    high, low = digits(swt, 6, 2)
    row = dot_nt(high, of_action) * 64.0 + dot_nt(low, of_action)
    row = jnp.where(iota((rank, picks), 1) % rank == iota((rank, picks), 0), row, 0.0)
    row = jnp.sum(row, axis=0, keepdims=True).astype(jnp.int32)
    tiles = branch_ref.shape[1] // LANES
    table = jnp.concatenate(
        [branch_ref[:, at * LANES:(at + 1) * LANES] for at in range(tiles)], axis=0
    )
    onehot = jnp.where(iota((LANES, picks), 0) == row % LANES, 1.0, 0.0).astype(jnp.bfloat16)
    high, middle, low = [dot(part, onehot) for part in digits(table, 6, 3)]
    found = high * 4096.0 + middle * 64.0 + low
    line = iota((2 * tiles, picks), 0) - row // LANES * 2
    ends = [
        jnp.sum(jnp.where(line == end, found, 0.0), axis=0, keepdims=True).astype(jnp.int32)
        for end in (0, 1)
    ]
    return row, ends


def slot_matrix(slots, count):
    shape = (count, slots[0].shape[1])
    first, second = [jnp.where(iota(shape, 0) == slot, 1.0, 0.0) for slot in slots]
    return (first - second).astype(jnp.bfloat16)


def partial_kernel(
    swt_hbm, branch_hbm, weight_hbm, zone_hbm, sens_hbm, pay_ref, meta_ref,
    swt_ref, branch_ref, weight_ref, zone_ref, sens_ref, acc_ref, coupled_ref, sems
):
    cols = sens_ref.shape[1]
    rows = sens_ref.shape[0] - 2 * SUB
    rank, actions = swt_ref.shape
    picks = rank * actions
    zones = HALF
    steps = cols // BLOCK
    bf16 = jnp.bfloat16
    small = [
        pltpu.make_async_copy(source, target, sems.at[steps + at])
        for at, (source, target) in enumerate(
            [(swt_hbm, swt_ref), (branch_hbm, branch_ref), (weight_hbm, weight_ref), (zone_hbm, zone_ref)]
        )
    ]
    for copy in small:
        copy.start()

    def block_copy(step):
        at = pl.ds(pl.multiple_of(step * BLOCK, BLOCK), BLOCK)
        return pltpu.make_async_copy(sens_hbm.at[:, at], sens_ref.at[0:rows, at], sems.at[step])

    for step in range(steps):
        block_copy(step).start()

    shard = lax.axis_index(BUS)
    row_start = lax.axis_index(CNEC) * rows
    acc_ref[...] = jnp.zeros_like(acc_ref)
    sens_ref[rows:, :] = jnp.ones((sens_ref.shape[0] - rows, cols), bf16)

    for copy in small[:2]:
        copy.wait()
    row, ends = find_picks(swt_ref[...], branch_ref)

    def ranks(owner, owners):
        count = owner.shape[1]
        inside = iota((owners, count), 0) == owner
        before = jnp.where(iota((count, count), 0) < iota((count, count), 1), 1.0, 0.0)
        place = dot(jnp.where(inside, 1.0, 0.0).astype(bf16), before.astype(bf16))
        return jnp.sum(jnp.where(inside, place, 0.0), axis=0, keepdims=True)

    bus = jnp.concatenate(ends, axis=1)
    count = 2 * picks
    held, place = bus // cols, ranks(bus // cols, lax.axis_size(BUS))
    owner, row_place = row // rows, ranks(row // rows, lax.axis_size(CNEC))
    most = jnp.maximum(
        jnp.max(place, axis=1, keepdims=True), jnp.max(row_place, axis=1, keepdims=True)
    )
    over = jnp.where(most >= SLOTS, 1.0, 0.0)
    meta_ref[0:1, :] = held.astype(jnp.float32)
    meta_ref[1:2, :] = place
    meta_ref[2:3, :] = jnp.broadcast_to(over, (1, count))
    meta_ref[3:4, :] = jnp.concatenate([owner.astype(jnp.float32), row_place], axis=1)
    meta_ref[4:, :] = jnp.zeros((SUB - 4, count), jnp.float32)
    place = place.astype(jnp.int32)
    mine = held == shard
    slot = jnp.where(mine, place, -1)
    local = bus - shard * cols

    def buses_of(group):
        match = iota((SLOTS, count), 0) + group * SLOTS == slot
        return jnp.sum(jnp.where(match, (local + 1).astype(jnp.float32), 0.0), axis=1, keepdims=True).astype(jnp.int32) - 1

    first_buses = buses_of(0)
    row_slot = jnp.where(owner == lax.axis_index(CNEC), row_place.astype(jnp.int32), -1)
    match = iota((SLOTS, picks), 0) == row_slot
    slot_row = jnp.where(match, (row - row_start + 1).astype(jnp.float32), 0.0)
    slot_row = jnp.sum(slot_row, axis=1, keepdims=True).astype(jnp.int32) - 1
    action_of = iota((SLOTS, picks), 1) // rank
    slot_action = jnp.where(match, action_of.astype(jnp.float32), 0.0)
    slot_action = jnp.sum(slot_action, axis=1, keepdims=True).astype(jnp.int32)
    zone_id = iota((zones, BLOCK), 0).astype(jnp.float32).astype(bf16)
    lane = iota((SLOTS, BLOCK), 1)
    for copy in small[2:]:
        copy.wait()

    def select(buses, step):
        return jnp.where(lane == buses - step * BLOCK, 1.0, 0.0).astype(bf16)

    def step_body(step, carry):
        at = pl.ds(pl.multiple_of(step * BLOCK, BLOCK), BLOCK)
        inside = zone_ref[:, at].astype(jnp.float32).astype(bf16) == zone_id
        high, low = two_parts(weight_ref[:, at])
        key = jnp.concatenate(
            [
                jnp.where(inside, high, bf16(0.0)),
                jnp.where(inside, low, bf16(0.0)),
                select(first_buses, step),
            ],
            axis=0,
        )
        block_copy(step).wait()
        acc_ref[...] += dot_nt(sens_ref[:, at], key)
        return carry

    lax.fori_loop(0, steps, step_body, 0)

    chunks = pay_ref.shape[0]
    zonal = acc_ref[0:rows, 0:zones] + acc_ref[0:rows, zones:2 * zones]
    total = acc_ref[rows:rows + 1, 0:2 * zones]
    total = total + pltpu.roll(total, HALF, 1)
    total = jnp.where(iota((1, LANES), 1) < HALF, 0.0, total)
    held_columns = acc_ref[0:rows, 2 * zones:]
    choose = jnp.where(iota((SLOTS, rows), 1) == slot_row, 1.0, 0.0).astype(bf16)
    chosen = dot(
        choose, jnp.concatenate([*two_parts(zonal), held_columns.astype(bf16)], axis=1)
    )
    switched = chosen[:, 0:zones] + chosen[:, zones:2 * zones]

    def coupled_of(chosen_columns, group):
        slots = [slot[:, at * picks:(at + 1) * picks] - group * SLOTS for at in (0, 1)]
        return dot(chosen_columns.astype(bf16), slot_matrix(slots, SLOTS))

    coupled_ref[...] = coupled_of(chosen[:, 2 * zones:], 0)

    def group_body(group, carry):
        buses = buses_of(group)
        columns = jnp.zeros((rows, SLOTS), jnp.float32)
        for step in range(steps):
            at = pl.ds(step * BLOCK, BLOCK)
            columns += dot_nt(sens_ref[0:rows, at], select(buses, step))
        coupled_ref[...] += coupled_of(dot(choose, columns.astype(bf16)), group)
        return carry

    groups = (jnp.sum(jnp.where(mine, 1.0, 0.0)).astype(jnp.int32) + SLOTS - 1) // SLOTS
    lax.fori_loop(1, groups, group_body, 0)

    coupled = jnp.where(action_of == slot_action, coupled_ref[...], 0.0)
    fold = jnp.where(iota((picks, LANES), 0) % rank == iota((picks, LANES), 1) % rank, 1.0, 0.0)
    high, low = [dot(part, fold.astype(bf16)) for part in two_parts(coupled)]
    shape = (SLOTS, LANES)
    coupled = jnp.where(iota(shape, 1) // rank == iota(shape, 0) // SUB, high + low, 0.0)
    coupled = jnp.sum(coupled.reshape(SLOTS // SUB, SUB, LANES), axis=0)

    share = zonal.reshape(chunks, 2, 2, 2, SUB, zones)
    share = jnp.where(lax.axis_index("act") == 0, share[:, :, 0], share[:, :, 1])
    share = jnp.concatenate([share[:, :, 0], share[:, :, 1]], axis=-1)
    half = SLOTS // 2
    switched = jnp.concatenate([switched[:half], switched[half:]], axis=1)
    block = jnp.concatenate([switched, coupled + total], axis=0)
    held_columns = held_columns.reshape(chunks, 2, rows // chunks // 2, SLOTS)
    pay_ref[:, 0:2 * SUB, :] = share.reshape(chunks, 2 * SUB, LANES)
    pay_ref[:, 2 * SUB:SUMMED, :] = jnp.broadcast_to(block[None], (chunks, *block.shape))
    pay_ref[:, SUMMED:, :] = jnp.concatenate([held_columns[:, 0], held_columns[:, 1]], axis=-1)


def place_kernel(parts_ref, local_ref, meta_ref, mine_ref, theirs_ref):
    chunks = parts_ref.shape[0]
    picks = meta_ref.shape[1] // 2
    half = parts_ref.shape[1] - SUMMED
    y_here, y_size = lax.axis_index("yh"), lax.axis_size("yh")
    held = meta_ref[0:1, :].astype(jnp.int32)
    place = meta_ref[1:2, :].astype(jnp.int32)
    known = (held % y_size == y_here) & (place < SLOTS)
    slot = jnp.where(known, held // y_size * SLOTS + place, -1)
    spread = slot_matrix([slot[:, at * picks:(at + 1) * picks] for at in (0, 1)], chunks * SLOTS)
    columns = [
        jnp.concatenate(
            [parts_ref[z, SUMMED:, at * SLOTS:(at + 1) * SLOTS] for z in range(chunks)], axis=1
        )
        for at in (0, 1)
    ]
    columns = jnp.concatenate(columns, axis=0).astype(jnp.bfloat16)
    diff = lax.dot_general(
        spread, columns, (((0,), (1,)), ((), ())), preferred_element_type=jnp.float32
    )
    diff = diff.reshape(2, picks // (2 * SUB), SUB, 2 * half)
    diff = jnp.concatenate([diff[0], diff[1]], axis=1).reshape(4, picks // 4, 2 * half)
    lower = y_here == 0
    packed = [
        jnp.concatenate([diff[g, :, at * half:(at + 1) * half] for g in range(4)], axis=1)
        for at in (0, 1)
    ]
    for ref, first in ((mine_ref, lower), (theirs_ref, ~lower)):
        ref[0:SUB, :] = jnp.where(first, local_ref[0:SUB, :], local_ref[SUB:2 * SUB, :])
        ref[SUB:, :] = jnp.where(first, packed[0], packed[1])


def copy_kernel(*refs):
    count = len(refs) // 2
    copies = [
        pltpu.make_async_copy(refs[at], refs[count + at], refs[-1].at[at]) for at in range(count)
    ]
    for copy in copies:
        copy.start()
    for copy in copies:
        copy.wait()


def final_kernel(
    meta_ref, mine_ref, theirs_ref, other_ref, here_ref, x1_ref, x2_ref, x3_ref, position_ref,
    limit_ref, after_ref, loading_ref, margin_ref
):
    actions, share, zones = after_ref.shape
    pairs = actions // 2
    picks = actions * SUB
    bf16 = jnp.bfloat16

    size_x = lax.axis_size("x")
    owner = meta_ref[3:4, :picks].astype(jnp.int32)
    slot = meta_ref[3:4, picks:].astype(jnp.int32)
    back = (lax.axis_index("x") - owner % size_x + size_x) % size_x
    flip = jnp.where(owner // size_x == lax.axis_index("yl"), 0, 1)
    blocks = [
        ref[at * BLOCK_ROWS:(at + 1) * BLOCK_ROWS, :]
        for ref in (here_ref, x1_ref, x2_ref, x3_ref)
        for at in (0, 1)
    ]
    count = len(blocks) * SLOTS
    spread = iota((count, picks), 0) == (back * 2 + flip) * SLOTS + slot
    spread = jnp.where(spread, 1.0, 0.0).astype(bf16)
    half = SLOTS // 2
    switched, coupled = [], []
    lane = iota((half, LANES), 1)
    for block in blocks:
        rows = block[0:half]
        turned = pltpu.roll(rows, HALF, 1)
        switched += [jnp.where(lane < HALF, rows, turned), jnp.where(lane < HALF, turned, rows)]
        extra = block[half:]
        for g in range(SLOTS // SUB):
            coupled.append(jnp.where(iota(extra.shape, 1) // SUB == g, extra, 0.0))
    parts = two_parts(jnp.concatenate(switched, axis=0)) + two_parts(jnp.concatenate(coupled, axis=0))
    found = lax.dot_general(
        spread, jnp.concatenate(parts, axis=1), (((0,), (0,)), ((), ())),
        preferred_element_type=jnp.float32,
    )
    switched = found[:, 0:LANES] + found[:, LANES:2 * LANES]
    coupled = found[:, 2 * LANES:3 * LANES] + found[:, 3 * LANES:]
    shape = (LANES, LANES)
    repeat = (iota(shape, 0) < SLOTS) & (iota(shape, 0) % SUB == iota(shape, 1) % SUB)
    repeat = jnp.where(repeat, 1.0, 0.0).astype(bf16)
    high, low = [dot(part, repeat) for part in two_parts(coupled)]
    coupled = high + low

    total = here_ref[half:half + 1, HALF:]
    total = jnp.concatenate([total, total], axis=1)
    shape = (pairs, SUB, LANES)
    row_id, lane = iota(shape, 1), iota(shape, 2)

    def side_by_side(x):
        return jnp.where(
            lane < HALF, x[:picks // 2].reshape(shape), x[picks // 2:].reshape(shape)
        )

    left = jnp.where(lane % SUB == row_id, 1.0, 0.0) - side_by_side(coupled)
    right = side_by_side(switched) / total[None]
    for pivot in range(SUB):
        factor = jnp.where(
            lane < HALF, left[:, :, pivot:pivot + 1], left[:, :, HALF + pivot:HALF + pivot + 1]
        )
        diagonal = factor[:, pivot:pivot + 1]
        left_now = left[:, pivot:pivot + 1] / diagonal
        right_now = right[:, pivot:pivot + 1] / diagonal
        left = jnp.where(row_id == pivot, left_now, left - factor * left_now)
        right = jnp.where(row_id == pivot, right_now, right - factor * right_now)

    lower = lax.axis_index("act") == 0
    whole = mine_ref[...] + theirs_ref[BLOCK_ROWS:]
    mine, other = whole[0:SUB], other_ref[...]
    low, high = jnp.where(lower, mine, other), jnp.where(lower, other, mine)
    zonal = jnp.concatenate(
        [low[:, :HALF], low[:, HALF:], high[:, :HALF], high[:, HALF:]], axis=0
    ) / total[:, :HALF]
    zonal_twice = jnp.concatenate([zonal, zonal], axis=1)
    groups = [whole[SUB:, g * share:(g + 1) * share] for g in range(LANES // share)]
    diff = jnp.concatenate(groups, axis=0)
    solved = jnp.concatenate(
        [jnp.where(lane < HALF, right, 0.0), jnp.where(lane < HALF, 0.0, right)], axis=1
    )
    diff_high, diff_low = two_parts(diff)
    solved_high, solved_low = two_parts(solved)

    def product(x, y):
        return lax.dot_general(
            x, y, (((0,), (0,)), ((), ())), preferred_element_type=jnp.float32
        )

    size = 2 * SUB
    for pair in range(pairs):
        at = slice(pair * size, (pair + 1) * size)
        left = jnp.concatenate([diff_high[at], diff_high[at], diff_low[at]], axis=0)
        right = jnp.concatenate(
            [solved_high[pair], solved_low[pair], solved_high[pair]], axis=0
        )
        total = zonal_twice + product(left, right)
        after_ref[2 * pair] = total[:, :HALF]
        after_ref[2 * pair + 1] = total[:, HALF:]
    position = position_ref[...]
    twice = jnp.concatenate([position, position], axis=1)
    moved = by_parts(dot_nt, twice, solved.reshape(pairs * size, LANES))
    shape = (actions, pairs * size)
    same = iota(shape, 1) // SUB == iota(shape, 0)
    flow = by_parts(dot_nt, position, zonal) + by_parts(dot, jnp.where(same, moved, 0.0), diff)
    limit = limit_ref[...]
    loading_ref[...] = flow / limit
    margin_ref[...] = limit - jnp.abs(flow)


def in_hbm(x):
    return pltpu.with_memory_space_constraint(x, pltpu.HBM)


def copied(arrays):
    hbm = pl.BlockSpec(memory_space=pltpu.HBM)
    return pl.pallas_call(
        copy_kernel,
        out_shape=[jax.ShapeDtypeStruct(x.shape, x.dtype) for x in arrays],
        in_specs=[hbm] * len(arrays),
        out_specs=[hbm] * len(arrays),
        scratch_shapes=[pltpu.SemaphoreType.DMA((len(arrays),))],
        name="copies",
    )(*[in_hbm(x) for x in arrays])


def params():
    return pltpu.CompilerParams(vmem_limit_bytes=48 * 1024 * 1024)


def body(
    nodal_sensitivity, shift_weight, bus_zone, branch_buses, switched_rows, net_position, flow_limit
):
    rows, cols = nodal_sensitivity.shape
    zones = net_position.shape[0]
    actions, rank = switched_rows.shape
    picks = actions * rank
    n_z, n_yh = lax.axis_size("z"), lax.axis_size("yh")
    share = rows // n_z // n_yh
    f32, i32 = jnp.float32, jnp.int32
    vmem = pl.BlockSpec(memory_space=pltpu.VMEM)
    hbm = pl.BlockSpec(memory_space=pltpu.HBM)

    weight, zone = shift_weight.reshape(1, cols), bus_zone.reshape(1, cols)
    pay, meta = pl.pallas_call(
        partial_kernel,
        out_shape=(
            jax.ShapeDtypeStruct((n_z, SUMMED + share, LANES), f32),
            jax.ShapeDtypeStruct((SUB, 2 * picks), f32),
        ),
        in_specs=[hbm] * 5,
        out_specs=(vmem, vmem),
        scratch_shapes=[
            pltpu.VMEM((rank, actions), i32),
            pltpu.VMEM(branch_buses.shape, i32),
            pltpu.VMEM((1, cols), f32),
            pltpu.VMEM((1, cols), i32),
            pltpu.VMEM((rows + 2 * SUB, cols), jnp.bfloat16),
            pltpu.VMEM((rows + 2 * SUB, 2 * zones + SLOTS), f32),
            pltpu.VMEM((SLOTS, picks), f32),
            pltpu.SemaphoreType.DMA((cols // BLOCK + 4,)),
        ],
        compiler_params=params(),
        name="partials",
    )(
        *[in_hbm(x) for x in (switched_rows.T, branch_buses, weight, zone, nodal_sensitivity)]
    )

    swap = [(0, 1), (1, 0)]
    parts = lax.all_to_all(pay, "z", 0, 0, tiled=True)
    local = jnp.sum(parts[:, :SUMMED], axis=0)
    part = jax.ShapeDtypeStruct((SUB + 2 * share, LANES), f32)
    mine, theirs = pl.pallas_call(
        place_kernel,
        out_shape=(part, part),
        in_specs=[vmem] * 3,
        out_specs=(vmem, vmem),
        compiler_params=params(),
        name="place",
    )(parts, local, meta)

    block = local[2 * SUB:]
    theirs = lax.ppermute(jnp.concatenate([block, theirs], axis=0), "yh", swap)
    beside = lax.ppermute(block, "yl", swap)
    across = lax.ppermute(block, ("yl", "yh"), [(0, 3), (3, 0), (1, 2), (2, 1)])
    here = jnp.concatenate([block + theirs[:BLOCK_ROWS], beside + across], axis=0)
    n_x = lax.axis_size("x")
    others = [
        lax.ppermute(here, "x", [(at, (at + by) % n_x) for at in range(n_x)])
        for by in range(1, n_x)
    ]
    other = lax.ppermute(
        mine[:SUB] + theirs[BLOCK_ROWS:BLOCK_ROWS + SUB], "act", swap
    )

    def compact():
        outputs = pl.pallas_call(
            final_kernel,
            out_shape=(
                jax.ShapeDtypeStruct((actions, share, zones), f32),
                jax.ShapeDtypeStruct((actions, share), f32),
                jax.ShapeDtypeStruct((actions, share), f32),
            ),
            in_specs=[vmem] * 10,
            out_specs=(vmem, vmem, vmem),
            compiler_params=params(),
            name="update",
        )(
            meta, mine, theirs, other, here, *others,
            net_position.reshape(1, zones), flow_limit.reshape(1, share),
        )
        return tuple(outputs)

    def general():
        inputs = nodal_sensitivity, shift_weight, bus_zone, branch_buses, switched_rows
        return tuple(copied(plain(*copied(inputs), net_position, flow_limit)))

    return lax.cond(meta[2, 0] > 0.5, general, compact)


def sum_over(x, axes):
    spread = jnp.broadcast_to(x[None], (lax.axis_size(axes), *x.shape))
    return jnp.sum(lax.all_to_all(spread, axes, 0, 0, tiled=True), axis=0)


def scattered_sum(x):
    shares = lax.axis_size(BUS)
    x = x.reshape(shares, x.shape[0] // shares, x.shape[1])
    return jnp.sum(lax.all_to_all(x, BUS, 0, 0, tiled=True), axis=0)


def plain(
    nodal_sensitivity, shift_weight, bus_zone, branch_buses, switched_rows, net_position, flow_limit
):
    rows, cols = nodal_sensitivity.shape
    zones = net_position.shape[0]
    actions, rank = switched_rows.shape
    onehot = (bus_zone[:, None] == jnp.arange(zones)[None, :]).astype(jnp.float32)
    total = sum_over(jnp.sum(onehot * shift_weight[:, None], axis=0), BUS)
    key = (onehot * shift_weight[:, None] / total[None, :]).astype(jnp.bfloat16)
    zonal = jnp.dot(nodal_sensitivity, key, preferred_element_type=jnp.float32)
    picks = switched_rows.reshape(-1)

    def columns(buses):
        local = buses - lax.axis_index(BUS) * cols
        owned = (local >= 0) & (local < cols)
        picked = jnp.take(nodal_sensitivity, jnp.clip(local, 0, cols - 1), axis=1)
        return jnp.where(owned[None, :], picked.astype(jnp.float32), 0.0)

    diff = columns(branch_buses[0][picks]) - columns(branch_buses[1][picks])
    zonal, diff = scattered_sum(zonal), scattered_sum(diff)
    share = rows // lax.axis_size(BUS)
    local = picks - lax.axis_index(CNEC) * rows - lax.axis_index(BUS) * share
    owned = ((local >= 0) & (local < share))[:, None]
    local = jnp.clip(local, 0, share - 1)
    switched = jnp.where(owned, jnp.take(zonal, local, axis=0), 0.0)
    coupled = jnp.where(owned, jnp.take(diff, local, axis=0), 0.0)
    coupled = jnp.einsum("aiaj->aij", coupled.reshape(actions, rank, actions, rank))
    both = jnp.concatenate([switched, coupled.reshape(actions * rank, rank)], axis=1)
    both = sum_over(sum_over(both, BUS), CNEC).reshape(actions, rank, zones + rank)
    left, right = jnp.eye(rank, dtype=jnp.float32)[None] - both[:, :, zones:], both[:, :, :zones]
    for pivot in range(rank):
        is_pivot = (jnp.arange(rank) == pivot)[None, :, None]
        factor = left[:, :, pivot:pivot + 1]
        diagonal = factor[:, pivot:pivot + 1]
        left_now, right_now = left[:, pivot:pivot + 1] / diagonal, right[:, pivot:pivot + 1] / diagonal
        left = jnp.where(is_pivot, left_now, left - factor * left_now)
        right = jnp.where(is_pivot, right_now, right - factor * right_now)
    after = zonal[None] + jnp.einsum(
        "caj,ajz->acz", diff.reshape(share, actions, rank), right, precision=HIGHEST
    )
    flow = jnp.einsum("acz,z->ac", after, net_position, precision=HIGHEST)
    return after, flow / flow_limit[None, :], flow_limit[None, :] - jnp.abs(flow)


def solution(mesh):
    n_cnec, n_bus, n_act = mesh.devices.shape
    split = Mesh(
        mesh.devices.reshape(2, n_cnec // 2, n_bus // 2, 2, n_act), ("yl", "x", "z", "yh", "act")
    )
    return jax.shard_map(
        body,
        mesh=split,
        in_specs=(
            P(CNEC, BUS),
            P(BUS),
            P(BUS),
            P(),
            P("act", None),
            P(),
            P(CNEC + BUS),
        ),
        out_specs=(
            P("act", CNEC + BUS, None),
            P("act", CNEC + BUS),
            P("act", CNEC + BUS),
        ),
        check_vma=False,
    )
```

```python
import jax
import jax.numpy as jnp
from jax import lax
from jax.experimental import pallas as pl
from jax.experimental.pallas import tpu as pltpu
from jax.sharding import Mesh
from jax.sharding import PartitionSpec as P

HIGHEST = lax.Precision.HIGHEST
LANES = 128
HALF = 64
SUB = 8
BLOCK = 2048
SLOTS = 64
BLOCK_ROWS = SLOTS // 2 + SUB
SUMMED = 2 * SUB + BLOCK_ROWS
CNEC, BUS = ("yl", "x"), ("z", "yh")


def iota(shape, dim):
    return lax.broadcasted_iota(jnp.int32, shape, dim)


def dot_nt(x, y, precision=None):
    return lax.dot_general(
        x, y, (((1,), (1,)), ((), ())), precision=precision, preferred_element_type=jnp.float32
    )


def dot(x, y, precision=None):
    return jnp.dot(x, y, precision=precision, preferred_element_type=jnp.float32)


def two_parts(values):
    high = values.astype(jnp.bfloat16)
    return high, (values - high.astype(jnp.float32)).astype(jnp.bfloat16)


def three_parts(values):
    high = values.astype(jnp.bfloat16)
    rest = values - high.astype(jnp.float32)
    middle = rest.astype(jnp.bfloat16)
    return high, middle, (rest - middle.astype(jnp.float32)).astype(jnp.bfloat16)


def by_parts(product, x, y):
    x_high, x_low = two_parts(x)
    y_high, y_low = two_parts(y)
    return product(x_high, y_high) + product(x_high, y_low) + product(x_low, y_high)


def digits(values, base, count):
    return [((values >> (base * at)) & ((1 << base) - 1)).astype(jnp.float32).astype(jnp.bfloat16)
            for at in reversed(range(count))]


def find_picks(swt, branch_ref):
    rank, actions = swt.shape
    picks = rank * actions
    pick_id = iota((picks, actions), 0)
    of_action = pick_id % LANES // rank * 2 + pick_id // LANES == iota((picks, actions), 1)
    of_action = jnp.where(of_action, 1.0, 0.0).astype(jnp.bfloat16)
    high, low = digits(swt, 6, 2)
    row = dot_nt(high, of_action) * 64.0 + dot_nt(low, of_action)
    row = jnp.where(iota((rank, picks), 1) % rank == iota((rank, picks), 0), row, 0.0)
    row = jnp.sum(row, axis=0, keepdims=True).astype(jnp.int32)
    tiles = branch_ref.shape[1] // LANES
    table = jnp.concatenate(
        [branch_ref[:, at * LANES:(at + 1) * LANES] for at in range(tiles)], axis=0
    )
    onehot = jnp.where(iota((LANES, picks), 0) == row % LANES, 1.0, 0.0).astype(jnp.bfloat16)
    high, middle, low = [dot(part, onehot) for part in digits(table, 6, 3)]
    found = high * 4096.0 + middle * 64.0 + low
    line = iota((2 * tiles, picks), 0) - row // LANES * 2
    ends = [
        jnp.sum(jnp.where(line == end, found, 0.0), axis=0, keepdims=True).astype(jnp.int32)
        for end in (0, 1)
    ]
    return row, ends


def slot_matrix(slots, count):
    shape = (count, slots[0].shape[1])
    first, second = [jnp.where(iota(shape, 0) == slot, 1.0, 0.0) for slot in slots]
    return (first - second).astype(jnp.bfloat16)


def total_kernel(weight_hbm, zone_hbm, out_ref, weight_ref, zone_ref, sems):
    copies = [
        pltpu.make_async_copy(weight_hbm, weight_ref, sems.at[0]),
        pltpu.make_async_copy(zone_hbm, zone_ref, sems.at[1]),
    ]
    for copy in copies:
        copy.start()
    for copy in copies:
        copy.wait()
    ids = iota((HALF, LANES), 0)
    total = jnp.zeros((HALF, LANES), jnp.float32)
    for start in range(0, weight_ref.shape[1], LANES):
        at = pl.ds(start, LANES)
        total += jnp.where(zone_ref[:, at] == ids, weight_ref[:, at], 0.0)
    total = jnp.sum(total, axis=1, keepdims=True)
    total = jnp.sum(jnp.where(ids == iota((HALF, LANES), 1), total, 0.0), axis=0, keepdims=True)
    out_ref[...] = jnp.broadcast_to(total[None], out_ref.shape)


def column_kernel(
    swt_hbm, branch_hbm, sens_hbm, held_ref, meta_ref, extra_ref, sens_ref,
    swt_ref, branch_ref, acc_ref, coupled_ref, sems
):
    rows, cols = sens_ref.shape
    rank, actions = swt_ref.shape
    picks = rank * actions
    steps = cols // BLOCK
    bf16 = jnp.bfloat16
    small = [
        pltpu.make_async_copy(swt_hbm, swt_ref, sems.at[steps]),
        pltpu.make_async_copy(branch_hbm, branch_ref, sems.at[steps + 1]),
    ]
    for copy in small:
        copy.start()

    def block_copy(step):
        at = pl.ds(pl.multiple_of(step * BLOCK, BLOCK), BLOCK)
        return pltpu.make_async_copy(sens_hbm.at[:, at], sens_ref.at[:, at], sems.at[step])

    for step in range(steps):
        block_copy(step).start()

    shard = lax.axis_index(BUS)
    row_start = lax.axis_index(CNEC) * rows
    acc_ref[...] = jnp.zeros_like(acc_ref)
    for copy in small:
        copy.wait()
    row, ends = find_picks(swt_ref[...], branch_ref)

    def ranks(owner, owners):
        count = owner.shape[1]
        inside = iota((owners, count), 0) == owner
        before = jnp.where(iota((count, count), 0) < iota((count, count), 1), 1.0, 0.0)
        place = dot(jnp.where(inside, 1.0, 0.0).astype(bf16), before.astype(bf16))
        return jnp.sum(jnp.where(inside, place, 0.0), axis=0, keepdims=True)

    bus = jnp.concatenate(ends, axis=1)
    count = 2 * picks
    held, place = bus // cols, ranks(bus // cols, lax.axis_size(BUS))
    owner, row_place = row // rows, ranks(row // rows, lax.axis_size(CNEC))
    most = jnp.maximum(
        jnp.max(place, axis=1, keepdims=True), jnp.max(row_place, axis=1, keepdims=True)
    )
    over = jnp.where(most >= SLOTS, 1.0, 0.0)
    meta_ref[0:1, :] = held.astype(jnp.float32)
    meta_ref[1:2, :] = place
    meta_ref[2:3, :] = jnp.broadcast_to(over, (1, count))
    meta_ref[3:4, :] = jnp.concatenate([owner.astype(jnp.float32), row_place], axis=1)
    meta_ref[4:, :] = jnp.zeros((SUB - 4, count), jnp.float32)
    place = place.astype(jnp.int32)
    mine = held == shard
    slot = jnp.where(mine, place, -1)
    local = bus - shard * cols

    def buses_of(group):
        match = iota((SLOTS, count), 0) + group * SLOTS == slot
        match = jnp.where(match, (local + 1).astype(jnp.float32), 0.0)
        return jnp.sum(match, axis=1, keepdims=True).astype(jnp.int32) - 1

    first_buses = buses_of(0)
    row_slot = jnp.where(owner == lax.axis_index(CNEC), row_place.astype(jnp.int32), -1)
    match = iota((SLOTS, picks), 0) == row_slot
    slot_row = jnp.where(match, (row - row_start + 1).astype(jnp.float32), 0.0)
    slot_row = jnp.sum(slot_row, axis=1, keepdims=True) - 1.0
    action_of = iota((SLOTS, picks), 1) // rank
    slot_action = jnp.where(match, action_of.astype(jnp.float32), 0.0)
    slot_action = jnp.sum(slot_action, axis=1, keepdims=True).astype(jnp.int32)
    extra_ref[0:SLOTS, :] = jnp.broadcast_to(slot_row, (SLOTS, LANES))
    choose = iota((SLOTS, rows), 1) == slot_row.astype(jnp.int32)
    choose = jnp.where(choose, 1.0, 0.0).astype(bf16)
    lane = iota((SLOTS, BLOCK), 1)

    def select(buses, step):
        return jnp.where(lane == buses - step * BLOCK, 1.0, 0.0).astype(bf16)

    def step_body(step, carry):
        at = pl.ds(pl.multiple_of(step * BLOCK, BLOCK), BLOCK)
        chosen = select(first_buses, step)
        block_copy(step).wait()
        acc_ref[...] += dot_nt(sens_ref[:, at], chosen)
        return carry

    lax.fori_loop(0, steps, step_body, 0)

    def coupled_of(columns, group):
        slots = [slot[:, at * picks:(at + 1) * picks] - group * SLOTS for at in (0, 1)]
        chosen = dot(choose, columns.astype(bf16))
        return dot(chosen.astype(bf16), slot_matrix(slots, SLOTS))

    columns = acc_ref[...]
    coupled_ref[...] = coupled_of(columns, 0)

    def group_body(group, carry):
        buses = buses_of(group)
        columns = jnp.zeros((rows, SLOTS), jnp.float32)
        for step in range(steps):
            at = pl.ds(step * BLOCK, BLOCK)
            columns += dot_nt(sens_ref[:, at], select(buses, step))
        coupled_ref[...] += coupled_of(columns, group)
        return carry

    groups = (jnp.sum(jnp.where(mine, 1.0, 0.0)).astype(jnp.int32) + SLOTS - 1) // SLOTS
    lax.fori_loop(1, groups, group_body, 0)

    coupled = jnp.where(action_of == slot_action, coupled_ref[...], 0.0)
    fold = jnp.where(iota((picks, LANES), 0) % rank == iota((picks, LANES), 1) % rank, 1.0, 0.0)
    high, low = [dot(part, fold.astype(bf16)) for part in two_parts(coupled)]
    shape = (SLOTS, LANES)
    coupled = jnp.where(iota(shape, 1) // rank == iota(shape, 0) // SUB, high + low, 0.0)
    extra_ref[SLOTS:, :] = jnp.sum(coupled.reshape(SLOTS // SUB, SUB, LANES), axis=0)
    chunks = held_ref.shape[0]
    columns = columns.reshape(chunks, 2, rows // chunks // 2, SLOTS)
    held_ref[...] = jnp.concatenate([columns[:, 0], columns[:, 1]], axis=-1)


def zonal_kernel(totals_ref, weight_hbm, zone_hbm, sens_ref, held_ref, extra_ref, pay_ref,
                 weight_ref, zone_ref, acc_ref, sems):
    copies = [
        pltpu.make_async_copy(weight_hbm, weight_ref, sems.at[0]),
        pltpu.make_async_copy(zone_hbm, zone_ref, sems.at[1]),
    ]
    for copy in copies:
        copy.start()
    rows, cols = sens_ref.shape
    zones = HALF
    bf16 = jnp.bfloat16
    acc_ref[...] = jnp.zeros_like(acc_ref)
    pay_ref[:, SUMMED:, :] = held_ref[...]
    total = jnp.sum(totals_ref[...], axis=0)[:, :zones]
    part = iota(total.shape, 0)
    high, middle, low = [x.astype(jnp.float32) for x in three_parts(total)]
    total = jnp.where(part == 0, high, jnp.where(part == 1, middle, low)).astype(bf16)
    zone_id = iota((zones, BLOCK), 0).astype(jnp.float32).astype(bf16)
    for copy in copies:
        copy.wait()

    def step_body(step, carry):
        at = pl.ds(pl.multiple_of(step * BLOCK, BLOCK), BLOCK)
        inside = zone_ref[:, at].astype(jnp.float32).astype(bf16) == zone_id
        of_bus = dot(total, jnp.where(inside, bf16(1.0), bf16(0.0)))
        of_bus = (of_bus[0:1] + of_bus[1:2]) + of_bus[2:3]
        key = (weight_ref[:, at] / of_bus).astype(bf16)
        acc_ref[...] += dot_nt(sens_ref[:, at], jnp.where(inside, key, bf16(0.0)))
        return carry

    lax.fori_loop(0, cols // BLOCK, step_body, 0)

    chunks = pay_ref.shape[0]
    zonal = acc_ref[...]
    choose = iota((SLOTS, rows), 1) == extra_ref[0:SLOTS, 0:1].astype(jnp.int32)
    choose = jnp.where(choose, 1.0, 0.0).astype(bf16)
    switched = dot(choose, jnp.concatenate(two_parts(zonal), axis=1))
    switched = switched[:, 0:zones] + switched[:, zones:]
    share = zonal.reshape(chunks, 2, 2, 2, SUB, zones)
    share = jnp.where(lax.axis_index("act") == 0, share[:, :, 0], share[:, :, 1])
    share = jnp.concatenate([share[:, :, 0], share[:, :, 1]], axis=-1)
    half = SLOTS // 2
    switched = jnp.concatenate([switched[:half], switched[half:]], axis=1)
    block = jnp.concatenate([switched, extra_ref[SLOTS:, :]], axis=0)
    pay_ref[:, 0:2 * SUB, :] = share.reshape(chunks, 2 * SUB, LANES)
    pay_ref[:, 2 * SUB:SUMMED, :] = jnp.broadcast_to(block[None], (chunks, *block.shape))


def place_kernel(parts_ref, local_ref, meta_ref, mine_ref, theirs_ref):
    chunks = parts_ref.shape[0]
    picks = meta_ref.shape[1] // 2
    half = parts_ref.shape[1] - SUMMED
    y_here, y_size = lax.axis_index("yh"), lax.axis_size("yh")
    held = meta_ref[0:1, :].astype(jnp.int32)
    place = meta_ref[1:2, :].astype(jnp.int32)
    known = (held % y_size == y_here) & (place < SLOTS)
    slot = jnp.where(known, held // y_size * SLOTS + place, -1)
    spread = slot_matrix([slot[:, at * picks:(at + 1) * picks] for at in (0, 1)], chunks * SLOTS)
    columns = [
        jnp.concatenate(
            [parts_ref[z, SUMMED:, at * SLOTS:(at + 1) * SLOTS] for z in range(chunks)], axis=1
        )
        for at in (0, 1)
    ]
    columns = jnp.concatenate(columns, axis=0).astype(jnp.bfloat16)
    diff = lax.dot_general(
        spread, columns, (((0,), (1,)), ((), ())), preferred_element_type=jnp.float32
    )
    diff = diff.reshape(2, picks // (2 * SUB), SUB, 2 * half)
    diff = jnp.concatenate([diff[0], diff[1]], axis=1).reshape(4, picks // 4, 2 * half)
    lower = y_here == 0
    packed = [
        jnp.concatenate([diff[g, :, at * half:(at + 1) * half] for g in range(4)], axis=1)
        for at in (0, 1)
    ]
    for ref, first in ((mine_ref, lower), (theirs_ref, ~lower)):
        ref[0:SUB, :] = jnp.where(first, local_ref[0:SUB, :], local_ref[SUB:2 * SUB, :])
        ref[SUB:, :] = jnp.where(first, packed[0], packed[1])


def copy_kernel(*refs):
    count = len(refs) // 2
    copies = [
        pltpu.make_async_copy(refs[at], refs[count + at], refs[-1].at[at]) for at in range(count)
    ]
    for copy in copies:
        copy.start()
    for copy in copies:
        copy.wait()


def final_kernel(
    meta_ref, mine_ref, theirs_ref, other_ref, here_ref, x1_ref, x2_ref, x3_ref, position_ref,
    limit_ref, after_ref, loading_ref, margin_ref
):
    actions, share, zones = after_ref.shape
    pairs = actions // 2
    picks = actions * SUB
    bf16 = jnp.bfloat16

    size_x = lax.axis_size("x")
    owner = meta_ref[3:4, :picks].astype(jnp.int32)
    slot = meta_ref[3:4, picks:].astype(jnp.int32)
    back = (lax.axis_index("x") - owner % size_x + size_x) % size_x
    flip = jnp.where(owner // size_x == lax.axis_index("yl"), 0, 1)
    blocks = [
        ref[at * BLOCK_ROWS:(at + 1) * BLOCK_ROWS, :]
        for ref in (here_ref, x1_ref, x2_ref, x3_ref)
        for at in (0, 1)
    ]
    count = len(blocks) * SLOTS
    spread = iota((count, picks), 0) == (back * 2 + flip) * SLOTS + slot
    spread = jnp.where(spread, 1.0, 0.0).astype(bf16)
    half = SLOTS // 2
    switched, coupled = [], []
    lane = iota((half, LANES), 1)
    for block in blocks:
        rows = block[0:half]
        turned = pltpu.roll(rows, HALF, 1)
        switched += [jnp.where(lane < HALF, rows, turned), jnp.where(lane < HALF, turned, rows)]
        extra = block[half:]
        for g in range(SLOTS // SUB):
            coupled.append(jnp.where(iota(extra.shape, 1) // SUB == g, extra, 0.0))
    parts = two_parts(jnp.concatenate(switched, axis=0)) + two_parts(jnp.concatenate(coupled, axis=0))
    found = lax.dot_general(
        spread, jnp.concatenate(parts, axis=1), (((0,), (0,)), ((), ())),
        preferred_element_type=jnp.float32,
    )
    switched = found[:, 0:LANES] + found[:, LANES:2 * LANES]
    coupled = found[:, 2 * LANES:3 * LANES] + found[:, 3 * LANES:]
    shape = (LANES, LANES)
    repeat = (iota(shape, 0) < SLOTS) & (iota(shape, 0) % SUB == iota(shape, 1) % SUB)
    repeat = jnp.where(repeat, 1.0, 0.0).astype(bf16)
    high, low = [dot(part, repeat) for part in two_parts(coupled)]
    coupled = high + low

    shape = (pairs, SUB, LANES)
    row_id, lane = iota(shape, 1), iota(shape, 2)

    def side_by_side(x):
        return jnp.where(
            lane < HALF, x[:picks // 2].reshape(shape), x[picks // 2:].reshape(shape)
        )

    left = jnp.where(lane % SUB == row_id, 1.0, 0.0) - side_by_side(coupled)
    right = side_by_side(switched)
    for pivot in range(SUB):
        factor = jnp.where(
            lane < HALF, left[:, :, pivot:pivot + 1], left[:, :, HALF + pivot:HALF + pivot + 1]
        )
        diagonal = factor[:, pivot:pivot + 1]
        left_now = left[:, pivot:pivot + 1] / diagonal
        right_now = right[:, pivot:pivot + 1] / diagonal
        left = jnp.where(row_id == pivot, left_now, left - factor * left_now)
        right = jnp.where(row_id == pivot, right_now, right - factor * right_now)

    lower = lax.axis_index("act") == 0
    whole = mine_ref[...] + theirs_ref[BLOCK_ROWS:]
    mine, other = whole[0:SUB], other_ref[...]
    low, high = jnp.where(lower, mine, other), jnp.where(lower, other, mine)
    zonal = jnp.concatenate(
        [low[:, :HALF], low[:, HALF:], high[:, :HALF], high[:, HALF:]], axis=0
    )
    zonal_twice = jnp.concatenate([zonal, zonal], axis=1)
    groups = [whole[SUB:, g * share:(g + 1) * share] for g in range(LANES // share)]
    diff = jnp.concatenate(groups, axis=0)
    solved = jnp.concatenate(
        [jnp.where(lane < HALF, right, 0.0), jnp.where(lane < HALF, 0.0, right)], axis=1
    )
    diff_high, diff_low = two_parts(diff)
    solved_high, solved_low = two_parts(solved)

    def product(x, y):
        return lax.dot_general(
            x, y, (((0,), (0,)), ((), ())), preferred_element_type=jnp.float32
        )

    size = 2 * SUB
    for pair in range(pairs):
        at = slice(pair * size, (pair + 1) * size)
        left = jnp.concatenate([diff_high[at], diff_high[at], diff_low[at]], axis=0)
        right = jnp.concatenate(
            [solved_high[pair], solved_low[pair], solved_high[pair]], axis=0
        )
        total = zonal_twice + product(left, right)
        after_ref[2 * pair] = total[:, :HALF]
        after_ref[2 * pair + 1] = total[:, HALF:]
    position = position_ref[...]
    twice = jnp.concatenate([position, position], axis=1)
    moved = by_parts(dot_nt, twice, solved.reshape(pairs * size, LANES))
    shape = (actions, pairs * size)
    same = iota(shape, 1) // SUB == iota(shape, 0)
    flow = by_parts(dot_nt, position, zonal) + by_parts(dot, jnp.where(same, moved, 0.0), diff)
    limit = limit_ref[...]
    loading_ref[...] = flow / limit
    margin_ref[...] = limit - jnp.abs(flow)


def in_hbm(x):
    return pltpu.with_memory_space_constraint(x, pltpu.HBM)


def in_vmem(x):
    return pltpu.with_memory_space_constraint(x, pltpu.VMEM)


def copied(arrays):
    hbm = pl.BlockSpec(memory_space=pltpu.HBM)
    return pl.pallas_call(
        copy_kernel,
        out_shape=[jax.ShapeDtypeStruct(x.shape, x.dtype) for x in arrays],
        in_specs=[hbm] * len(arrays),
        out_specs=[hbm] * len(arrays),
        scratch_shapes=[pltpu.SemaphoreType.DMA((len(arrays),))],
        name="copies",
    )(*[in_hbm(x) for x in arrays])


def params():
    return pltpu.CompilerParams(vmem_limit_bytes=48 * 1024 * 1024)


def body(
    nodal_sensitivity, shift_weight, bus_zone, branch_buses, switched_rows, net_position, flow_limit
):
    rows, cols = nodal_sensitivity.shape
    zones = net_position.shape[0]
    actions, rank = switched_rows.shape
    picks = actions * rank
    n_z, n_yh = lax.axis_size("z"), lax.axis_size("yh")
    share = rows // n_z // n_yh
    f32, i32 = jnp.float32, jnp.int32
    vmem = pl.BlockSpec(memory_space=pltpu.VMEM)
    hbm = pl.BlockSpec(memory_space=pltpu.HBM)

    weight, zone = shift_weight.reshape(1, cols), bus_zone.reshape(1, cols)
    weight, zone = in_hbm(weight), in_hbm(zone)
    bus_scratch = [pltpu.VMEM((1, cols), f32), pltpu.VMEM((1, cols), i32)]
    totals = pl.pallas_call(
        total_kernel,
        out_shape=jax.ShapeDtypeStruct((lax.axis_size(BUS), SUB, LANES), f32),
        in_specs=[hbm] * 2,
        out_specs=vmem,
        scratch_shapes=[*bus_scratch, pltpu.SemaphoreType.DMA((2,))],
        compiler_params=params(),
        name="totals",
    )(weight, zone)
    totals = lax.all_to_all(totals, BUS, 0, 0, tiled=True)
    held, meta, extra, sens = pl.pallas_call(
        column_kernel,
        out_shape=(
            pltpu.VMEM((n_z, share, LANES), f32),
            jax.ShapeDtypeStruct((SUB, 2 * picks), f32),
            pltpu.VMEM((SLOTS + SUB, LANES), f32),
            pltpu.VMEM((rows, cols), jnp.bfloat16),
        ),
        in_specs=[hbm] * 3,
        out_specs=(vmem,) * 4,
        scratch_shapes=[
            pltpu.VMEM((rank, actions), i32),
            pltpu.VMEM(branch_buses.shape, i32),
            pltpu.VMEM((rows, SLOTS), f32),
            pltpu.VMEM((SLOTS, picks), f32),
            pltpu.SemaphoreType.DMA((cols // BLOCK + 2,)),
        ],
        compiler_params=params(),
        name="columns",
    )(*[in_hbm(x) for x in (switched_rows.T, branch_buses, nodal_sensitivity)])
    pay = pl.pallas_call(
        zonal_kernel,
        out_shape=jax.ShapeDtypeStruct((n_z, SUMMED + share, LANES), f32),
        in_specs=[vmem, hbm, hbm, vmem, vmem, vmem],
        out_specs=vmem,
        scratch_shapes=[
            *bus_scratch, pltpu.VMEM((rows, zones), f32), pltpu.SemaphoreType.DMA((2,))
        ],
        compiler_params=params(),
        name="zonal",
    )(totals, weight, zone, *[in_vmem(x) for x in (sens, held, extra)])

    swap = [(0, 1), (1, 0)]
    parts = lax.all_to_all(pay, "z", 0, 0, tiled=True)
    local = jnp.sum(parts[:, :SUMMED], axis=0)
    part = jax.ShapeDtypeStruct((SUB + 2 * share, LANES), f32)
    mine, theirs = pl.pallas_call(
        place_kernel,
        out_shape=(part, part),
        in_specs=[vmem] * 3,
        out_specs=(vmem, vmem),
        compiler_params=params(),
        name="place",
    )(parts, local, meta)

    block = local[2 * SUB:]
    theirs = lax.ppermute(jnp.concatenate([block, theirs], axis=0), "yh", swap)
    beside = lax.ppermute(block, "yl", swap)
    across = lax.ppermute(block, ("yl", "yh"), [(0, 3), (3, 0), (1, 2), (2, 1)])
    here = jnp.concatenate([block + theirs[:BLOCK_ROWS], beside + across], axis=0)
    n_x = lax.axis_size("x")
    others = [
        lax.ppermute(here, "x", [(at, (at + by) % n_x) for at in range(n_x)])
        for by in range(1, n_x)
    ]
    other = lax.ppermute(
        mine[:SUB] + theirs[BLOCK_ROWS:BLOCK_ROWS + SUB], "act", swap
    )

    def compact():
        outputs = pl.pallas_call(
            final_kernel,
            out_shape=(
                jax.ShapeDtypeStruct((actions, share, zones), f32),
                jax.ShapeDtypeStruct((actions, share), f32),
                jax.ShapeDtypeStruct((actions, share), f32),
            ),
            in_specs=[vmem] * 10,
            out_specs=(vmem, vmem, vmem),
            compiler_params=params(),
            name="update",
        )(
            meta, mine, theirs, other, here, *others,
            net_position.reshape(1, zones), flow_limit.reshape(1, share),
        )
        return tuple(outputs)

    def general():
        inputs = nodal_sensitivity, shift_weight, bus_zone, branch_buses, switched_rows
        return tuple(copied(plain(*copied(inputs), net_position, flow_limit)))

    return lax.cond(meta[2, 0] > 0.5, general, compact)


def sum_over(x, axes):
    spread = jnp.broadcast_to(x[None], (lax.axis_size(axes), *x.shape))
    return jnp.sum(lax.all_to_all(spread, axes, 0, 0, tiled=True), axis=0)


def scattered_sum(x):
    shares = lax.axis_size(BUS)
    x = x.reshape(shares, x.shape[0] // shares, x.shape[1])
    return jnp.sum(lax.all_to_all(x, BUS, 0, 0, tiled=True), axis=0)


def plain(
    nodal_sensitivity, shift_weight, bus_zone, branch_buses, switched_rows, net_position, flow_limit
):
    rows, cols = nodal_sensitivity.shape
    zones = net_position.shape[0]
    actions, rank = switched_rows.shape
    onehot = (bus_zone[:, None] == jnp.arange(zones)[None, :]).astype(jnp.float32)
    total = sum_over(jnp.sum(onehot * shift_weight[:, None], axis=0), BUS)
    key = (onehot * shift_weight[:, None] / total[None, :]).astype(jnp.bfloat16)
    zonal = jnp.dot(nodal_sensitivity, key, preferred_element_type=jnp.float32)
    picks = switched_rows.reshape(-1)

    def columns(buses):
        local = buses - lax.axis_index(BUS) * cols
        owned = (local >= 0) & (local < cols)
        picked = jnp.take(nodal_sensitivity, jnp.clip(local, 0, cols - 1), axis=1)
        return jnp.where(owned[None, :], picked.astype(jnp.float32), 0.0)

    diff = columns(branch_buses[0][picks]) - columns(branch_buses[1][picks])
    zonal, diff = scattered_sum(zonal), scattered_sum(diff)
    share = rows // lax.axis_size(BUS)
    local = picks - lax.axis_index(CNEC) * rows - lax.axis_index(BUS) * share
    owned = ((local >= 0) & (local < share))[:, None]
    local = jnp.clip(local, 0, share - 1)
    switched = jnp.where(owned, jnp.take(zonal, local, axis=0), 0.0)
    coupled = jnp.where(owned, jnp.take(diff, local, axis=0), 0.0)
    coupled = jnp.einsum("aiaj->aij", coupled.reshape(actions, rank, actions, rank))
    both = jnp.concatenate([switched, coupled.reshape(actions * rank, rank)], axis=1)
    both = sum_over(sum_over(both, BUS), CNEC).reshape(actions, rank, zones + rank)
    left, right = jnp.eye(rank, dtype=jnp.float32)[None] - both[:, :, zones:], both[:, :, :zones]
    for pivot in range(rank):
        is_pivot = (jnp.arange(rank) == pivot)[None, :, None]
        factor = left[:, :, pivot:pivot + 1]
        diagonal = factor[:, pivot:pivot + 1]
        left_now, right_now = left[:, pivot:pivot + 1] / diagonal, right[:, pivot:pivot + 1] / diagonal
        left = jnp.where(is_pivot, left_now, left - factor * left_now)
        right = jnp.where(is_pivot, right_now, right - factor * right_now)
    after = zonal[None] + jnp.einsum(
        "caj,ajz->acz", diff.reshape(share, actions, rank), right, precision=HIGHEST
    )
    flow = jnp.einsum("acz,z->ac", after, net_position, precision=HIGHEST)
    return after, flow / flow_limit[None, :], flow_limit[None, :] - jnp.abs(flow)


def solution(mesh):
    n_cnec, n_bus, n_act = mesh.devices.shape
    split = Mesh(
        mesh.devices.reshape(2, n_cnec // 2, n_bus // 2, 2, n_act), ("yl", "x", "z", "yh", "act")
    )
    return jax.shard_map(
        body,
        mesh=split,
        in_specs=(
            P(CNEC, BUS),
            P(BUS),
            P(BUS),
            P(),
            P("act", None),
            P(),
            P(CNEC + BUS),
        ),
        out_specs=(
            P("act", CNEC + BUS, None),
            P("act", CNEC + BUS),
            P("act", CNEC + BUS),
        ),
        check_vma=False,
    )
```

```python
import jax
import jax.numpy as jnp
from jax import lax
from jax.experimental import pallas as pl
from jax.experimental.pallas import tpu as pltpu
from jax.sharding import Mesh
from jax.sharding import PartitionSpec as P

HIGHEST = lax.Precision.HIGHEST
LANES = 128
HALF = 64
SUB = 8
BLOCK = 2048
SLOTS = 64
BLOCK_ROWS = SLOTS // 2 + SUB
SUMMED = 2 * SUB + BLOCK_ROWS
CNEC, BUS = ("yl", "x"), ("z", "yh")


def iota(shape, dim):
    return lax.broadcasted_iota(jnp.int32, shape, dim)


def dot_nt(x, y, precision=None):
    return lax.dot_general(
        x, y, (((1,), (1,)), ((), ())), precision=precision, preferred_element_type=jnp.float32
    )


def dot(x, y, precision=None):
    return jnp.dot(x, y, precision=precision, preferred_element_type=jnp.float32)


def two_parts(values):
    high = values.astype(jnp.bfloat16)
    return high, (values - high.astype(jnp.float32)).astype(jnp.bfloat16)


def by_parts(product, x, y):
    x_high, x_low = two_parts(x)
    y_high, y_low = two_parts(y)
    return product(x_high, y_high) + product(x_high, y_low) + product(x_low, y_high)


def digits(values, base, count):
    return [((values >> (base * at)) & ((1 << base) - 1)).astype(jnp.float32).astype(jnp.bfloat16)
            for at in reversed(range(count))]


def find_picks(swt, branch_ref):
    rank, actions = swt.shape
    picks = rank * actions
    pick_id = iota((picks, actions), 0)
    of_action = pick_id % LANES // rank * 2 + pick_id // LANES == iota((picks, actions), 1)
    of_action = jnp.where(of_action, 1.0, 0.0).astype(jnp.bfloat16)
    high, low = digits(swt, 6, 2)
    row = dot_nt(high, of_action) * 64.0 + dot_nt(low, of_action)
    row = jnp.where(iota((rank, picks), 1) % rank == iota((rank, picks), 0), row, 0.0)
    row = jnp.sum(row, axis=0, keepdims=True).astype(jnp.int32)
    tiles = branch_ref.shape[1] // LANES
    table = jnp.concatenate(
        [branch_ref[:, at * LANES:(at + 1) * LANES] for at in range(tiles)], axis=0
    )
    onehot = jnp.where(iota((LANES, picks), 0) == row % LANES, 1.0, 0.0).astype(jnp.bfloat16)
    high, middle, low = [dot(part, onehot) for part in digits(table, 6, 3)]
    found = high * 4096.0 + middle * 64.0 + low
    line = iota((2 * tiles, picks), 0) - row // LANES * 2
    ends = [
        jnp.sum(jnp.where(line == end, found, 0.0), axis=0, keepdims=True).astype(jnp.int32)
        for end in (0, 1)
    ]
    return row, ends


def slot_matrix(slots, count):
    shape = (count, slots[0].shape[1])
    first, second = [jnp.where(iota(shape, 0) == slot, 1.0, 0.0) for slot in slots]
    return (first - second).astype(jnp.bfloat16)


def total_kernel(weight_hbm, zone_hbm, out_ref, weight_ref, zone_ref, sems):
    copies = [
        pltpu.make_async_copy(weight_hbm, weight_ref, sems.at[0]),
        pltpu.make_async_copy(zone_hbm, zone_ref, sems.at[1]),
    ]
    for copy in copies:
        copy.start()
    for copy in copies:
        copy.wait()
    ids = iota((HALF, LANES), 0)
    total = jnp.zeros((HALF, LANES), jnp.float32)
    for at in range(weight_ref.shape[0]):
        total += jnp.where(zone_ref[at:at + 1, :] == ids, weight_ref[at:at + 1, :], 0.0)
    total = jnp.sum(total, axis=1, keepdims=True)
    total = jnp.sum(jnp.where(ids == iota((HALF, LANES), 1), total, 0.0), axis=0, keepdims=True)
    out_ref[...] = jnp.broadcast_to(total[None], out_ref.shape)


def column_kernel(
    swt_hbm, branch_hbm, sens_hbm, held_ref, meta_ref, extra_ref,
    swt_ref, branch_ref, sens_ref, acc_ref, coupled_ref, sems
):
    rows, cols = sens_ref.shape
    rank, actions = swt_ref.shape
    picks = rank * actions
    steps = cols // BLOCK
    bf16 = jnp.bfloat16
    small = [
        pltpu.make_async_copy(swt_hbm, swt_ref, sems.at[steps]),
        pltpu.make_async_copy(branch_hbm, branch_ref, sems.at[steps + 1]),
    ]
    for copy in small:
        copy.start()

    def block_copy(step):
        at = pl.ds(pl.multiple_of(step * BLOCK, BLOCK), BLOCK)
        return pltpu.make_async_copy(sens_hbm.at[:, at], sens_ref.at[:, at], sems.at[step])

    for step in range(steps):
        block_copy(step).start()

    shard = lax.axis_index(BUS)
    row_start = lax.axis_index(CNEC) * rows
    acc_ref[...] = jnp.zeros_like(acc_ref)
    for copy in small:
        copy.wait()
    row, ends = find_picks(swt_ref[...], branch_ref)

    def ranks(owner, owners):
        count = owner.shape[1]
        inside = iota((owners, count), 0) == owner
        before = jnp.where(iota((count, count), 0) < iota((count, count), 1), 1.0, 0.0)
        place = dot(jnp.where(inside, 1.0, 0.0).astype(bf16), before.astype(bf16))
        return jnp.sum(jnp.where(inside, place, 0.0), axis=0, keepdims=True)

    bus = jnp.concatenate(ends, axis=1)
    count = 2 * picks
    held, place = bus // cols, ranks(bus // cols, lax.axis_size(BUS))
    owner, row_place = row // rows, ranks(row // rows, lax.axis_size(CNEC))
    most = jnp.maximum(
        jnp.max(place, axis=1, keepdims=True), jnp.max(row_place, axis=1, keepdims=True)
    )
    over = jnp.where(most >= SLOTS, 1.0, 0.0)
    meta_ref[0:1, :] = held.astype(jnp.float32)
    meta_ref[1:2, :] = place
    meta_ref[2:3, :] = jnp.broadcast_to(over, (1, count))
    meta_ref[3:4, :] = jnp.concatenate([owner.astype(jnp.float32), row_place], axis=1)
    meta_ref[4:, :] = jnp.zeros((SUB - 4, count), jnp.float32)
    place = place.astype(jnp.int32)
    mine = held == shard
    slot = jnp.where(mine, place, -1)
    local = bus - shard * cols

    def buses_of(group):
        match = iota((SLOTS, count), 0) + group * SLOTS == slot
        match = jnp.where(match, (local + 1).astype(jnp.float32), 0.0)
        return jnp.sum(match, axis=1, keepdims=True).astype(jnp.int32) - 1

    first_buses = buses_of(0)
    row_slot = jnp.where(owner == lax.axis_index(CNEC), row_place.astype(jnp.int32), -1)
    match = iota((SLOTS, picks), 0) == row_slot
    slot_row = jnp.where(match, (row - row_start + 1).astype(jnp.float32), 0.0)
    slot_row = jnp.sum(slot_row, axis=1, keepdims=True) - 1.0
    action_of = iota((SLOTS, picks), 1) // rank
    slot_action = jnp.where(match, action_of.astype(jnp.float32), 0.0)
    slot_action = jnp.sum(slot_action, axis=1, keepdims=True).astype(jnp.int32)
    extra_ref[0:SLOTS, :] = jnp.broadcast_to(slot_row, (SLOTS, LANES))
    choose = iota((SLOTS, rows), 1) == slot_row.astype(jnp.int32)
    choose = jnp.where(choose, 1.0, 0.0).astype(bf16)
    lane = iota((SLOTS, BLOCK), 1)

    def select(buses, step):
        return jnp.where(lane == buses - step * BLOCK, 1.0, 0.0).astype(bf16)

    def step_body(step, carry):
        at = pl.ds(pl.multiple_of(step * BLOCK, BLOCK), BLOCK)
        chosen = select(first_buses, step)
        block_copy(step).wait()
        acc_ref[...] += dot_nt(sens_ref[:, at], chosen)
        return carry

    lax.fori_loop(0, steps, step_body, 0)

    def coupled_of(columns, group):
        slots = [slot[:, at * picks:(at + 1) * picks] - group * SLOTS for at in (0, 1)]
        chosen = dot(choose, columns.astype(bf16))
        return dot(chosen.astype(bf16), slot_matrix(slots, SLOTS))

    columns = acc_ref[...]
    coupled_ref[...] = coupled_of(columns, 0)

    def group_body(group, carry):
        buses = buses_of(group)
        columns = jnp.zeros((rows, SLOTS), jnp.float32)
        for step in range(steps):
            at = pl.ds(step * BLOCK, BLOCK)
            columns += dot_nt(sens_ref[:, at], select(buses, step))
        coupled_ref[...] += coupled_of(columns, group)
        return carry

    groups = (jnp.sum(jnp.where(mine, 1.0, 0.0)).astype(jnp.int32) + SLOTS - 1) // SLOTS
    lax.fori_loop(1, groups, group_body, 0)

    coupled = jnp.where(action_of == slot_action, coupled_ref[...], 0.0)
    fold = jnp.where(iota((picks, LANES), 0) % rank == iota((picks, LANES), 1) % rank, 1.0, 0.0)
    high, low = [dot(part, fold.astype(bf16)) for part in two_parts(coupled)]
    shape = (SLOTS, LANES)
    coupled = jnp.where(iota(shape, 1) // rank == iota(shape, 0) // SUB, high + low, 0.0)
    extra_ref[SLOTS:, :] = jnp.sum(coupled.reshape(SLOTS // SUB, SUB, LANES), axis=0)
    chunks = held_ref.shape[0]
    columns = columns.reshape(chunks, 2, rows // chunks // 2, SLOTS)
    held_ref[...] = jnp.concatenate([columns[:, 0], columns[:, 1]], axis=-1)


def zonal_kernel(totals_ref, weight_hbm, zone_hbm, sens_hbm, held_ref, extra_ref, pay_ref,
                 weight_ref, zone_ref, sens_ref, key_ref, sums_ref, acc_ref, sems):
    rows, cols = sens_ref.shape
    zones = HALF
    part = BLOCK // 2
    steps = cols // part
    bf16 = jnp.bfloat16
    copies = [
        pltpu.make_async_copy(weight_hbm, weight_ref, sems.at[steps]),
        pltpu.make_async_copy(zone_hbm, zone_ref, sems.at[steps + 1]),
    ]
    for copy in copies:
        copy.start()

    def block_copy(step):
        at = pl.ds(pl.multiple_of(step * part, part), part)
        return pltpu.make_async_copy(sens_hbm.at[:, at], sens_ref.at[:, at], sems.at[step])

    for step in range(steps):
        block_copy(step).start()

    acc_ref[...] = jnp.zeros_like(acc_ref)
    pay_ref[:, SUMMED:, :] = held_ref[...]
    total = jnp.sum(totals_ref[...], axis=0)[0:1]
    for copy in copies:
        copy.wait()
    of_bus = jnp.take_along_axis(
        jnp.broadcast_to(total, weight_ref.shape), zone_ref[...], axis=1
    )
    sums_ref[...] = weight_ref[...] / of_bus
    ids = iota((zones, LANES), 0)
    for at in range(cols // LANES):
        key = jnp.where(zone_ref[at:at + 1, :] == ids, sums_ref[at:at + 1, :], 0.0)
        key_ref[:, at * LANES:(at + 1) * LANES] = key.astype(bf16)

    def step_body(step, carry):
        at = pl.ds(pl.multiple_of(step * part, part), part)
        block_copy(step).wait()
        acc_ref[...] += dot_nt(sens_ref[:, at], key_ref[:, at])
        return carry

    lax.fori_loop(0, steps, step_body, 0)

    chunks = pay_ref.shape[0]
    zonal = acc_ref[...]
    choose = iota((SLOTS, rows), 1) == extra_ref[0:SLOTS, 0:1].astype(jnp.int32)
    choose = jnp.where(choose, 1.0, 0.0).astype(bf16)
    switched = dot(choose, jnp.concatenate(two_parts(zonal), axis=1))
    switched = switched[:, 0:zones] + switched[:, zones:]
    share = zonal.reshape(chunks, 2, 2, 2, SUB, zones)
    share = jnp.where(lax.axis_index("act") == 0, share[:, :, 0], share[:, :, 1])
    share = jnp.concatenate([share[:, :, 0], share[:, :, 1]], axis=-1)
    half = SLOTS // 2
    switched = jnp.concatenate([switched[:half], switched[half:]], axis=1)
    block = jnp.concatenate([switched, extra_ref[SLOTS:, :]], axis=0)
    pay_ref[:, 0:2 * SUB, :] = share.reshape(chunks, 2 * SUB, LANES)
    pay_ref[:, 2 * SUB:SUMMED, :] = jnp.broadcast_to(block[None], (chunks, *block.shape))


def place_kernel(parts_ref, local_ref, meta_ref, mine_ref, theirs_ref):
    chunks = parts_ref.shape[0]
    picks = meta_ref.shape[1] // 2
    half = parts_ref.shape[1] - SUMMED
    y_here, y_size = lax.axis_index("yh"), lax.axis_size("yh")
    held = meta_ref[0:1, :].astype(jnp.int32)
    place = meta_ref[1:2, :].astype(jnp.int32)
    known = (held % y_size == y_here) & (place < SLOTS)
    slot = jnp.where(known, held // y_size * SLOTS + place, -1)
    spread = slot_matrix([slot[:, at * picks:(at + 1) * picks] for at in (0, 1)], chunks * SLOTS)
    columns = [
        jnp.concatenate(
            [parts_ref[z, SUMMED:, at * SLOTS:(at + 1) * SLOTS] for z in range(chunks)], axis=1
        )
        for at in (0, 1)
    ]
    columns = jnp.concatenate(columns, axis=0).astype(jnp.bfloat16)
    diff = lax.dot_general(
        spread, columns, (((0,), (1,)), ((), ())), preferred_element_type=jnp.float32
    )
    diff = diff.reshape(2, picks // (2 * SUB), SUB, 2 * half)
    diff = jnp.concatenate([diff[0], diff[1]], axis=1).reshape(4, picks // 4, 2 * half)
    lower = y_here == 0
    packed = [
        jnp.concatenate([diff[g, :, at * half:(at + 1) * half] for g in range(4)], axis=1)
        for at in (0, 1)
    ]
    for ref, first in ((mine_ref, lower), (theirs_ref, ~lower)):
        ref[0:SUB, :] = jnp.where(first, local_ref[0:SUB, :], local_ref[SUB:2 * SUB, :])
        ref[SUB:, :] = jnp.where(first, packed[0], packed[1])


def copy_kernel(*refs):
    count = len(refs) // 2
    copies = [
        pltpu.make_async_copy(refs[at], refs[count + at], refs[-1].at[at]) for at in range(count)
    ]
    for copy in copies:
        copy.start()
    for copy in copies:
        copy.wait()


def final_kernel(
    meta_ref, mine_ref, theirs_ref, other_ref, here_ref, x1_ref, x2_ref, x3_ref, position_ref,
    limit_ref, after_ref, loading_ref, margin_ref
):
    actions, share, zones = after_ref.shape
    pairs = actions // 2
    picks = actions * SUB
    bf16 = jnp.bfloat16

    size_x = lax.axis_size("x")
    owner = meta_ref[3:4, :picks].astype(jnp.int32)
    slot = meta_ref[3:4, picks:].astype(jnp.int32)
    back = (lax.axis_index("x") - owner % size_x + size_x) % size_x
    flip = jnp.where(owner // size_x == lax.axis_index("yl"), 0, 1)
    blocks = [
        ref[at * BLOCK_ROWS:(at + 1) * BLOCK_ROWS, :]
        for ref in (here_ref, x1_ref, x2_ref, x3_ref)
        for at in (0, 1)
    ]
    count = len(blocks) * SLOTS
    spread = iota((count, picks), 0) == (back * 2 + flip) * SLOTS + slot
    spread = jnp.where(spread, 1.0, 0.0).astype(bf16)
    half = SLOTS // 2
    switched, coupled = [], []
    lane = iota((half, LANES), 1)
    for block in blocks:
        rows = block[0:half]
        turned = pltpu.roll(rows, HALF, 1)
        switched += [jnp.where(lane < HALF, rows, turned), jnp.where(lane < HALF, turned, rows)]
        extra = block[half:]
        for g in range(SLOTS // SUB):
            coupled.append(jnp.where(iota(extra.shape, 1) // SUB == g, extra, 0.0))
    parts = two_parts(jnp.concatenate(switched, axis=0)) + two_parts(jnp.concatenate(coupled, axis=0))
    found = lax.dot_general(
        spread, jnp.concatenate(parts, axis=1), (((0,), (0,)), ((), ())),
        preferred_element_type=jnp.float32,
    )
    switched = found[:, 0:LANES] + found[:, LANES:2 * LANES]
    coupled = found[:, 2 * LANES:3 * LANES] + found[:, 3 * LANES:]
    shape = (LANES, LANES)
    repeat = (iota(shape, 0) < SLOTS) & (iota(shape, 0) % SUB == iota(shape, 1) % SUB)
    repeat = jnp.where(repeat, 1.0, 0.0).astype(bf16)
    high, low = [dot(part, repeat) for part in two_parts(coupled)]
    coupled = high + low

    shape = (pairs, SUB, LANES)
    row_id, lane = iota(shape, 1), iota(shape, 2)

    def side_by_side(x):
        return jnp.where(
            lane < HALF, x[:picks // 2].reshape(shape), x[picks // 2:].reshape(shape)
        )

    left = jnp.where(lane % SUB == row_id, 1.0, 0.0) - side_by_side(coupled)
    right = side_by_side(switched)
    for pivot in range(SUB):
        factor = jnp.where(
            lane < HALF, left[:, :, pivot:pivot + 1], left[:, :, HALF + pivot:HALF + pivot + 1]
        )
        diagonal = factor[:, pivot:pivot + 1]
        left_now = left[:, pivot:pivot + 1] / diagonal
        right_now = right[:, pivot:pivot + 1] / diagonal
        left = jnp.where(row_id == pivot, left_now, left - factor * left_now)
        right = jnp.where(row_id == pivot, right_now, right - factor * right_now)

    lower = lax.axis_index("act") == 0
    whole = mine_ref[...] + theirs_ref[BLOCK_ROWS:]
    mine, other = whole[0:SUB], other_ref[...]
    low, high = jnp.where(lower, mine, other), jnp.where(lower, other, mine)
    zonal = jnp.concatenate(
        [low[:, :HALF], low[:, HALF:], high[:, :HALF], high[:, HALF:]], axis=0
    )
    zonal_twice = jnp.concatenate([zonal, zonal], axis=1)
    groups = [whole[SUB:, g * share:(g + 1) * share] for g in range(LANES // share)]
    diff = jnp.concatenate(groups, axis=0)
    solved = jnp.concatenate(
        [jnp.where(lane < HALF, right, 0.0), jnp.where(lane < HALF, 0.0, right)], axis=1
    )
    diff_high, diff_low = two_parts(diff)
    solved_high, solved_low = two_parts(solved)

    def product(x, y):
        return lax.dot_general(
            x, y, (((0,), (0,)), ((), ())), preferred_element_type=jnp.float32
        )

    size = 2 * SUB
    for pair in range(pairs):
        at = slice(pair * size, (pair + 1) * size)
        left = jnp.concatenate([diff_high[at], diff_high[at], diff_low[at]], axis=0)
        right = jnp.concatenate(
            [solved_high[pair], solved_low[pair], solved_high[pair]], axis=0
        )
        total = zonal_twice + product(left, right)
        after_ref[2 * pair] = total[:, :HALF]
        after_ref[2 * pair + 1] = total[:, HALF:]
    position = position_ref[...]
    twice = jnp.concatenate([position, position], axis=1)
    moved = by_parts(dot_nt, twice, solved.reshape(pairs * size, LANES))
    shape = (actions, pairs * size)
    same = iota(shape, 1) // SUB == iota(shape, 0)
    flow = by_parts(dot_nt, position, zonal) + by_parts(dot, jnp.where(same, moved, 0.0), diff)
    limit = limit_ref[...]
    loading_ref[...] = flow / limit
    margin_ref[...] = limit - jnp.abs(flow)


def in_hbm(x):
    return pltpu.with_memory_space_constraint(x, pltpu.HBM)


def copied(arrays):
    hbm = pl.BlockSpec(memory_space=pltpu.HBM)
    return pl.pallas_call(
        copy_kernel,
        out_shape=[jax.ShapeDtypeStruct(x.shape, x.dtype) for x in arrays],
        in_specs=[hbm] * len(arrays),
        out_specs=[hbm] * len(arrays),
        scratch_shapes=[pltpu.SemaphoreType.DMA((len(arrays),))],
        name="copies",
    )(*[in_hbm(x) for x in arrays])


def params():
    return pltpu.CompilerParams(vmem_limit_bytes=48 * 1024 * 1024)


def body(
    nodal_sensitivity, shift_weight, bus_zone, branch_buses, switched_rows, net_position, flow_limit
):
    rows, cols = nodal_sensitivity.shape
    zones = net_position.shape[0]
    actions, rank = switched_rows.shape
    picks = actions * rank
    n_z, n_yh = lax.axis_size("z"), lax.axis_size("yh")
    share = rows // n_z // n_yh
    f32, i32 = jnp.float32, jnp.int32
    vmem = pl.BlockSpec(memory_space=pltpu.VMEM)
    hbm = pl.BlockSpec(memory_space=pltpu.HBM)

    weight, zone = [x.reshape(cols // LANES, LANES) for x in (shift_weight, bus_zone)]
    weight, zone = in_hbm(weight), in_hbm(zone)
    bus_scratch = [pltpu.VMEM((cols // LANES, LANES), kind) for kind in (f32, i32)]
    totals = pl.pallas_call(
        total_kernel,
        out_shape=jax.ShapeDtypeStruct((lax.axis_size(BUS), SUB, LANES), f32),
        in_specs=[hbm] * 2,
        out_specs=vmem,
        scratch_shapes=[*bus_scratch, pltpu.SemaphoreType.DMA((2,))],
        compiler_params=params(),
        name="totals",
    )(weight, zone)
    totals = lax.all_to_all(totals, BUS, 0, 0, tiled=True)
    sens_scratch = pltpu.VMEM((rows, cols), jnp.bfloat16)
    held, meta, extra = pl.pallas_call(
        column_kernel,
        out_shape=(
            jax.ShapeDtypeStruct((n_z, share, LANES), f32),
            jax.ShapeDtypeStruct((SUB, 2 * picks), f32),
            jax.ShapeDtypeStruct((SLOTS + SUB, LANES), f32),
        ),
        in_specs=[hbm] * 3,
        out_specs=(vmem,) * 3,
        scratch_shapes=[
            pltpu.VMEM((rank, actions), i32),
            pltpu.VMEM(branch_buses.shape, i32),
            sens_scratch,
            pltpu.VMEM((rows, SLOTS), f32),
            pltpu.VMEM((SLOTS, picks), f32),
            pltpu.SemaphoreType.DMA((cols // BLOCK + 2,)),
        ],
        compiler_params=params(),
        name="columns",
    )(*[in_hbm(x) for x in (switched_rows.T, branch_buses, nodal_sensitivity)])
    pay = pl.pallas_call(
        zonal_kernel,
        out_shape=jax.ShapeDtypeStruct((n_z, SUMMED + share, LANES), f32),
        in_specs=[vmem, hbm, hbm, hbm, vmem, vmem],
        out_specs=vmem,
        scratch_shapes=[
            *bus_scratch,
            sens_scratch,
            pltpu.VMEM((zones, cols), jnp.bfloat16),
            pltpu.VMEM((cols // LANES, LANES), f32),
            pltpu.VMEM((rows, zones), f32),
            pltpu.SemaphoreType.DMA((2 * cols // BLOCK + 2,)),
        ],
        compiler_params=params(),
        name="zonal",
    )(totals, weight, zone, in_hbm(nodal_sensitivity), held, extra)

    swap = [(0, 1), (1, 0)]
    parts = lax.all_to_all(pay, "z", 0, 0, tiled=True)
    local = jnp.sum(parts[:, :SUMMED], axis=0)
    part = jax.ShapeDtypeStruct((SUB + 2 * share, LANES), f32)
    mine, theirs = pl.pallas_call(
        place_kernel,
        out_shape=(part, part),
        in_specs=[vmem] * 3,
        out_specs=(vmem, vmem),
        compiler_params=params(),
        name="place",
    )(parts, local, meta)

    block = local[2 * SUB:]
    theirs = lax.ppermute(jnp.concatenate([block, theirs], axis=0), "yh", swap)
    beside = lax.ppermute(block, "yl", swap)
    across = lax.ppermute(block, ("yl", "yh"), [(0, 3), (3, 0), (1, 2), (2, 1)])
    here = jnp.concatenate([block + theirs[:BLOCK_ROWS], beside + across], axis=0)
    n_x = lax.axis_size("x")
    others = [
        lax.ppermute(here, "x", [(at, (at + by) % n_x) for at in range(n_x)])
        for by in range(1, n_x)
    ]
    other = lax.ppermute(
        mine[:SUB] + theirs[BLOCK_ROWS:BLOCK_ROWS + SUB], "act", swap
    )

    def compact():
        outputs = pl.pallas_call(
            final_kernel,
            out_shape=(
                jax.ShapeDtypeStruct((actions, share, zones), f32),
                jax.ShapeDtypeStruct((actions, share), f32),
                jax.ShapeDtypeStruct((actions, share), f32),
            ),
            in_specs=[vmem] * 10,
            out_specs=(vmem, vmem, vmem),
            compiler_params=params(),
            name="update",
        )(
            meta, mine, theirs, other, here, *others,
            net_position.reshape(1, zones), flow_limit.reshape(1, share),
        )
        return tuple(outputs)

    def general():
        inputs = nodal_sensitivity, shift_weight, bus_zone, branch_buses, switched_rows
        return tuple(copied(plain(*copied(inputs), net_position, flow_limit)))

    return lax.cond(meta[2, 0] > 0.5, general, compact)


def sum_over(x, axes):
    spread = jnp.broadcast_to(x[None], (lax.axis_size(axes), *x.shape))
    return jnp.sum(lax.all_to_all(spread, axes, 0, 0, tiled=True), axis=0)


def scattered_sum(x):
    shares = lax.axis_size(BUS)
    x = x.reshape(shares, x.shape[0] // shares, x.shape[1])
    return jnp.sum(lax.all_to_all(x, BUS, 0, 0, tiled=True), axis=0)


def plain(
    nodal_sensitivity, shift_weight, bus_zone, branch_buses, switched_rows, net_position, flow_limit
):
    rows, cols = nodal_sensitivity.shape
    zones = net_position.shape[0]
    actions, rank = switched_rows.shape
    onehot = (bus_zone[:, None] == jnp.arange(zones)[None, :]).astype(jnp.float32)
    total = sum_over(jnp.sum(onehot * shift_weight[:, None], axis=0), BUS)
    key = (onehot * shift_weight[:, None] / total[None, :]).astype(jnp.bfloat16)
    zonal = jnp.dot(nodal_sensitivity, key, preferred_element_type=jnp.float32)
    picks = switched_rows.reshape(-1)

    def columns(buses):
        local = buses - lax.axis_index(BUS) * cols
        owned = (local >= 0) & (local < cols)
        picked = jnp.take(nodal_sensitivity, jnp.clip(local, 0, cols - 1), axis=1)
        return jnp.where(owned[None, :], picked.astype(jnp.float32), 0.0)

    diff = columns(branch_buses[0][picks]) - columns(branch_buses[1][picks])
    zonal, diff = scattered_sum(zonal), scattered_sum(diff)
    share = rows // lax.axis_size(BUS)
    local = picks - lax.axis_index(CNEC) * rows - lax.axis_index(BUS) * share
    owned = ((local >= 0) & (local < share))[:, None]
    local = jnp.clip(local, 0, share - 1)
    switched = jnp.where(owned, jnp.take(zonal, local, axis=0), 0.0)
    coupled = jnp.where(owned, jnp.take(diff, local, axis=0), 0.0)
    coupled = jnp.einsum("aiaj->aij", coupled.reshape(actions, rank, actions, rank))
    both = jnp.concatenate([switched, coupled.reshape(actions * rank, rank)], axis=1)
    both = sum_over(sum_over(both, BUS), CNEC).reshape(actions, rank, zones + rank)
    left, right = jnp.eye(rank, dtype=jnp.float32)[None] - both[:, :, zones:], both[:, :, :zones]
    for pivot in range(rank):
        is_pivot = (jnp.arange(rank) == pivot)[None, :, None]
        factor = left[:, :, pivot:pivot + 1]
        diagonal = factor[:, pivot:pivot + 1]
        left_now, right_now = left[:, pivot:pivot + 1] / diagonal, right[:, pivot:pivot + 1] / diagonal
        left = jnp.where(is_pivot, left_now, left - factor * left_now)
        right = jnp.where(is_pivot, right_now, right - factor * right_now)
    after = zonal[None] + jnp.einsum(
        "caj,ajz->acz", diff.reshape(share, actions, rank), right, precision=HIGHEST
    )
    flow = jnp.einsum("acz,z->ac", after, net_position, precision=HIGHEST)
    return after, flow / flow_limit[None, :], flow_limit[None, :] - jnp.abs(flow)


def solution(mesh):
    n_cnec, n_bus, n_act = mesh.devices.shape
    split = Mesh(
        mesh.devices.reshape(2, n_cnec // 2, n_bus // 2, 2, n_act), ("yl", "x", "z", "yh", "act")
    )
    return jax.shard_map(
        body,
        mesh=split,
        in_specs=(
            P(CNEC, BUS),
            P(BUS),
            P(BUS),
            P(),
            P("act", None),
            P(),
            P(CNEC + BUS),
        ),
        out_specs=(
            P("act", CNEC + BUS, None),
            P("act", CNEC + BUS),
            P("act", CNEC + BUS),
        ),
        check_vma=False,
    )
```

```python
import jax
import jax.numpy as jnp
from jax import lax
from jax.experimental import pallas as pl
from jax.experimental.pallas import tpu as pltpu
from jax.sharding import Mesh
from jax.sharding import PartitionSpec as P

HIGHEST = lax.Precision.HIGHEST
LANES = 128
HALF = 64
SUB = 8
BLOCK = 2048
SLOTS = 64
BLOCK_ROWS = SLOTS // 2 + SUB
CNEC, BUS = ("yl", "x"), ("z", "yh")


def iota(shape, dim):
    return lax.broadcasted_iota(jnp.int32, shape, dim)


def dot_nt(x, y, precision=None):
    return lax.dot_general(
        x, y, (((1,), (1,)), ((), ())), precision=precision, preferred_element_type=jnp.float32
    )


def dot(x, y, precision=None):
    return jnp.dot(x, y, precision=precision, preferred_element_type=jnp.float32)


def two_parts(values):
    high = values.astype(jnp.bfloat16)
    return high, (values - high.astype(jnp.float32)).astype(jnp.bfloat16)


def by_parts(product, x, y):
    x_high, x_low = two_parts(x)
    y_high, y_low = two_parts(y)
    return product(x_high, y_high) + product(x_high, y_low) + product(x_low, y_high)


def digits(values, base, count):
    return [((values >> (base * at)) & ((1 << base) - 1)).astype(jnp.float32).astype(jnp.bfloat16)
            for at in reversed(range(count))]


def find_picks(swt, branch_ref):
    rank, actions = swt.shape
    picks = rank * actions
    pick_id = iota((picks, actions), 0)
    of_action = pick_id % LANES // rank * 2 + pick_id // LANES == iota((picks, actions), 1)
    of_action = jnp.where(of_action, 1.0, 0.0).astype(jnp.bfloat16)
    high, low = digits(swt, 6, 2)
    row = dot_nt(high, of_action) * 64.0 + dot_nt(low, of_action)
    row = jnp.where(iota((rank, picks), 1) % rank == iota((rank, picks), 0), row, 0.0)
    row = jnp.sum(row, axis=0, keepdims=True).astype(jnp.int32)
    tiles = branch_ref.shape[1] // LANES
    table = jnp.concatenate(
        [branch_ref[:, at * LANES:(at + 1) * LANES] for at in range(tiles)], axis=0
    )
    onehot = jnp.where(iota((LANES, picks), 0) == row % LANES, 1.0, 0.0).astype(jnp.bfloat16)
    high, middle, low = [dot(part, onehot) for part in digits(table, 6, 3)]
    found = high * 4096.0 + middle * 64.0 + low
    line = iota((2 * tiles, picks), 0) - row // LANES * 2
    ends = [
        jnp.sum(jnp.where(line == end, found, 0.0), axis=0, keepdims=True).astype(jnp.int32)
        for end in (0, 1)
    ]
    return row, ends


def slot_matrix(slots, count):
    shape = (count, slots[0].shape[1])
    first, second = [jnp.where(iota(shape, 0) == slot, 1.0, 0.0) for slot in slots]
    return (first - second).astype(jnp.bfloat16)


def total_kernel(weight_hbm, zone_hbm, out_ref, weight_ref, zone_ref, sems):
    copies = [
        pltpu.make_async_copy(weight_hbm, weight_ref, sems.at[0]),
        pltpu.make_async_copy(zone_hbm, zone_ref, sems.at[1]),
    ]
    for copy in copies:
        copy.start()
    for copy in copies:
        copy.wait()
    ids = iota((HALF, LANES), 0)
    total = jnp.zeros((HALF, LANES), jnp.float32)
    for at in range(weight_ref.shape[0]):
        total += jnp.where(zone_ref[at:at + 1, :] == ids, weight_ref[at:at + 1, :], 0.0)
    total = jnp.sum(total, axis=1, keepdims=True)
    eye = ids + HALF == iota((HALF, LANES), 1)
    total = jnp.sum(jnp.where(eye, total, 0.0), axis=0, keepdims=True)
    out_ref[...] = jnp.broadcast_to(total, out_ref.shape)


def column_kernel(
    swt_hbm, branch_hbm, sens_hbm, held_ref, meta_ref, extra_ref, sens_ref,
    swt_ref, branch_ref, acc_ref, coupled_ref, sems
):
    rows, cols = sens_ref.shape
    rank, actions = swt_ref.shape
    picks = rank * actions
    steps = cols // BLOCK
    bf16 = jnp.bfloat16
    small = [
        pltpu.make_async_copy(swt_hbm, swt_ref, sems.at[steps]),
        pltpu.make_async_copy(branch_hbm, branch_ref, sems.at[steps + 1]),
    ]
    for copy in small:
        copy.start()

    def block_copy(step):
        at = pl.ds(pl.multiple_of(step * BLOCK, BLOCK), BLOCK)
        return pltpu.make_async_copy(sens_hbm.at[:, at], sens_ref.at[:, at], sems.at[step])

    for step in range(steps):
        block_copy(step).start()

    shard = lax.axis_index(BUS)
    row_start = lax.axis_index(CNEC) * rows
    acc_ref[...] = jnp.zeros_like(acc_ref)
    for copy in small:
        copy.wait()
    row, ends = find_picks(swt_ref[...], branch_ref)

    def ranks(owner, owners):
        count = owner.shape[1]
        inside = iota((owners, count), 0) == owner
        before = jnp.where(iota((count, count), 0) < iota((count, count), 1), 1.0, 0.0)
        place = dot(jnp.where(inside, 1.0, 0.0).astype(bf16), before.astype(bf16))
        return jnp.sum(jnp.where(inside, place, 0.0), axis=0, keepdims=True)

    bus = jnp.concatenate(ends, axis=1)
    count = 2 * picks
    held, place = bus // cols, ranks(bus // cols, lax.axis_size(BUS))
    owner, row_place = row // rows, ranks(row // rows, lax.axis_size(CNEC))
    most = jnp.maximum(
        jnp.max(place, axis=1, keepdims=True), jnp.max(row_place, axis=1, keepdims=True)
    )
    over = jnp.where(most >= SLOTS, 1.0, 0.0)
    meta_ref[0:1, :] = held.astype(jnp.float32)
    meta_ref[1:2, :] = place
    meta_ref[2:3, :] = jnp.broadcast_to(over, (1, count))
    meta_ref[3:4, :] = jnp.concatenate([owner.astype(jnp.float32), row_place], axis=1)
    meta_ref[4:, :] = jnp.zeros((SUB - 4, count), jnp.float32)
    place = place.astype(jnp.int32)
    mine = held == shard
    slot = jnp.where(mine, place, -1)
    local = bus - shard * cols

    def buses_of(group):
        match = iota((SLOTS, count), 0) + group * SLOTS == slot
        match = jnp.where(match, (local + 1).astype(jnp.float32), 0.0)
        return jnp.sum(match, axis=1, keepdims=True).astype(jnp.int32) - 1

    first_buses = buses_of(0)
    row_slot = jnp.where(owner == lax.axis_index(CNEC), row_place.astype(jnp.int32), -1)
    match = iota((SLOTS, picks), 0) == row_slot
    slot_row = jnp.where(match, (row - row_start + 1).astype(jnp.float32), 0.0)
    slot_row = jnp.sum(slot_row, axis=1, keepdims=True) - 1.0
    action_of = iota((SLOTS, picks), 1) // rank
    slot_action = jnp.where(match, action_of.astype(jnp.float32), 0.0)
    slot_action = jnp.sum(slot_action, axis=1, keepdims=True).astype(jnp.int32)
    extra_ref[0:SLOTS, :] = jnp.broadcast_to(slot_row, (SLOTS, LANES))
    choose = iota((SLOTS, rows), 1) == slot_row.astype(jnp.int32)
    choose = jnp.where(choose, 1.0, 0.0).astype(bf16)
    lane = iota((SLOTS, BLOCK), 1)

    def select(buses, step):
        return jnp.where(lane == buses - step * BLOCK, 1.0, 0.0).astype(bf16)

    def step_body(step, carry):
        at = pl.ds(pl.multiple_of(step * BLOCK, BLOCK), BLOCK)
        chosen = select(first_buses, step)
        block_copy(step).wait()
        acc_ref[...] += dot_nt(sens_ref[:, at], chosen)
        return carry

    lax.fori_loop(0, steps, step_body, 0)

    def coupled_of(columns, group):
        slots = [slot[:, at * picks:(at + 1) * picks] - group * SLOTS for at in (0, 1)]
        chosen = dot(choose, columns.astype(bf16))
        return dot(chosen.astype(bf16), slot_matrix(slots, SLOTS))

    columns = acc_ref[...]
    coupled_ref[...] = coupled_of(columns, 0)

    def group_body(group, carry):
        buses = buses_of(group)
        columns = jnp.zeros((rows, SLOTS), jnp.float32)
        for step in range(steps):
            at = pl.ds(step * BLOCK, BLOCK)
            columns += dot_nt(sens_ref[:, at], select(buses, step))
        coupled_ref[...] += coupled_of(columns, group)
        return carry

    groups = (jnp.sum(jnp.where(mine, 1.0, 0.0)).astype(jnp.int32) + SLOTS - 1) // SLOTS
    lax.fori_loop(1, groups, group_body, 0)

    coupled = jnp.where(action_of == slot_action, coupled_ref[...], 0.0)
    fold = jnp.where(iota((picks, LANES), 0) % rank == iota((picks, LANES), 1) % rank, 1.0, 0.0)
    high, low = [dot(part, fold.astype(bf16)) for part in two_parts(coupled)]
    shape = (SLOTS, LANES)
    coupled = jnp.where(iota(shape, 1) // rank == iota(shape, 0) // SUB, high + low, 0.0)
    extra_ref[SLOTS:, :] = jnp.sum(coupled.reshape(SLOTS // SUB, SUB, LANES), axis=0)
    chunks = held_ref.shape[0]
    columns = columns.reshape(chunks, 2, rows // chunks // 2, SLOTS)
    held_ref[...] = jnp.concatenate([columns[:, 0], columns[:, 1]], axis=-1)


def zonal_kernel(parts_ref, weight_hbm, zone_hbm, sens_ref, extra_ref, pay_ref, coupled_ref,
                 weight_ref, zone_ref, key_ref, sums_ref, acc_ref, sems):
    rows, cols = sens_ref.shape
    zones = HALF
    bf16 = jnp.bfloat16
    copies = [
        pltpu.make_async_copy(weight_hbm, weight_ref, sems.at[0]),
        pltpu.make_async_copy(zone_hbm, zone_ref, sems.at[1]),
    ]
    for copy in copies:
        copy.start()
    acc_ref[...] = jnp.zeros_like(acc_ref)
    coupled = jnp.sum(parts_ref[:, SLOTS // 2:, :], axis=0)
    coupled_ref[...] = coupled
    for copy in copies:
        copy.wait()
    of_bus = jnp.take_along_axis(
        jnp.broadcast_to(coupled[0:1], weight_ref.shape), zone_ref[...] + HALF, axis=1
    )
    sums_ref[...] = weight_ref[...] / of_bus
    ids = iota((zones, LANES), 0)
    for at in range(cols // LANES):
        key = jnp.where(zone_ref[at:at + 1, :] == ids, sums_ref[at:at + 1, :], 0.0)
        key_ref[:, at * LANES:(at + 1) * LANES] = key.astype(bf16)

    def step_body(step, carry):
        at = pl.ds(pl.multiple_of(step * BLOCK, BLOCK), BLOCK)
        acc_ref[...] += dot_nt(sens_ref[:, at], key_ref[:, at])
        return carry

    lax.fori_loop(0, cols // BLOCK, step_body, 0)

    chunks = pay_ref.shape[0]
    zonal = acc_ref[...]
    choose = iota((SLOTS, rows), 1) == extra_ref[0:SLOTS, 0:1].astype(jnp.int32)
    choose = jnp.where(choose, 1.0, 0.0).astype(bf16)
    switched = dot(choose, jnp.concatenate(two_parts(zonal), axis=1))
    switched = switched[:, 0:zones] + switched[:, zones:]
    share = zonal.reshape(chunks, 2, 2, 2, SUB, zones)
    share = jnp.where(lax.axis_index("act") == 0, share[:, :, 0], share[:, :, 1])
    share = jnp.concatenate([share[:, :, 0], share[:, :, 1]], axis=-1)
    half = SLOTS // 2
    switched = jnp.concatenate([switched[:half], switched[half:]], axis=1)
    pay_ref[:, 0:2 * SUB, :] = share.reshape(chunks, 2 * SUB, LANES)
    pay_ref[:, 2 * SUB:, :] = jnp.broadcast_to(switched[None], (chunks, half, LANES))


def place_kernel(parts_ref, local_ref, meta_ref, mine_ref, theirs_ref):
    chunks = parts_ref.shape[0]
    picks = meta_ref.shape[1] // 2
    half = parts_ref.shape[1] - SUB
    y_here, y_size = lax.axis_index("yh"), lax.axis_size("yh")
    held = meta_ref[0:1, :].astype(jnp.int32)
    place = meta_ref[1:2, :].astype(jnp.int32)
    known = (held % y_size == y_here) & (place < SLOTS)
    slot = jnp.where(known, held // y_size * SLOTS + place, -1)
    spread = slot_matrix([slot[:, at * picks:(at + 1) * picks] for at in (0, 1)], chunks * SLOTS)
    columns = [
        jnp.concatenate(
            [parts_ref[z, 0:half, at * SLOTS:(at + 1) * SLOTS] for z in range(chunks)], axis=1
        )
        for at in (0, 1)
    ]
    columns = jnp.concatenate(columns, axis=0).astype(jnp.bfloat16)
    diff = lax.dot_general(
        spread, columns, (((0,), (1,)), ((), ())), preferred_element_type=jnp.float32
    )
    diff = diff.reshape(2, picks // (2 * SUB), SUB, 2 * half)
    diff = jnp.concatenate([diff[0], diff[1]], axis=1).reshape(4, picks // 4, 2 * half)
    lower = y_here == 0
    packed = [
        jnp.concatenate([diff[g, :, at * half:(at + 1) * half] for g in range(4)], axis=1)
        for at in (0, 1)
    ]
    for ref, first in ((mine_ref, lower), (theirs_ref, ~lower)):
        ref[0:SUB, :] = jnp.where(first, local_ref[0:SUB, :], local_ref[SUB:2 * SUB, :])
        ref[SUB:, :] = jnp.where(first, packed[0], packed[1])


def copy_kernel(*refs):
    count = len(refs) // 2
    copies = [
        pltpu.make_async_copy(refs[at], refs[count + at], refs[-1].at[at]) for at in range(count)
    ]
    for copy in copies:
        copy.start()
    for copy in copies:
        copy.wait()


def final_kernel(
    meta_ref, mine_ref, theirs_ref, other_ref, here_ref, x1_ref, x2_ref, x3_ref, position_ref,
    limit_ref, after_ref, loading_ref, margin_ref
):
    actions, share, zones = after_ref.shape
    pairs = actions // 2
    picks = actions * SUB
    bf16 = jnp.bfloat16

    size_x = lax.axis_size("x")
    owner = meta_ref[3:4, :picks].astype(jnp.int32)
    slot = meta_ref[3:4, picks:].astype(jnp.int32)
    back = (lax.axis_index("x") - owner % size_x + size_x) % size_x
    flip = jnp.where(owner // size_x == lax.axis_index("yl"), 0, 1)
    blocks = [
        ref[at * BLOCK_ROWS:(at + 1) * BLOCK_ROWS, :]
        for ref in (here_ref, x1_ref, x2_ref, x3_ref)
        for at in (0, 1)
    ]
    count = len(blocks) * SLOTS
    spread = iota((count, picks), 0) == (back * 2 + flip) * SLOTS + slot
    spread = jnp.where(spread, 1.0, 0.0).astype(bf16)
    half = SLOTS // 2
    switched, coupled = [], []
    lane = iota((half, LANES), 1)
    for block in blocks:
        rows = block[0:half]
        turned = pltpu.roll(rows, HALF, 1)
        switched += [jnp.where(lane < HALF, rows, turned), jnp.where(lane < HALF, turned, rows)]
        extra = block[half:]
        for g in range(SLOTS // SUB):
            coupled.append(jnp.where(iota(extra.shape, 1) // SUB == g, extra, 0.0))
    parts = two_parts(jnp.concatenate(switched, axis=0)) + two_parts(jnp.concatenate(coupled, axis=0))
    found = lax.dot_general(
        spread, jnp.concatenate(parts, axis=1), (((0,), (0,)), ((), ())),
        preferred_element_type=jnp.float32,
    )
    switched = found[:, 0:LANES] + found[:, LANES:2 * LANES]
    coupled = found[:, 2 * LANES:3 * LANES] + found[:, 3 * LANES:]
    shape = (LANES, LANES)
    repeat = (iota(shape, 0) < SLOTS) & (iota(shape, 0) % SUB == iota(shape, 1) % SUB)
    repeat = jnp.where(repeat, 1.0, 0.0).astype(bf16)
    high, low = [dot(part, repeat) for part in two_parts(coupled)]
    coupled = high + low

    shape = (pairs, SUB, LANES)
    row_id, lane = iota(shape, 1), iota(shape, 2)

    def side_by_side(x):
        return jnp.where(
            lane < HALF, x[:picks // 2].reshape(shape), x[picks // 2:].reshape(shape)
        )

    left = jnp.where(lane % SUB == row_id, 1.0, 0.0) - side_by_side(coupled)
    right = side_by_side(switched)
    for pivot in range(SUB):
        factor = jnp.where(
            lane < HALF, left[:, :, pivot:pivot + 1], left[:, :, HALF + pivot:HALF + pivot + 1]
        )
        diagonal = factor[:, pivot:pivot + 1]
        left_now = left[:, pivot:pivot + 1] / diagonal
        right_now = right[:, pivot:pivot + 1] / diagonal
        left = jnp.where(row_id == pivot, left_now, left - factor * left_now)
        right = jnp.where(row_id == pivot, right_now, right - factor * right_now)

    lower = lax.axis_index("act") == 0
    whole = mine_ref[...] + theirs_ref[BLOCK_ROWS:]
    mine, other = whole[0:SUB], other_ref[...]
    low, high = jnp.where(lower, mine, other), jnp.where(lower, other, mine)
    zonal = jnp.concatenate(
        [low[:, :HALF], low[:, HALF:], high[:, :HALF], high[:, HALF:]], axis=0
    )
    zonal_twice = jnp.concatenate([zonal, zonal], axis=1)
    groups = [whole[SUB:, g * share:(g + 1) * share] for g in range(LANES // share)]
    diff = jnp.concatenate(groups, axis=0)
    solved = jnp.concatenate(
        [jnp.where(lane < HALF, right, 0.0), jnp.where(lane < HALF, 0.0, right)], axis=1
    )
    diff_high, diff_low = two_parts(diff)
    solved_high, solved_low = two_parts(solved)

    def product(x, y):
        return lax.dot_general(
            x, y, (((0,), (0,)), ((), ())), preferred_element_type=jnp.float32
        )

    size = 2 * SUB
    for pair in range(pairs):
        at = slice(pair * size, (pair + 1) * size)
        left = jnp.concatenate([diff_high[at], diff_high[at], diff_low[at]], axis=0)
        right = jnp.concatenate(
            [solved_high[pair], solved_low[pair], solved_high[pair]], axis=0
        )
        total = zonal_twice + product(left, right)
        after_ref[2 * pair] = total[:, :HALF]
        after_ref[2 * pair + 1] = total[:, HALF:]
    position = position_ref[...]
    twice = jnp.concatenate([position, position], axis=1)
    moved = by_parts(dot_nt, twice, solved.reshape(pairs * size, LANES))
    shape = (actions, pairs * size)
    same = iota(shape, 1) // SUB == iota(shape, 0)
    flow = by_parts(dot_nt, position, zonal) + by_parts(dot, jnp.where(same, moved, 0.0), diff)
    limit = limit_ref[...]
    loading_ref[...] = flow / limit
    margin_ref[...] = limit - jnp.abs(flow)


def in_hbm(x):
    return pltpu.with_memory_space_constraint(x, pltpu.HBM)


def copied(arrays):
    hbm = pl.BlockSpec(memory_space=pltpu.HBM)
    return pl.pallas_call(
        copy_kernel,
        out_shape=[jax.ShapeDtypeStruct(x.shape, x.dtype) for x in arrays],
        in_specs=[hbm] * len(arrays),
        out_specs=[hbm] * len(arrays),
        scratch_shapes=[pltpu.SemaphoreType.DMA((len(arrays),))],
        name="copies",
    )(*[in_hbm(x) for x in arrays])


def params():
    return pltpu.CompilerParams(vmem_limit_bytes=48 * 1024 * 1024)


def body(
    nodal_sensitivity, shift_weight, bus_zone, branch_buses, switched_rows, net_position, flow_limit
):
    rows, cols = nodal_sensitivity.shape
    zones = net_position.shape[0]
    actions, rank = switched_rows.shape
    picks = actions * rank
    n_z, n_yh = lax.axis_size("z"), lax.axis_size("yh")
    share = rows // n_z // n_yh
    f32, i32 = jnp.float32, jnp.int32
    vmem = pl.BlockSpec(memory_space=pltpu.VMEM)
    hbm = pl.BlockSpec(memory_space=pltpu.HBM)

    weight, zone = [x.reshape(cols // LANES, LANES) for x in (shift_weight, bus_zone)]
    weight, zone = in_hbm(weight), in_hbm(zone)
    bus_scratch = [pltpu.VMEM((cols // LANES, LANES), kind) for kind in (f32, i32)]
    swap = [(0, 1), (1, 0)]
    turn = [(0, 3), (3, 0), (1, 2), (2, 1)]
    totals = pl.pallas_call(
        total_kernel,
        out_shape=jax.ShapeDtypeStruct((SUB, LANES), f32),
        in_specs=[hbm] * 2,
        out_specs=vmem,
        scratch_shapes=[*bus_scratch, pltpu.SemaphoreType.DMA((2,))],
        compiler_params=params(),
        name="totals",
    )(weight, zone)
    totals = totals + lax.ppermute(totals, ("yl", "yh"), turn)
    held, meta, extra, sens = pl.pallas_call(
        column_kernel,
        out_shape=(
            jax.ShapeDtypeStruct((n_z, share, LANES), f32),
            jax.ShapeDtypeStruct((SUB, 2 * picks), f32),
            jax.ShapeDtypeStruct((SLOTS + SUB, LANES), f32),
            pltpu.VMEM((rows, cols), jnp.bfloat16),
        ),
        in_specs=[hbm] * 3,
        out_specs=(vmem,) * 4,
        scratch_shapes=[
            pltpu.VMEM((rank, actions), i32),
            pltpu.VMEM(branch_buses.shape, i32),
            pltpu.VMEM((rows, SLOTS), f32),
            pltpu.VMEM((SLOTS, picks), f32),
            pltpu.SemaphoreType.DMA((cols // BLOCK + 2,)),
        ],
        compiler_params=params(),
        name="columns",
    )(*[in_hbm(x) for x in (switched_rows.T, branch_buses, nodal_sensitivity)])
    coupled = jnp.broadcast_to((extra[SLOTS:] + totals)[None], (n_z, SUB, LANES))
    parts = jnp.concatenate([held, coupled], axis=1)
    parts = lax.all_to_all(parts, "z", 0, 0, tiled=True)
    pay, coupled = pl.pallas_call(
        zonal_kernel,
        out_shape=(
            jax.ShapeDtypeStruct((n_z, 2 * SUB + SLOTS // 2, LANES), f32),
            jax.ShapeDtypeStruct((SUB, LANES), f32),
        ),
        in_specs=[vmem, hbm, hbm, vmem, vmem],
        out_specs=(vmem, vmem),
        scratch_shapes=[
            *bus_scratch,
            pltpu.VMEM((zones, cols), jnp.bfloat16),
            pltpu.VMEM((cols // LANES, LANES), f32),
            pltpu.VMEM((rows, zones), f32),
            pltpu.SemaphoreType.DMA((2,)),
        ],
        compiler_params=params(),
        name="zonal",
    )(parts, weight, zone, pltpu.with_memory_space_constraint(sens, pltpu.VMEM), extra)
    local = jnp.sum(lax.all_to_all(pay, "z", 0, 0, tiled=True), axis=0)
    part = jax.ShapeDtypeStruct((SUB + 2 * share, LANES), f32)
    mine, theirs = pl.pallas_call(
        place_kernel,
        out_shape=(part, part),
        in_specs=[vmem] * 3,
        out_specs=(vmem, vmem),
        compiler_params=params(),
        name="place",
    )(parts, local, meta)

    block = jnp.concatenate([local[2 * SUB:], coupled], axis=0)
    theirs = lax.ppermute(jnp.concatenate([block, theirs], axis=0), "yh", swap)
    beside = lax.ppermute(block, "yl", swap)
    across = lax.ppermute(block, ("yl", "yh"), turn)
    here = jnp.concatenate([block + theirs[:BLOCK_ROWS], beside + across], axis=0)
    n_x = lax.axis_size("x")
    others = [
        lax.ppermute(here, "x", [(at, (at + by) % n_x) for at in range(n_x)])
        for by in range(1, n_x)
    ]
    other = lax.ppermute(
        mine[:SUB] + theirs[BLOCK_ROWS:BLOCK_ROWS + SUB], "act", swap
    )

    def compact():
        outputs = pl.pallas_call(
            final_kernel,
            out_shape=(
                jax.ShapeDtypeStruct((actions, share, zones), f32),
                jax.ShapeDtypeStruct((actions, share), f32),
                jax.ShapeDtypeStruct((actions, share), f32),
            ),
            in_specs=[vmem] * 10,
            out_specs=(vmem, vmem, vmem),
            compiler_params=params(),
            name="update",
        )(
            meta, mine, theirs, other, here, *others,
            net_position.reshape(1, zones), flow_limit.reshape(1, share),
        )
        return tuple(outputs)

    def general():
        inputs = nodal_sensitivity, shift_weight, bus_zone, branch_buses, switched_rows
        return tuple(copied(plain(*copied(inputs), net_position, flow_limit)))

    return lax.cond(meta[2, 0] > 0.5, general, compact)


def sum_over(x, axes):
    spread = jnp.broadcast_to(x[None], (lax.axis_size(axes), *x.shape))
    return jnp.sum(lax.all_to_all(spread, axes, 0, 0, tiled=True), axis=0)


def scattered_sum(x):
    shares = lax.axis_size(BUS)
    x = x.reshape(shares, x.shape[0] // shares, x.shape[1])
    return jnp.sum(lax.all_to_all(x, BUS, 0, 0, tiled=True), axis=0)


def plain(
    nodal_sensitivity, shift_weight, bus_zone, branch_buses, switched_rows, net_position, flow_limit
):
    rows, cols = nodal_sensitivity.shape
    zones = net_position.shape[0]
    actions, rank = switched_rows.shape
    onehot = (bus_zone[:, None] == jnp.arange(zones)[None, :]).astype(jnp.float32)
    total = sum_over(jnp.sum(onehot * shift_weight[:, None], axis=0), BUS)
    key = (onehot * shift_weight[:, None] / total[None, :]).astype(jnp.bfloat16)
    zonal = jnp.dot(nodal_sensitivity, key, preferred_element_type=jnp.float32)
    picks = switched_rows.reshape(-1)

    def columns(buses):
        local = buses - lax.axis_index(BUS) * cols
        owned = (local >= 0) & (local < cols)
        picked = jnp.take(nodal_sensitivity, jnp.clip(local, 0, cols - 1), axis=1)
        return jnp.where(owned[None, :], picked.astype(jnp.float32), 0.0)

    diff = columns(branch_buses[0][picks]) - columns(branch_buses[1][picks])
    zonal, diff = scattered_sum(zonal), scattered_sum(diff)
    share = rows // lax.axis_size(BUS)
    local = picks - lax.axis_index(CNEC) * rows - lax.axis_index(BUS) * share
    owned = ((local >= 0) & (local < share))[:, None]
    local = jnp.clip(local, 0, share - 1)
    switched = jnp.where(owned, jnp.take(zonal, local, axis=0), 0.0)
    coupled = jnp.where(owned, jnp.take(diff, local, axis=0), 0.0)
    coupled = jnp.einsum("aiaj->aij", coupled.reshape(actions, rank, actions, rank))
    both = jnp.concatenate([switched, coupled.reshape(actions * rank, rank)], axis=1)
    both = sum_over(sum_over(both, BUS), CNEC).reshape(actions, rank, zones + rank)
    left, right = jnp.eye(rank, dtype=jnp.float32)[None] - both[:, :, zones:], both[:, :, :zones]
    for pivot in range(rank):
        is_pivot = (jnp.arange(rank) == pivot)[None, :, None]
        factor = left[:, :, pivot:pivot + 1]
        diagonal = factor[:, pivot:pivot + 1]
        left_now, right_now = left[:, pivot:pivot + 1] / diagonal, right[:, pivot:pivot + 1] / diagonal
        left = jnp.where(is_pivot, left_now, left - factor * left_now)
        right = jnp.where(is_pivot, right_now, right - factor * right_now)
    after = zonal[None] + jnp.einsum(
        "caj,ajz->acz", diff.reshape(share, actions, rank), right, precision=HIGHEST
    )
    flow = jnp.einsum("acz,z->ac", after, net_position, precision=HIGHEST)
    return after, flow / flow_limit[None, :], flow_limit[None, :] - jnp.abs(flow)


def solution(mesh):
    n_cnec, n_bus, n_act = mesh.devices.shape
    split = Mesh(
        mesh.devices.reshape(2, n_cnec // 2, n_bus // 2, 2, n_act), ("yl", "x", "z", "yh", "act")
    )
    return jax.shard_map(
        body,
        mesh=split,
        in_specs=(
            P(CNEC, BUS),
            P(BUS),
            P(BUS),
            P(),
            P("act", None),
            P(),
            P(CNEC + BUS),
        ),
        out_specs=(
            P("act", CNEC + BUS, None),
            P("act", CNEC + BUS),
            P("act", CNEC + BUS),
        ),
        check_vma=False,
    )
```

```python
import functools

import jax
import jax.numpy as jnp
from jax import lax
from jax.experimental import pallas as pl
from jax.experimental.pallas import tpu as pltpu
from jax.sharding import Mesh
from jax.sharding import PartitionSpec as P

HIGHEST = lax.Precision.HIGHEST
LANES = 128
HALF = 64
SUB = 8
BLOCK = 2048
SLOTS = 64
BLOCK_ROWS = SLOTS // 2 + SUB
SUMMED = 2 * SUB + BLOCK_ROWS
CNEC, BUS = ("yl", "x"), ("z", "yh")
PLANE = ("yl", "x", "yh")


def iota(shape, dim):
    return lax.broadcasted_iota(jnp.int32, shape, dim)


def dot_nt(x, y, precision=None):
    return lax.dot_general(
        x, y, (((1,), (1,)), ((), ())), precision=precision, preferred_element_type=jnp.float32
    )


def dot(x, y, precision=None):
    return jnp.dot(x, y, precision=precision, preferred_element_type=jnp.float32)


def two_parts(values):
    high = values.astype(jnp.bfloat16)
    return high, (values - high.astype(jnp.float32)).astype(jnp.bfloat16)


def by_parts(product, x, y):
    x_high, x_low = two_parts(x)
    y_high, y_low = two_parts(y)
    return product(x_high, y_high) + product(x_high, y_low) + product(x_low, y_high)


def digits(values, base, count):
    return [((values >> (base * at)) & ((1 << base) - 1)).astype(jnp.float32).astype(jnp.bfloat16)
            for at in reversed(range(count))]


def find_picks(swt, branch_ref):
    rank, actions = swt.shape
    picks = rank * actions
    pick_id = iota((picks, actions), 0)
    of_action = pick_id % LANES // rank * 2 + pick_id // LANES == iota((picks, actions), 1)
    of_action = jnp.where(of_action, 1.0, 0.0).astype(jnp.bfloat16)
    high, low = digits(swt, 6, 2)
    row = dot_nt(high, of_action) * 64.0 + dot_nt(low, of_action)
    row = jnp.where(iota((rank, picks), 1) % rank == iota((rank, picks), 0), row, 0.0)
    row = jnp.sum(row, axis=0, keepdims=True).astype(jnp.int32)
    tiles = branch_ref.shape[1] // LANES
    table = jnp.concatenate(
        [branch_ref[:, at * LANES:(at + 1) * LANES] for at in range(tiles)], axis=0
    )
    onehot = jnp.where(iota((LANES, picks), 0) == row % LANES, 1.0, 0.0).astype(jnp.bfloat16)
    high, middle, low = [dot(part, onehot) for part in digits(table, 6, 3)]
    found = high * 4096.0 + middle * 64.0 + low
    line = iota((2 * tiles, picks), 0) - row // LANES * 2
    ends = [
        jnp.sum(jnp.where(line == end, found, 0.0), axis=0, keepdims=True).astype(jnp.int32)
        for end in (0, 1)
    ]
    return row, ends


def slot_matrix(slots, count):
    shape = (count, slots[0].shape[1])
    first, second = [jnp.where(iota(shape, 0) == slot, 1.0, 0.0) for slot in slots]
    return (first - second).astype(jnp.bfloat16)


def total_kernel(weight_hbm, zone_hbm, out_ref, weight_ref, zone_ref, sems):
    copies = [
        pltpu.make_async_copy(weight_hbm, weight_ref, sems.at[0]),
        pltpu.make_async_copy(zone_hbm, zone_ref, sems.at[1]),
    ]
    for copy in copies:
        copy.start()
    for copy in copies:
        copy.wait()
    ids = iota((HALF, LANES), 0)
    total = jnp.zeros((HALF, LANES), jnp.float32)
    for at in range(weight_ref.shape[0]):
        total += jnp.where(zone_ref[at:at + 1, :] == ids, weight_ref[at:at + 1, :], 0.0)
    total = jnp.sum(total, axis=1, keepdims=True)
    total = jnp.sum(jnp.where(ids == iota((HALF, LANES), 1), total, 0.0), axis=0, keepdims=True)
    out_ref[...] = jnp.broadcast_to(total, out_ref.shape)


def slot_kernel(rows, cols, swt_hbm, branch_hbm, meta_ref, swt_ref, branch_ref, sems):
    copies = [
        pltpu.make_async_copy(swt_hbm, swt_ref, sems.at[0]),
        pltpu.make_async_copy(branch_hbm, branch_ref, sems.at[1]),
    ]
    for copy in copies:
        copy.start()
    for copy in copies:
        copy.wait()
    rank, actions = swt_ref.shape
    picks = rank * actions
    shards, groups = lax.axis_size(BUS), lax.axis_size(CNEC)
    row, ends = find_picks(swt_ref[...], branch_ref)

    def ranks(owner, owners):
        count = owner.shape[1]
        inside = iota((owners, count), 0) == owner
        before = jnp.where(iota((count, count), 0) < iota((count, count), 1), 1.0, 0.0)
        place = dot(jnp.where(inside, 1.0, 0.0).astype(jnp.bfloat16), before.astype(jnp.bfloat16))
        return jnp.sum(jnp.where(inside, place, 0.0), axis=0, keepdims=True)

    bus = jnp.concatenate(ends, axis=1)
    held, place = bus // cols, ranks(bus // cols, shards)
    owner, row_place = row // rows, ranks(row // rows, groups)
    most = jnp.maximum(
        jnp.max(place, axis=1, keepdims=True), jnp.max(row_place, axis=1, keepdims=True)
    )
    over = jnp.where(most >= SLOTS, 1.0, 0.0)
    f32 = jnp.float32
    meta_ref[0:1, :] = held.astype(f32)
    meta_ref[1:2, :] = place
    meta_ref[2:3, :] = jnp.broadcast_to(over, place.shape)
    meta_ref[3:4, :] = jnp.concatenate([owner.astype(f32), row_place], axis=1)
    meta_ref[4:5, :] = (bus - held * cols).astype(f32)
    row = (row - owner * rows).astype(f32)
    meta_ref[5:6, :] = jnp.concatenate([row, row], axis=1)
    meta_ref[6:, :] = jnp.zeros((SUB - 6, place.shape[1]), f32)


def column_kernel(
    meta_ref, after_ref, sens_hbm, held_ref, extra_ref, sens_ref, acc_ref, coupled_ref, sems
):
    rows, cols = sens_ref.shape
    rank = SUB
    count = meta_ref.shape[1]
    picks = count // 2
    steps = cols // BLOCK
    bf16 = jnp.bfloat16

    def block_copy(step):
        at = pl.ds(pl.multiple_of(step * BLOCK, BLOCK), BLOCK)
        return pltpu.make_async_copy(sens_hbm.at[:, at], sens_ref.at[:, at], sems.at[step])

    for step in range(steps):
        block_copy(step).start()

    acc_ref[...] = jnp.zeros_like(acc_ref)
    held = meta_ref[0:1, :].astype(jnp.int32)
    place = meta_ref[1:2, :]
    owner = meta_ref[3:4, :picks].astype(jnp.int32)
    row_place = meta_ref[3:4, picks:]
    local = meta_ref[4:5, :]
    row = meta_ref[5:6, :picks]
    place = place.astype(jnp.int32)
    mine = held == lax.axis_index(BUS)
    slot = jnp.where(mine, place, -1)

    def buses_of(group):
        match = iota((SLOTS, count), 0) + group * SLOTS == slot
        match = jnp.where(match, local + 1.0, 0.0)
        return jnp.sum(match, axis=1, keepdims=True).astype(jnp.int32) - 1

    first_buses = buses_of(0)
    row_slot = jnp.where(owner == lax.axis_index(CNEC), row_place.astype(jnp.int32), -1)
    match = iota((SLOTS, picks), 0) == row_slot
    slot_row = jnp.where(match, row + 1.0, 0.0)
    slot_row = jnp.sum(slot_row, axis=1, keepdims=True) - 1.0
    action_of = iota((SLOTS, picks), 1) // rank
    slot_action = jnp.where(match, action_of.astype(jnp.float32), 0.0)
    slot_action = jnp.sum(slot_action, axis=1, keepdims=True).astype(jnp.int32)
    extra_ref[0:SLOTS, :] = jnp.broadcast_to(slot_row, (SLOTS, LANES))
    choose = iota((SLOTS, rows), 1) == slot_row.astype(jnp.int32)
    choose = jnp.where(choose, 1.0, 0.0).astype(bf16)
    lane = iota((SLOTS, BLOCK), 1)

    def select(buses, step):
        return jnp.where(lane == buses - step * BLOCK, 1.0, 0.0).astype(bf16)

    def step_body(step, carry):
        at = pl.ds(pl.multiple_of(step * BLOCK, BLOCK), BLOCK)
        chosen = select(first_buses, step)
        block_copy(step).wait()
        acc_ref[...] += dot_nt(sens_ref[:, at], chosen)
        return carry

    lax.fori_loop(0, steps, step_body, 0)

    def coupled_of(columns, group):
        slots = [slot[:, at * picks:(at + 1) * picks] - group * SLOTS for at in (0, 1)]
        chosen = dot(choose, columns.astype(bf16))
        return dot(chosen.astype(bf16), slot_matrix(slots, SLOTS))

    columns = acc_ref[...]
    coupled_ref[...] = coupled_of(columns, 0)

    def group_body(group, carry):
        buses = buses_of(group)
        columns = jnp.zeros((rows, SLOTS), jnp.float32)
        for step in range(steps):
            at = pl.ds(step * BLOCK, BLOCK)
            columns += dot_nt(sens_ref[:, at], select(buses, step))
        coupled_ref[...] += coupled_of(columns, group)
        return carry

    groups = (jnp.sum(jnp.where(mine, 1.0, 0.0)).astype(jnp.int32) + SLOTS - 1) // SLOTS
    lax.fori_loop(1, groups, group_body, 0)

    coupled = jnp.where(action_of == slot_action, coupled_ref[...], 0.0)
    fold = jnp.where(iota((picks, LANES), 0) % rank == iota((picks, LANES), 1) % rank, 1.0, 0.0)
    high, low = [dot(part, fold.astype(bf16)) for part in two_parts(coupled)]
    shape = (SLOTS, LANES)
    coupled = jnp.where(iota(shape, 1) // rank == iota(shape, 0) // SUB, high + low, 0.0)
    extra_ref[SLOTS:, :] = jnp.sum(coupled.reshape(SLOTS // SUB, SUB, LANES), axis=0)
    chunks = held_ref.shape[0]
    columns = columns.reshape(chunks, 2, rows // chunks // 2, SLOTS)
    held_ref[...] = jnp.concatenate([columns[:, 0], columns[:, 1]], axis=-1)


def zonal_kernel(totals_ref, weight_hbm, zone_hbm, sens_hbm, held_ref, extra_ref, pay_ref,
                 weight_ref, zone_ref, sens_ref, key_ref, sums_ref, acc_ref, sems):
    rows, cols = sens_ref.shape
    zones = HALF
    part = BLOCK // 2
    steps = cols // part
    bf16 = jnp.bfloat16
    copies = [
        pltpu.make_async_copy(weight_hbm, weight_ref, sems.at[steps]),
        pltpu.make_async_copy(zone_hbm, zone_ref, sems.at[steps + 1]),
    ]
    for copy in copies:
        copy.start()

    def block_copy(step):
        at = pl.ds(pl.multiple_of(step * part, part), part)
        return pltpu.make_async_copy(sens_hbm.at[:, at], sens_ref.at[:, at], sems.at[step])

    for step in range(steps):
        block_copy(step).start()

    acc_ref[...] = jnp.zeros_like(acc_ref)
    pay_ref[:, SUMMED:, :] = held_ref[...]
    total = jnp.sum(totals_ref[...], axis=0)[0:1]
    for copy in copies:
        copy.wait()
    of_bus = jnp.take_along_axis(
        jnp.broadcast_to(total, weight_ref.shape), zone_ref[...], axis=1
    )
    sums_ref[...] = weight_ref[...] / of_bus
    ids = iota((zones, LANES), 0)
    for at in range(cols // LANES):
        key = jnp.where(zone_ref[at:at + 1, :] == ids, sums_ref[at:at + 1, :], 0.0)
        key_ref[:, at * LANES:(at + 1) * LANES] = key.astype(bf16)

    def step_body(step, carry):
        at = pl.ds(pl.multiple_of(step * part, part), part)
        block_copy(step).wait()
        acc_ref[...] += dot_nt(sens_ref[:, at], key_ref[:, at])
        return carry

    lax.fori_loop(0, steps, step_body, 0)

    chunks = pay_ref.shape[0]
    zonal = acc_ref[...]
    choose = iota((SLOTS, rows), 1) == extra_ref[0:SLOTS, 0:1].astype(jnp.int32)
    choose = jnp.where(choose, 1.0, 0.0).astype(bf16)
    switched = dot(choose, jnp.concatenate(two_parts(zonal), axis=1))
    switched = switched[:, 0:zones] + switched[:, zones:]
    share = zonal.reshape(chunks, 2, 2, 2, SUB, zones)
    share = jnp.where(lax.axis_index("act") == 0, share[:, :, 0], share[:, :, 1])
    share = jnp.concatenate([share[:, :, 0], share[:, :, 1]], axis=-1)
    half = SLOTS // 2
    switched = jnp.concatenate([switched[:half], switched[half:]], axis=1)
    block = jnp.concatenate([switched, extra_ref[SLOTS:, :]], axis=0)
    pay_ref[:, 0:2 * SUB, :] = share.reshape(chunks, 2 * SUB, LANES)
    pay_ref[:, 2 * SUB:SUMMED, :] = jnp.broadcast_to(block[None], (chunks, *block.shape))


def spread_kernel(parts_ref, block_ref, local_ref):
    local_ref[...] = jnp.sum(parts_ref[:, 0:2 * SUB, :], axis=0)
    block = jnp.sum(parts_ref[:, 2 * SUB:SUMMED, :], axis=0)
    block_ref[...] = jnp.broadcast_to(block[None], block_ref.shape)


def place_kernel(parts_ref, local_ref, meta_ref, mine_ref, theirs_ref):
    chunks = parts_ref.shape[0]
    picks = meta_ref.shape[1] // 2
    half = parts_ref.shape[1] - SUMMED
    y_here, y_size = lax.axis_index("yh"), lax.axis_size("yh")
    held = meta_ref[0:1, :].astype(jnp.int32)
    place = meta_ref[1:2, :].astype(jnp.int32)
    known = (held % y_size == y_here) & (place < SLOTS)
    slot = jnp.where(known, held // y_size * SLOTS + place, -1)
    spread = slot_matrix([slot[:, at * picks:(at + 1) * picks] for at in (0, 1)], chunks * SLOTS)
    columns = [
        jnp.concatenate(
            [parts_ref[z, SUMMED:, at * SLOTS:(at + 1) * SLOTS] for z in range(chunks)], axis=1
        )
        for at in (0, 1)
    ]
    columns = jnp.concatenate(columns, axis=0).astype(jnp.bfloat16)
    diff = lax.dot_general(
        spread, columns, (((0,), (1,)), ((), ())), preferred_element_type=jnp.float32
    )
    diff = diff.reshape(2, picks // (2 * SUB), SUB, 2 * half)
    diff = jnp.concatenate([diff[0], diff[1]], axis=1).reshape(4, picks // 4, 2 * half)
    lower = y_here == 0
    packed = [
        jnp.concatenate([diff[g, :, at * half:(at + 1) * half] for g in range(4)], axis=1)
        for at in (0, 1)
    ]
    for ref, first in ((mine_ref, lower), (theirs_ref, ~lower)):
        ref[0:SUB, :] = jnp.where(first, local_ref[0:SUB, :], local_ref[SUB:2 * SUB, :])
        ref[SUB:, :] = jnp.where(first, packed[0], packed[1])


def copy_kernel(*refs):
    count = len(refs) // 2
    copies = [
        pltpu.make_async_copy(refs[at], refs[count + at], refs[-1].at[at]) for at in range(count)
    ]
    for copy in copies:
        copy.start()
    for copy in copies:
        copy.wait()


def final_kernel(
    meta_ref, mine_ref, theirs_ref, other_ref, blocks_ref, position_ref, limit_ref,
    after_ref, loading_ref, margin_ref
):
    actions, share, zones = after_ref.shape
    pairs = actions // 2
    picks = actions * SUB
    bf16 = jnp.bfloat16

    owner = meta_ref[3:4, :picks].astype(jnp.int32)
    slot = meta_ref[3:4, picks:].astype(jnp.int32)
    groups = lax.axis_size(CNEC)
    blocks = [blocks_ref[2 * at] + blocks_ref[2 * at + 1] for at in range(groups)]
    count = groups * SLOTS
    spread = iota((count, picks), 0) == owner * SLOTS + slot
    spread = jnp.where(spread, 1.0, 0.0).astype(bf16)
    half = SLOTS // 2
    switched, coupled = [], []
    lane = iota((half, LANES), 1)
    for block in blocks:
        rows = block[0:half]
        turned = pltpu.roll(rows, HALF, 1)
        switched += [jnp.where(lane < HALF, rows, turned), jnp.where(lane < HALF, turned, rows)]
        extra = block[half:]
        for g in range(SLOTS // SUB):
            coupled.append(jnp.where(iota(extra.shape, 1) // SUB == g, extra, 0.0))
    parts = two_parts(jnp.concatenate(switched, axis=0)) + two_parts(jnp.concatenate(coupled, axis=0))
    found = lax.dot_general(
        spread, jnp.concatenate(parts, axis=1), (((0,), (0,)), ((), ())),
        preferred_element_type=jnp.float32,
    )
    switched = found[:, 0:LANES] + found[:, LANES:2 * LANES]
    coupled = found[:, 2 * LANES:3 * LANES] + found[:, 3 * LANES:]
    shape = (LANES, LANES)
    repeat = (iota(shape, 0) < SLOTS) & (iota(shape, 0) % SUB == iota(shape, 1) % SUB)
    repeat = jnp.where(repeat, 1.0, 0.0).astype(bf16)
    high, low = [dot(part, repeat) for part in two_parts(coupled)]
    coupled = high + low

    shape = (pairs, SUB, LANES)
    row_id, lane = iota(shape, 1), iota(shape, 2)

    def side_by_side(x):
        return jnp.where(
            lane < HALF, x[:picks // 2].reshape(shape), x[picks // 2:].reshape(shape)
        )

    left = jnp.where(lane % SUB == row_id, 1.0, 0.0) - side_by_side(coupled)
    right = side_by_side(switched)
    for pivot in range(SUB):
        factor = jnp.where(
            lane < HALF, left[:, :, pivot:pivot + 1], left[:, :, HALF + pivot:HALF + pivot + 1]
        )
        diagonal = factor[:, pivot:pivot + 1]
        left_now = left[:, pivot:pivot + 1] / diagonal
        right_now = right[:, pivot:pivot + 1] / diagonal
        left = jnp.where(row_id == pivot, left_now, left - factor * left_now)
        right = jnp.where(row_id == pivot, right_now, right - factor * right_now)

    lower = lax.axis_index("act") == 0
    whole = mine_ref[...] + theirs_ref[...]
    mine, other = whole[0:SUB], other_ref[...]
    low, high = jnp.where(lower, mine, other), jnp.where(lower, other, mine)
    zonal = jnp.concatenate(
        [low[:, :HALF], low[:, HALF:], high[:, :HALF], high[:, HALF:]], axis=0
    )
    zonal_twice = jnp.concatenate([zonal, zonal], axis=1)
    groups = [whole[SUB:, g * share:(g + 1) * share] for g in range(LANES // share)]
    diff = jnp.concatenate(groups, axis=0)
    solved = jnp.concatenate(
        [jnp.where(lane < HALF, right, 0.0), jnp.where(lane < HALF, 0.0, right)], axis=1
    )
    diff_high, diff_low = two_parts(diff)
    solved_high, solved_low = two_parts(solved)

    def product(x, y):
        return lax.dot_general(
            x, y, (((0,), (0,)), ((), ())), preferred_element_type=jnp.float32
        )

    size = 2 * SUB
    for pair in range(pairs):
        at = slice(pair * size, (pair + 1) * size)
        left = jnp.concatenate([diff_high[at], diff_high[at], diff_low[at]], axis=0)
        right = jnp.concatenate(
            [solved_high[pair], solved_low[pair], solved_high[pair]], axis=0
        )
        total = zonal_twice + product(left, right)
        after_ref[2 * pair] = total[:, :HALF]
        after_ref[2 * pair + 1] = total[:, HALF:]
    position = position_ref[...]
    twice = jnp.concatenate([position, position], axis=1)
    moved = by_parts(dot_nt, twice, solved.reshape(pairs * size, LANES))
    shape = (actions, pairs * size)
    same = iota(shape, 1) // SUB == iota(shape, 0)
    flow = by_parts(dot_nt, position, zonal) + by_parts(dot, jnp.where(same, moved, 0.0), diff)
    limit = limit_ref[...]
    loading_ref[...] = flow / limit
    margin_ref[...] = limit - jnp.abs(flow)


def in_hbm(x):
    return pltpu.with_memory_space_constraint(x, pltpu.HBM)


def copied(arrays):
    hbm = pl.BlockSpec(memory_space=pltpu.HBM)
    return pl.pallas_call(
        copy_kernel,
        out_shape=[jax.ShapeDtypeStruct(x.shape, x.dtype) for x in arrays],
        in_specs=[hbm] * len(arrays),
        out_specs=[hbm] * len(arrays),
        scratch_shapes=[pltpu.SemaphoreType.DMA((len(arrays),))],
        name="copies",
    )(*[in_hbm(x) for x in arrays])


def params():
    return pltpu.CompilerParams(vmem_limit_bytes=48 * 1024 * 1024)


def body(
    nodal_sensitivity, shift_weight, bus_zone, branch_buses, switched_rows, net_position, flow_limit
):
    rows, cols = nodal_sensitivity.shape
    zones = net_position.shape[0]
    actions, rank = switched_rows.shape
    picks = actions * rank
    n_z, n_yh = lax.axis_size("z"), lax.axis_size("yh")
    share = rows // n_z // n_yh
    f32, i32 = jnp.float32, jnp.int32
    vmem = pl.BlockSpec(memory_space=pltpu.VMEM)
    hbm = pl.BlockSpec(memory_space=pltpu.HBM)

    weight, zone = [x.reshape(cols // LANES, LANES) for x in (shift_weight, bus_zone)]
    weight, zone = in_hbm(weight), in_hbm(zone)
    bus_scratch = [pltpu.VMEM((cols // LANES, LANES), kind) for kind in (f32, i32)]
    totals = pl.pallas_call(
        total_kernel,
        out_shape=jax.ShapeDtypeStruct((SUB, LANES), f32),
        in_specs=[hbm] * 2,
        out_specs=vmem,
        scratch_shapes=[*bus_scratch, pltpu.SemaphoreType.DMA((2,))],
        compiler_params=params(),
        name="totals",
    )(weight, zone)
    turn = [(0, 3), (3, 0), (1, 2), (2, 1)]
    totals = totals + lax.ppermute(totals, ("yl", "yh"), turn)
    meta = pl.pallas_call(
        functools.partial(slot_kernel, rows, cols),
        out_shape=jax.ShapeDtypeStruct((SUB, 2 * picks), f32),
        in_specs=[hbm] * 2,
        out_specs=vmem,
        scratch_shapes=[
            pltpu.VMEM((rank, actions), i32),
            pltpu.VMEM(branch_buses.shape, i32),
            pltpu.SemaphoreType.DMA((2,)),
        ],
        compiler_params=params(),
        name="slots",
    )(in_hbm(switched_rows.T), in_hbm(branch_buses))
    sens_scratch = pltpu.VMEM((rows, cols), jnp.bfloat16)
    held, extra = pl.pallas_call(
        column_kernel,
        out_shape=(
            jax.ShapeDtypeStruct((n_z, share, LANES), f32),
            jax.ShapeDtypeStruct((SLOTS + SUB, LANES), f32),
        ),
        in_specs=[vmem, vmem, hbm],
        out_specs=(vmem,) * 2,
        scratch_shapes=[
            sens_scratch,
            pltpu.VMEM((rows, SLOTS), f32),
            pltpu.VMEM((SLOTS, picks), f32),
            pltpu.SemaphoreType.DMA((cols // BLOCK,)),
        ],
        compiler_params=params(),
        name="columns",
    )(meta, totals, in_hbm(nodal_sensitivity))
    totals = jnp.broadcast_to(totals[None], (n_z, SUB, LANES))
    totals = lax.all_to_all(totals, "z", 0, 0, tiled=True)
    pay = pl.pallas_call(
        zonal_kernel,
        out_shape=jax.ShapeDtypeStruct((n_z, SUMMED + share, LANES), f32),
        in_specs=[vmem, hbm, hbm, hbm, vmem, vmem],
        out_specs=vmem,
        scratch_shapes=[
            *bus_scratch,
            sens_scratch,
            pltpu.VMEM((zones, cols), jnp.bfloat16),
            pltpu.VMEM((cols // LANES, LANES), f32),
            pltpu.VMEM((rows, zones), f32),
            pltpu.SemaphoreType.DMA((2 * cols // BLOCK + 2,)),
        ],
        compiler_params=params(),
        name="zonal",
    )(totals, weight, zone, in_hbm(nodal_sensitivity), held, extra)

    swap = [(0, 1), (1, 0)]
    parts = lax.all_to_all(pay, "z", 0, 0, tiled=True)
    block, local = pl.pallas_call(
        spread_kernel,
        out_shape=(
            jax.ShapeDtypeStruct((lax.axis_size(PLANE), BLOCK_ROWS, LANES), f32),
            jax.ShapeDtypeStruct((2 * SUB, LANES), f32),
        ),
        in_specs=[vmem],
        out_specs=(vmem, vmem),
        compiler_params=params(),
        name="spread",
    )(parts)
    blocks = lax.all_to_all(block, PLANE, 0, 0, tiled=True)
    part = jax.ShapeDtypeStruct((SUB + 2 * share, LANES), f32)
    mine, theirs = pl.pallas_call(
        place_kernel,
        out_shape=(part, part),
        in_specs=[vmem] * 3,
        out_specs=(vmem, vmem),
        compiler_params=params(),
        name="place",
    )(parts, local, meta)

    theirs = lax.ppermute(theirs, "yh", swap)
    other = lax.ppermute(mine[:SUB] + theirs[:SUB], "act", swap)

    def compact():
        outputs = pl.pallas_call(
            final_kernel,
            out_shape=(
                jax.ShapeDtypeStruct((actions, share, zones), f32),
                jax.ShapeDtypeStruct((actions, share), f32),
                jax.ShapeDtypeStruct((actions, share), f32),
            ),
            in_specs=[vmem] * 7,
            out_specs=(vmem, vmem, vmem),
            compiler_params=params(),
            name="update",
        )(
            meta, mine, theirs, other, blocks,
            net_position.reshape(1, zones), flow_limit.reshape(1, share),
        )
        return tuple(outputs)

    def general():
        inputs = nodal_sensitivity, shift_weight, bus_zone, branch_buses, switched_rows
        return tuple(copied(plain(*copied(inputs), net_position, flow_limit)))

    return lax.cond(meta[2, 0] > 0.5, general, compact)


def sum_over(x, axes):
    spread = jnp.broadcast_to(x[None], (lax.axis_size(axes), *x.shape))
    return jnp.sum(lax.all_to_all(spread, axes, 0, 0, tiled=True), axis=0)


def scattered_sum(x):
    shares = lax.axis_size(BUS)
    x = x.reshape(shares, x.shape[0] // shares, x.shape[1])
    return jnp.sum(lax.all_to_all(x, BUS, 0, 0, tiled=True), axis=0)


def plain(
    nodal_sensitivity, shift_weight, bus_zone, branch_buses, switched_rows, net_position, flow_limit
):
    rows, cols = nodal_sensitivity.shape
    zones = net_position.shape[0]
    actions, rank = switched_rows.shape
    onehot = (bus_zone[:, None] == jnp.arange(zones)[None, :]).astype(jnp.float32)
    total = sum_over(jnp.sum(onehot * shift_weight[:, None], axis=0), BUS)
    key = (onehot * shift_weight[:, None] / total[None, :]).astype(jnp.bfloat16)
    zonal = jnp.dot(nodal_sensitivity, key, preferred_element_type=jnp.float32)
    picks = switched_rows.reshape(-1)

    def columns(buses):
        local = buses - lax.axis_index(BUS) * cols
        owned = (local >= 0) & (local < cols)
        picked = jnp.take(nodal_sensitivity, jnp.clip(local, 0, cols - 1), axis=1)
        return jnp.where(owned[None, :], picked.astype(jnp.float32), 0.0)

    diff = columns(branch_buses[0][picks]) - columns(branch_buses[1][picks])
    zonal, diff = scattered_sum(zonal), scattered_sum(diff)
    share = rows // lax.axis_size(BUS)
    local = picks - lax.axis_index(CNEC) * rows - lax.axis_index(BUS) * share
    owned = ((local >= 0) & (local < share))[:, None]
    local = jnp.clip(local, 0, share - 1)
    switched = jnp.where(owned, jnp.take(zonal, local, axis=0), 0.0)
    coupled = jnp.where(owned, jnp.take(diff, local, axis=0), 0.0)
    coupled = jnp.einsum("aiaj->aij", coupled.reshape(actions, rank, actions, rank))
    both = jnp.concatenate([switched, coupled.reshape(actions * rank, rank)], axis=1)
    both = sum_over(sum_over(both, BUS), CNEC).reshape(actions, rank, zones + rank)
    left, right = jnp.eye(rank, dtype=jnp.float32)[None] - both[:, :, zones:], both[:, :, :zones]
    for pivot in range(rank):
        is_pivot = (jnp.arange(rank) == pivot)[None, :, None]
        factor = left[:, :, pivot:pivot + 1]
        diagonal = factor[:, pivot:pivot + 1]
        left_now, right_now = left[:, pivot:pivot + 1] / diagonal, right[:, pivot:pivot + 1] / diagonal
        left = jnp.where(is_pivot, left_now, left - factor * left_now)
        right = jnp.where(is_pivot, right_now, right - factor * right_now)
    after = zonal[None] + jnp.einsum(
        "caj,ajz->acz", diff.reshape(share, actions, rank), right, precision=HIGHEST
    )
    flow = jnp.einsum("acz,z->ac", after, net_position, precision=HIGHEST)
    return after, flow / flow_limit[None, :], flow_limit[None, :] - jnp.abs(flow)


def solution(mesh):
    n_cnec, n_bus, n_act = mesh.devices.shape
    split = Mesh(
        mesh.devices.reshape(2, n_cnec // 2, n_bus // 2, 2, n_act), ("yl", "x", "z", "yh", "act")
    )
    return jax.shard_map(
        body,
        mesh=split,
        in_specs=(
            P(CNEC, BUS),
            P(BUS),
            P(BUS),
            P(),
            P("act", None),
            P(),
            P(CNEC + BUS),
        ),
        out_specs=(
            P("act", CNEC + BUS, None),
            P("act", CNEC + BUS),
            P("act", CNEC + BUS),
        ),
        check_vma=False,
    )
```

```python
import jax
import jax.numpy as jnp
from jax import lax
from jax.experimental import pallas as pl
from jax.experimental.pallas import tpu as pltpu
from jax.sharding import Mesh
from jax.sharding import PartitionSpec as P

HIGHEST = lax.Precision.HIGHEST
LANES = 128
HALF = 64
SUB = 8
BLOCK = 2048
SLOTS = 64
BLOCK_ROWS = SLOTS // 2 + SUB
SUMMED = 2 * SUB + BLOCK_ROWS
CNEC, BUS = ("yl", "x"), ("z", "yh")


def iota(shape, dim):
    return lax.broadcasted_iota(jnp.int32, shape, dim)


def dot_nt(x, y, precision=None):
    return lax.dot_general(
        x, y, (((1,), (1,)), ((), ())), precision=precision, preferred_element_type=jnp.float32
    )


def dot(x, y, precision=None):
    return jnp.dot(x, y, precision=precision, preferred_element_type=jnp.float32)


def two_parts(values):
    high = values.astype(jnp.bfloat16)
    return high, (values - high.astype(jnp.float32)).astype(jnp.bfloat16)


def by_parts(product, x, y):
    x_high, x_low = two_parts(x)
    y_high, y_low = two_parts(y)
    return product(x_high, y_high) + product(x_high, y_low) + product(x_low, y_high)


def digits(values, base, count):
    return [((values >> (base * at)) & ((1 << base) - 1)).astype(jnp.float32).astype(jnp.bfloat16)
            for at in reversed(range(count))]


def find_picks(swt, branch_ref):
    rank, actions = swt.shape
    picks = rank * actions
    pick_id = iota((picks, actions), 0)
    of_action = pick_id % LANES // rank * 2 + pick_id // LANES == iota((picks, actions), 1)
    of_action = jnp.where(of_action, 1.0, 0.0).astype(jnp.bfloat16)
    high, low = digits(swt, 6, 2)
    row = dot_nt(high, of_action) * 64.0 + dot_nt(low, of_action)
    row = jnp.where(iota((rank, picks), 1) % rank == iota((rank, picks), 0), row, 0.0)
    row = jnp.sum(row, axis=0, keepdims=True).astype(jnp.int32)
    tiles = branch_ref.shape[1] // LANES
    table = jnp.concatenate(
        [branch_ref[:, at * LANES:(at + 1) * LANES] for at in range(tiles)], axis=0
    )
    onehot = jnp.where(iota((LANES, picks), 0) == row % LANES, 1.0, 0.0).astype(jnp.bfloat16)
    high, middle, low = [dot(part, onehot) for part in digits(table, 6, 3)]
    found = high * 4096.0 + middle * 64.0 + low
    line = iota((2 * tiles, picks), 0) - row // LANES * 2
    ends = [
        jnp.sum(jnp.where(line == end, found, 0.0), axis=0, keepdims=True).astype(jnp.int32)
        for end in (0, 1)
    ]
    return row, ends


def slot_matrix(slots, count):
    shape = (count, slots[0].shape[1])
    first, second = [jnp.where(iota(shape, 0) == slot, 1.0, 0.0) for slot in slots]
    return (first - second).astype(jnp.bfloat16)


def total_kernel(weight_hbm, zone_hbm, out_ref, weight_ref, zone_ref, sems):
    copies = [
        pltpu.make_async_copy(weight_hbm, weight_ref, sems.at[0]),
        pltpu.make_async_copy(zone_hbm, zone_ref, sems.at[1]),
    ]
    for copy in copies:
        copy.start()
    for copy in copies:
        copy.wait()
    ids = iota((HALF, LANES), 0)
    total = jnp.zeros((HALF, LANES), jnp.float32)
    for at in range(weight_ref.shape[0]):
        total += jnp.where(zone_ref[at:at + 1, :] == ids, weight_ref[at:at + 1, :], 0.0)
    total = jnp.sum(total, axis=1, keepdims=True)
    total = jnp.sum(jnp.where(ids == iota((HALF, LANES), 1), total, 0.0), axis=0, keepdims=True)
    out_ref[...] = jnp.broadcast_to(total[None], out_ref.shape)


def column_kernel(
    swt_hbm, branch_hbm, sens_hbm, held_ref, meta_ref, extra_ref,
    swt_ref, branch_ref, sens_ref, acc_ref, coupled_ref, sems
):
    rows, cols = sens_ref.shape
    rank, actions = swt_ref.shape
    picks = rank * actions
    steps = cols // BLOCK
    bf16 = jnp.bfloat16
    small = [
        pltpu.make_async_copy(swt_hbm, swt_ref, sems.at[steps]),
        pltpu.make_async_copy(branch_hbm, branch_ref, sems.at[steps + 1]),
    ]
    for copy in small:
        copy.start()

    def block_copy(step):
        at = pl.ds(pl.multiple_of(step * BLOCK, BLOCK), BLOCK)
        return pltpu.make_async_copy(sens_hbm.at[:, at], sens_ref.at[:, at], sems.at[step])

    for step in range(steps):
        block_copy(step).start()

    shard = lax.axis_index(BUS)
    row_start = lax.axis_index(CNEC) * rows
    acc_ref[...] = jnp.zeros_like(acc_ref)
    for copy in small:
        copy.wait()
    row, ends = find_picks(swt_ref[...], branch_ref)

    def ranks(owner, owners):
        count = owner.shape[1]
        inside = iota((owners, count), 0) == owner
        before = jnp.where(iota((count, count), 0) < iota((count, count), 1), 1.0, 0.0)
        place = dot(jnp.where(inside, 1.0, 0.0).astype(bf16), before.astype(bf16))
        return jnp.sum(jnp.where(inside, place, 0.0), axis=0, keepdims=True)

    bus = jnp.concatenate(ends, axis=1)
    count = 2 * picks
    held, place = bus // cols, ranks(bus // cols, lax.axis_size(BUS))
    owner, row_place = row // rows, ranks(row // rows, lax.axis_size(CNEC))
    most = jnp.maximum(
        jnp.max(place, axis=1, keepdims=True), jnp.max(row_place, axis=1, keepdims=True)
    )
    over = jnp.where(most >= SLOTS, 1.0, 0.0)
    meta_ref[0:1, :] = held.astype(jnp.float32)
    meta_ref[1:2, :] = place
    meta_ref[2:3, :] = jnp.broadcast_to(over, (1, count))
    meta_ref[3:4, :] = jnp.concatenate([owner.astype(jnp.float32), row_place], axis=1)
    meta_ref[4:, :] = jnp.zeros((SUB - 4, count), jnp.float32)
    place = place.astype(jnp.int32)
    mine = held == shard
    slot = jnp.where(mine, place, -1)
    local = bus - shard * cols

    def buses_of(group):
        match = iota((SLOTS, count), 0) + group * SLOTS == slot
        match = jnp.where(match, (local + 1).astype(jnp.float32), 0.0)
        return jnp.sum(match, axis=1, keepdims=True).astype(jnp.int32) - 1

    first_buses = buses_of(0)
    row_slot = jnp.where(owner == lax.axis_index(CNEC), row_place.astype(jnp.int32), -1)
    match = iota((SLOTS, picks), 0) == row_slot
    slot_row = jnp.where(match, (row - row_start + 1).astype(jnp.float32), 0.0)
    slot_row = jnp.sum(slot_row, axis=1, keepdims=True) - 1.0
    action_of = iota((SLOTS, picks), 1) // rank
    slot_action = jnp.where(match, action_of.astype(jnp.float32), 0.0)
    slot_action = jnp.sum(slot_action, axis=1, keepdims=True).astype(jnp.int32)
    extra_ref[0:SLOTS, :] = jnp.broadcast_to(slot_row, (SLOTS, LANES))
    choose = iota((SLOTS, rows), 1) == slot_row.astype(jnp.int32)
    choose = jnp.where(choose, 1.0, 0.0).astype(bf16)
    lane = iota((SLOTS, BLOCK), 1)

    def select(buses, step):
        return jnp.where(lane == buses - step * BLOCK, 1.0, 0.0).astype(bf16)

    def step_body(step, carry):
        at = pl.ds(pl.multiple_of(step * BLOCK, BLOCK), BLOCK)
        chosen = select(first_buses, step)
        block_copy(step).wait()
        acc_ref[...] += dot_nt(sens_ref[:, at], chosen)
        return carry

    lax.fori_loop(0, steps, step_body, 0)

    def coupled_of(columns, group):
        slots = [slot[:, at * picks:(at + 1) * picks] - group * SLOTS for at in (0, 1)]
        chosen = dot(choose, columns.astype(bf16))
        return dot(chosen.astype(bf16), slot_matrix(slots, SLOTS))

    columns = acc_ref[...]
    coupled_ref[...] = coupled_of(columns, 0)

    def group_body(group, carry):
        buses = buses_of(group)
        columns = jnp.zeros((rows, SLOTS), jnp.float32)
        for step in range(steps):
            at = pl.ds(step * BLOCK, BLOCK)
            columns += dot_nt(sens_ref[:, at], select(buses, step))
        coupled_ref[...] += coupled_of(columns, group)
        return carry

    groups = (jnp.sum(jnp.where(mine, 1.0, 0.0)).astype(jnp.int32) + SLOTS - 1) // SLOTS
    lax.fori_loop(1, groups, group_body, 0)

    coupled = jnp.where(action_of == slot_action, coupled_ref[...], 0.0)
    fold = jnp.where(iota((picks, LANES), 0) % rank == iota((picks, LANES), 1) % rank, 1.0, 0.0)
    high, low = [dot(part, fold.astype(bf16)) for part in two_parts(coupled)]
    shape = (SLOTS, LANES)
    coupled = jnp.where(iota(shape, 1) // rank == iota(shape, 0) // SUB, high + low, 0.0)
    extra_ref[SLOTS:, :] = jnp.sum(coupled.reshape(SLOTS // SUB, SUB, LANES), axis=0)
    chunks = held_ref.shape[0]
    columns = columns.reshape(chunks, 2, rows // chunks // 2, SLOTS)
    held_ref[...] = jnp.concatenate([columns[:, 0], columns[:, 1]], axis=-1)


def zonal_kernel(totals_ref, weight_hbm, zone_hbm, sens_hbm, held_ref, extra_ref, pay_ref,
                 weight_ref, zone_ref, sens_ref, key_ref, sums_ref, acc_ref, sems):
    rows, cols = sens_ref.shape
    zones = HALF
    part = BLOCK // 2
    steps = cols // part
    bf16 = jnp.bfloat16
    copies = [
        pltpu.make_async_copy(weight_hbm, weight_ref, sems.at[steps]),
        pltpu.make_async_copy(zone_hbm, zone_ref, sems.at[steps + 1]),
    ]
    for copy in copies:
        copy.start()

    def block_copy(step):
        at = pl.ds(pl.multiple_of(step * part, part), part)
        return pltpu.make_async_copy(sens_hbm.at[:, at], sens_ref.at[:, at], sems.at[step])

    for step in range(steps):
        block_copy(step).start()

    acc_ref[...] = jnp.zeros_like(acc_ref)
    pay_ref[:, SUMMED:, :] = held_ref[...]
    total = jnp.sum(totals_ref[...], axis=0)
    for copy in copies:
        copy.wait()
    of_bus = jnp.take_along_axis(
        jnp.broadcast_to(total, weight_ref.shape), zone_ref[...], axis=1
    )
    sums_ref[...] = weight_ref[...] / of_bus
    ids = iota((zones, LANES), 0)
    for at in range(cols // LANES):
        key = jnp.where(zone_ref[at:at + 1, :] == ids, sums_ref[at:at + 1, :], 0.0)
        key_ref[:, at * LANES:(at + 1) * LANES] = key.astype(bf16)

    def step_body(step, carry):
        at = pl.ds(pl.multiple_of(step * part, part), part)
        block_copy(step).wait()
        acc_ref[...] += dot_nt(sens_ref[:, at], key_ref[:, at])
        return carry

    lax.fori_loop(0, steps, step_body, 0)

    chunks = pay_ref.shape[0]
    zonal = acc_ref[...]
    choose = iota((SLOTS, rows), 1) == extra_ref[0:SLOTS, 0:1].astype(jnp.int32)
    choose = jnp.where(choose, 1.0, 0.0).astype(bf16)
    switched = dot(choose, jnp.concatenate(two_parts(zonal), axis=1))
    switched = switched[:, 0:zones] + switched[:, zones:]
    share = zonal.reshape(chunks, 2, 2, 2, SUB, zones)
    share = jnp.where(lax.axis_index("act") == 0, share[:, :, 0], share[:, :, 1])
    share = jnp.concatenate([share[:, :, 0], share[:, :, 1]], axis=-1)
    half = SLOTS // 2
    switched = jnp.concatenate([switched[:half], switched[half:]], axis=1)
    block = jnp.concatenate([switched, extra_ref[SLOTS:, :]], axis=0)
    pay_ref[:, 0:2 * SUB, :] = share.reshape(chunks, 2 * SUB, LANES)
    pay_ref[:, 2 * SUB:SUMMED, :] = jnp.broadcast_to(block[None], (chunks, *block.shape))


def place_kernel(parts_ref, local_ref, meta_ref, mine_ref, theirs_ref):
    chunks = parts_ref.shape[0]
    picks = meta_ref.shape[1] // 2
    half = parts_ref.shape[1] - SUMMED
    y_here, y_size = lax.axis_index("yh"), lax.axis_size("yh")
    held = meta_ref[0:1, :].astype(jnp.int32)
    place = meta_ref[1:2, :].astype(jnp.int32)
    known = (held % y_size == y_here) & (place < SLOTS)
    slot = jnp.where(known, held // y_size * SLOTS + place, -1)
    spread = slot_matrix([slot[:, at * picks:(at + 1) * picks] for at in (0, 1)], chunks * SLOTS)
    columns = [
        jnp.concatenate(
            [parts_ref[z, SUMMED:, at * SLOTS:(at + 1) * SLOTS] for z in range(chunks)], axis=1
        )
        for at in (0, 1)
    ]
    columns = jnp.concatenate(columns, axis=0).astype(jnp.bfloat16)
    diff = lax.dot_general(
        spread, columns, (((0,), (1,)), ((), ())), preferred_element_type=jnp.float32
    )
    diff = diff.reshape(2, picks // (2 * SUB), SUB, 2 * half)
    diff = jnp.concatenate([diff[0], diff[1]], axis=1).reshape(4, picks // 4, 2 * half)
    lower = y_here == 0
    packed = [
        jnp.concatenate([diff[g, :, at * half:(at + 1) * half] for g in range(4)], axis=1)
        for at in (0, 1)
    ]
    for ref, first in ((mine_ref, lower), (theirs_ref, ~lower)):
        ref[0:SUB, :] = jnp.where(first, local_ref[0:SUB, :], local_ref[SUB:2 * SUB, :])
        ref[SUB:, :] = jnp.where(first, packed[0], packed[1])


def copy_kernel(*refs):
    count = len(refs) // 2
    copies = [
        pltpu.make_async_copy(refs[at], refs[count + at], refs[-1].at[at]) for at in range(count)
    ]
    for copy in copies:
        copy.start()
    for copy in copies:
        copy.wait()


def final_kernel(
    meta_ref, mine_ref, theirs_ref, other_ref, here_ref, x1_ref, x2_ref, x3_ref, position_ref,
    limit_ref, after_ref, loading_ref, margin_ref
):
    actions, share, zones = after_ref.shape
    pairs = actions // 2
    picks = actions * SUB
    bf16 = jnp.bfloat16

    size_x = lax.axis_size("x")
    owner = meta_ref[3:4, :picks].astype(jnp.int32)
    slot = meta_ref[3:4, picks:].astype(jnp.int32)
    back = (lax.axis_index("x") - owner % size_x + size_x) % size_x
    flip = jnp.where(owner // size_x == lax.axis_index("yl"), 0, 1)
    blocks = [
        ref[at * BLOCK_ROWS:(at + 1) * BLOCK_ROWS, :]
        for ref in (here_ref, x1_ref, x2_ref, x3_ref)
        for at in (0, 1)
    ]
    count = len(blocks) * SLOTS
    spread = iota((count, picks), 0) == (back * 2 + flip) * SLOTS + slot
    spread = jnp.where(spread, 1.0, 0.0).astype(bf16)
    half = SLOTS // 2
    switched, coupled = [], []
    lane = iota((half, LANES), 1)
    for block in blocks:
        rows = block[0:half]
        turned = pltpu.roll(rows, HALF, 1)
        switched += [jnp.where(lane < HALF, rows, turned), jnp.where(lane < HALF, turned, rows)]
        extra = block[half:]
        for g in range(SLOTS // SUB):
            coupled.append(jnp.where(iota(extra.shape, 1) // SUB == g, extra, 0.0))
    parts = two_parts(jnp.concatenate(switched, axis=0)) + two_parts(jnp.concatenate(coupled, axis=0))
    found = lax.dot_general(
        spread, jnp.concatenate(parts, axis=1), (((0,), (0,)), ((), ())),
        preferred_element_type=jnp.float32,
    )
    switched = found[:, 0:LANES] + found[:, LANES:2 * LANES]
    coupled = found[:, 2 * LANES:3 * LANES] + found[:, 3 * LANES:]
    shape = (LANES, LANES)
    repeat = (iota(shape, 0) < SLOTS) & (iota(shape, 0) % SUB == iota(shape, 1) % SUB)
    repeat = jnp.where(repeat, 1.0, 0.0).astype(bf16)
    high, low = [dot(part, repeat) for part in two_parts(coupled)]
    coupled = high + low

    shape = (pairs, SUB, LANES)
    row_id, lane = iota(shape, 1), iota(shape, 2)

    def side_by_side(x):
        return jnp.where(
            lane < HALF, x[:picks // 2].reshape(shape), x[picks // 2:].reshape(shape)
        )

    left = jnp.where(lane % SUB == row_id, 1.0, 0.0) - side_by_side(coupled)
    right = side_by_side(switched)
    for pivot in range(SUB):
        factor = jnp.where(
            lane < HALF, left[:, :, pivot:pivot + 1], left[:, :, HALF + pivot:HALF + pivot + 1]
        )
        inverse = 1.0 / factor[:, pivot:pivot + 1]
        left_now = left[:, pivot:pivot + 1] * inverse
        right_now = right[:, pivot:pivot + 1] * inverse
        left = jnp.where(row_id == pivot, left_now, left - factor * left_now)
        right = jnp.where(row_id == pivot, right_now, right - factor * right_now)

    lower = lax.axis_index("act") == 0
    whole = mine_ref[...] + theirs_ref[BLOCK_ROWS:]
    mine, other = whole[0:SUB], other_ref[...]
    low, high = jnp.where(lower, mine, other), jnp.where(lower, other, mine)
    zonal = jnp.concatenate(
        [low[:, :HALF], low[:, HALF:], high[:, :HALF], high[:, HALF:]], axis=0
    )
    zonal_twice = jnp.concatenate([zonal, zonal], axis=1)
    groups = [whole[SUB:, g * share:(g + 1) * share] for g in range(LANES // share)]
    diff = jnp.concatenate(groups, axis=0)
    solved = jnp.concatenate(
        [jnp.where(lane < HALF, right, 0.0), jnp.where(lane < HALF, 0.0, right)], axis=1
    )
    diff_high, diff_low = two_parts(diff)
    solved_high, solved_low = two_parts(solved)

    def product(x, y):
        return lax.dot_general(
            x, y, (((0,), (0,)), ((), ())), preferred_element_type=jnp.float32
        )

    size = 2 * SUB
    for pair in range(pairs):
        at = slice(pair * size, (pair + 1) * size)
        left = jnp.concatenate([diff_high[at], diff_high[at], diff_low[at]], axis=0)
        right = jnp.concatenate(
            [solved_high[pair], solved_low[pair], solved_high[pair]], axis=0
        )
        total = zonal_twice + product(left, right)
        after_ref[2 * pair] = total[:, :HALF]
        after_ref[2 * pair + 1] = total[:, HALF:]
    position = position_ref[...]
    twice = jnp.concatenate([position, position], axis=1)
    moved = by_parts(dot_nt, twice, solved.reshape(pairs * size, LANES))
    shape = (actions, pairs * size)
    same = iota(shape, 1) // SUB == iota(shape, 0)
    flow = by_parts(dot_nt, position, zonal) + by_parts(dot, jnp.where(same, moved, 0.0), diff)
    limit = limit_ref[...]
    loading_ref[...] = flow / limit
    margin_ref[...] = limit - jnp.abs(flow)


def in_hbm(x):
    return pltpu.with_memory_space_constraint(x, pltpu.HBM)


def copied(arrays):
    hbm = pl.BlockSpec(memory_space=pltpu.HBM)
    return pl.pallas_call(
        copy_kernel,
        out_shape=[jax.ShapeDtypeStruct(x.shape, x.dtype) for x in arrays],
        in_specs=[hbm] * len(arrays),
        out_specs=[hbm] * len(arrays),
        scratch_shapes=[pltpu.SemaphoreType.DMA((len(arrays),))],
        name="copies",
    )(*[in_hbm(x) for x in arrays])


def params():
    return pltpu.CompilerParams(vmem_limit_bytes=48 * 1024 * 1024)


def body(
    nodal_sensitivity, shift_weight, bus_zone, branch_buses, switched_rows, net_position, flow_limit
):
    rows, cols = nodal_sensitivity.shape
    zones = net_position.shape[0]
    actions, rank = switched_rows.shape
    picks = actions * rank
    n_z, n_yh = lax.axis_size("z"), lax.axis_size("yh")
    share = rows // n_z // n_yh
    f32, i32 = jnp.float32, jnp.int32
    vmem = pl.BlockSpec(memory_space=pltpu.VMEM)
    hbm = pl.BlockSpec(memory_space=pltpu.HBM)

    weight, zone = [x.reshape(cols // LANES, LANES) for x in (shift_weight, bus_zone)]
    weight, zone = in_hbm(weight), in_hbm(zone)
    bus_scratch = [pltpu.VMEM((cols // LANES, LANES), kind) for kind in (f32, i32)]
    totals = pl.pallas_call(
        total_kernel,
        out_shape=jax.ShapeDtypeStruct((lax.axis_size(BUS), 1, LANES), f32),
        in_specs=[hbm] * 2,
        out_specs=vmem,
        scratch_shapes=[*bus_scratch, pltpu.SemaphoreType.DMA((2,))],
        compiler_params=params(),
        name="totals",
    )(weight, zone)
    totals = lax.all_to_all(totals, BUS, 0, 0, tiled=True)
    sens_scratch = pltpu.VMEM((rows, cols), jnp.bfloat16)
    held, meta, extra = pl.pallas_call(
        column_kernel,
        out_shape=(
            jax.ShapeDtypeStruct((n_z, share, LANES), f32),
            jax.ShapeDtypeStruct((SUB, 2 * picks), f32),
            jax.ShapeDtypeStruct((SLOTS + SUB, LANES), f32),
        ),
        in_specs=[hbm] * 3,
        out_specs=(vmem,) * 3,
        scratch_shapes=[
            pltpu.VMEM((rank, actions), i32),
            pltpu.VMEM(branch_buses.shape, i32),
            sens_scratch,
            pltpu.VMEM((rows, SLOTS), f32),
            pltpu.VMEM((SLOTS, picks), f32),
            pltpu.SemaphoreType.DMA((cols // BLOCK + 2,)),
        ],
        compiler_params=params(),
        name="columns",
    )(*[in_hbm(x) for x in (switched_rows.T, branch_buses, nodal_sensitivity)])
    pay = pl.pallas_call(
        zonal_kernel,
        out_shape=jax.ShapeDtypeStruct((n_z, SUMMED + share, LANES), f32),
        in_specs=[vmem, hbm, hbm, hbm, vmem, vmem],
        out_specs=vmem,
        scratch_shapes=[
            *bus_scratch,
            sens_scratch,
            pltpu.VMEM((zones, cols), jnp.bfloat16),
            pltpu.VMEM((cols // LANES, LANES), f32),
            pltpu.VMEM((rows, zones), f32),
            pltpu.SemaphoreType.DMA((2 * cols // BLOCK + 2,)),
        ],
        compiler_params=params(),
        name="zonal",
    )(totals, weight, zone, in_hbm(nodal_sensitivity), held, extra)

    swap = [(0, 1), (1, 0)]
    parts = lax.all_to_all(pay, "z", 0, 0, tiled=True)
    local = jnp.sum(parts[:, :SUMMED], axis=0)
    part = jax.ShapeDtypeStruct((SUB + 2 * share, LANES), f32)
    mine, theirs = pl.pallas_call(
        place_kernel,
        out_shape=(part, part),
        in_specs=[vmem] * 3,
        out_specs=(vmem, vmem),
        compiler_params=params(),
        name="place",
    )(parts, local, meta)

    block = local[2 * SUB:]
    theirs = lax.ppermute(jnp.concatenate([block, theirs], axis=0), "yh", swap)
    beside = lax.ppermute(block, "yl", swap)
    across = lax.ppermute(block, ("yl", "yh"), [(0, 3), (3, 0), (1, 2), (2, 1)])
    here = jnp.concatenate([block + theirs[:BLOCK_ROWS], beside + across], axis=0)
    n_x = lax.axis_size("x")
    others = [
        lax.ppermute(here, "x", [(at, (at + by) % n_x) for at in range(n_x)])
        for by in range(1, n_x)
    ]
    other = lax.ppermute(
        mine[:SUB] + theirs[BLOCK_ROWS:BLOCK_ROWS + SUB], "act", swap
    )

    def compact():
        outputs = pl.pallas_call(
            final_kernel,
            out_shape=(
                jax.ShapeDtypeStruct((actions, share, zones), f32),
                jax.ShapeDtypeStruct((actions, share), f32),
                jax.ShapeDtypeStruct((actions, share), f32),
            ),
            in_specs=[vmem] * 10,
            out_specs=(vmem, vmem, vmem),
            compiler_params=params(),
            name="update",
        )(
            meta, mine, theirs, other, here, *others,
            net_position.reshape(1, zones), flow_limit.reshape(1, share),
        )
        return tuple(outputs)

    def general():
        inputs = nodal_sensitivity, shift_weight, bus_zone, branch_buses, switched_rows
        return tuple(copied(plain(*copied(inputs), net_position, flow_limit)))

    return lax.cond(meta[2, 0] > 0.5, general, compact)


def sum_over(x, axes):
    spread = jnp.broadcast_to(x[None], (lax.axis_size(axes), *x.shape))
    return jnp.sum(lax.all_to_all(spread, axes, 0, 0, tiled=True), axis=0)


def scattered_sum(x):
    shares = lax.axis_size(BUS)
    x = x.reshape(shares, x.shape[0] // shares, x.shape[1])
    return jnp.sum(lax.all_to_all(x, BUS, 0, 0, tiled=True), axis=0)


def plain(
    nodal_sensitivity, shift_weight, bus_zone, branch_buses, switched_rows, net_position, flow_limit
):
    rows, cols = nodal_sensitivity.shape
    zones = net_position.shape[0]
    actions, rank = switched_rows.shape
    onehot = (bus_zone[:, None] == jnp.arange(zones)[None, :]).astype(jnp.float32)
    total = sum_over(jnp.sum(onehot * shift_weight[:, None], axis=0), BUS)
    key = (onehot * shift_weight[:, None] / total[None, :]).astype(jnp.bfloat16)
    zonal = jnp.dot(nodal_sensitivity, key, preferred_element_type=jnp.float32)
    picks = switched_rows.reshape(-1)

    def columns(buses):
        local = buses - lax.axis_index(BUS) * cols
        owned = (local >= 0) & (local < cols)
        picked = jnp.take(nodal_sensitivity, jnp.clip(local, 0, cols - 1), axis=1)
        return jnp.where(owned[None, :], picked.astype(jnp.float32), 0.0)

    diff = columns(branch_buses[0][picks]) - columns(branch_buses[1][picks])
    zonal, diff = scattered_sum(zonal), scattered_sum(diff)
    share = rows // lax.axis_size(BUS)
    local = picks - lax.axis_index(CNEC) * rows - lax.axis_index(BUS) * share
    owned = ((local >= 0) & (local < share))[:, None]
    local = jnp.clip(local, 0, share - 1)
    switched = jnp.where(owned, jnp.take(zonal, local, axis=0), 0.0)
    coupled = jnp.where(owned, jnp.take(diff, local, axis=0), 0.0)
    coupled = jnp.einsum("aiaj->aij", coupled.reshape(actions, rank, actions, rank))
    both = jnp.concatenate([switched, coupled.reshape(actions * rank, rank)], axis=1)
    both = sum_over(sum_over(both, BUS), CNEC).reshape(actions, rank, zones + rank)
    left, right = jnp.eye(rank, dtype=jnp.float32)[None] - both[:, :, zones:], both[:, :, :zones]
    for pivot in range(rank):
        is_pivot = (jnp.arange(rank) == pivot)[None, :, None]
        factor = left[:, :, pivot:pivot + 1]
        diagonal = factor[:, pivot:pivot + 1]
        left_now, right_now = left[:, pivot:pivot + 1] / diagonal, right[:, pivot:pivot + 1] / diagonal
        left = jnp.where(is_pivot, left_now, left - factor * left_now)
        right = jnp.where(is_pivot, right_now, right - factor * right_now)
    after = zonal[None] + jnp.einsum(
        "caj,ajz->acz", diff.reshape(share, actions, rank), right, precision=HIGHEST
    )
    flow = jnp.einsum("acz,z->ac", after, net_position, precision=HIGHEST)
    return after, flow / flow_limit[None, :], flow_limit[None, :] - jnp.abs(flow)


def solution(mesh):
    n_cnec, n_bus, n_act = mesh.devices.shape
    split = Mesh(
        mesh.devices.reshape(2, n_cnec // 2, n_bus // 2, 2, n_act), ("yl", "x", "z", "yh", "act")
    )
    return jax.shard_map(
        body,
        mesh=split,
        in_specs=(
            P(CNEC, BUS),
            P(BUS),
            P(BUS),
            P(),
            P("act", None),
            P(),
            P(CNEC + BUS),
        ),
        out_specs=(
            P("act", CNEC + BUS, None),
            P("act", CNEC + BUS),
            P("act", CNEC + BUS),
        ),
        check_vma=False,
    )
```

```python
import jax
import jax.numpy as jnp
from jax import lax
from jax.experimental import pallas as pl
from jax.experimental.pallas import tpu as pltpu
from jax.sharding import Mesh
from jax.sharding import PartitionSpec as P

HIGHEST = lax.Precision.HIGHEST
LANES = 128
HALF = 64
SUB = 8
BLOCK = 2048
SLOTS = 64
BLOCK_ROWS = SLOTS // 2 + SUB
SUMMED = 2 * SUB + BLOCK_ROWS
CNEC, BUS = ("yl", "x"), ("z", "yh")


def iota(shape, dim):
    return lax.broadcasted_iota(jnp.int32, shape, dim)


def dot_nt(x, y, precision=None):
    return lax.dot_general(
        x, y, (((1,), (1,)), ((), ())), precision=precision, preferred_element_type=jnp.float32
    )


def dot(x, y, precision=None):
    return jnp.dot(x, y, precision=precision, preferred_element_type=jnp.float32)


def two_parts(values):
    high = values.astype(jnp.bfloat16)
    return high, (values - high.astype(jnp.float32)).astype(jnp.bfloat16)


def by_parts(product, x, y):
    x_high, x_low = two_parts(x)
    y_high, y_low = two_parts(y)
    return product(x_high, y_high) + product(x_high, y_low) + product(x_low, y_high)


def digits(values, base, count):
    return [((values >> (base * at)) & ((1 << base) - 1)).astype(jnp.float32).astype(jnp.bfloat16)
            for at in reversed(range(count))]


def find_picks(swt, branch_ref):
    rank, actions = swt.shape
    picks = rank * actions
    pick_id = iota((picks, actions), 0)
    of_action = pick_id % LANES // rank * 2 + pick_id // LANES == iota((picks, actions), 1)
    of_action = jnp.where(of_action, 1.0, 0.0).astype(jnp.bfloat16)
    high, low = digits(swt, 6, 2)
    row = dot_nt(high, of_action) * 64.0 + dot_nt(low, of_action)
    row = jnp.where(iota((rank, picks), 1) % rank == iota((rank, picks), 0), row, 0.0)
    row = jnp.sum(row, axis=0, keepdims=True).astype(jnp.int32)
    tiles = branch_ref.shape[1] // LANES
    table = jnp.concatenate(
        [branch_ref[:, at * LANES:(at + 1) * LANES] for at in range(tiles)], axis=0
    )
    onehot = jnp.where(iota((LANES, picks), 0) == row % LANES, 1.0, 0.0).astype(jnp.bfloat16)
    high, middle, low = [dot(part, onehot) for part in digits(table, 6, 3)]
    found = high * 4096.0 + middle * 64.0 + low
    line = iota((2 * tiles, picks), 0) - row // LANES * 2
    ends = [
        jnp.sum(jnp.where(line == end, found, 0.0), axis=0, keepdims=True).astype(jnp.int32)
        for end in (0, 1)
    ]
    return row, ends


def slot_matrix(slots, count):
    shape = (count, slots[0].shape[1])
    first, second = [jnp.where(iota(shape, 0) == slot, 1.0, 0.0) for slot in slots]
    return (first - second).astype(jnp.bfloat16)


def total_kernel(weight_hbm, zone_hbm, out_ref, weight_ref, zone_ref, sems):
    copies = [
        pltpu.make_async_copy(weight_hbm, weight_ref, sems.at[0]),
        pltpu.make_async_copy(zone_hbm, zone_ref, sems.at[1]),
    ]
    for copy in copies:
        copy.start()
    for copy in copies:
        copy.wait()
    ids = iota((HALF, LANES), 0)
    total = jnp.zeros((HALF, LANES), jnp.float32)
    for at in range(weight_ref.shape[0]):
        total += jnp.where(zone_ref[at:at + 1, :] == ids, weight_ref[at:at + 1, :], 0.0)
    total = jnp.sum(total, axis=1, keepdims=True)
    eye = ids + HALF == iota((HALF, LANES), 1)
    total = jnp.sum(jnp.where(eye, total, 0.0), axis=0, keepdims=True)
    out_ref[...] = jnp.where(iota(out_ref.shape, 0) == 0, total, 0.0)


def column_kernel(
    swt_hbm, branch_hbm, weight_hbm, zone_hbm, sens_hbm, pay_ref, meta_ref, extra_ref,
    swt_ref, branch_ref, weight_ref, zone_ref, sens_ref, rank_ref, chosen_ref, acc_ref,
    coupled_ref, sems
):
    rows, cols = sens_ref.shape
    rank, actions = swt_ref.shape
    picks = rank * actions
    steps = cols // BLOCK
    bf16 = jnp.bfloat16
    small = [
        pltpu.make_async_copy(source, target, sems.at[steps + at])
        for at, (source, target) in enumerate(
            [(swt_hbm, swt_ref), (branch_hbm, branch_ref), (weight_hbm, weight_ref), (zone_hbm, zone_ref)]
        )
    ]
    for copy in small:
        copy.start()

    def block_copy(step):
        at = pl.ds(pl.multiple_of(step * BLOCK, BLOCK), BLOCK)
        return pltpu.make_async_copy(sens_hbm.at[:, at], sens_ref.at[:, at], sems.at[step])

    for step in range(steps):
        block_copy(step).start()

    shard = lax.axis_index(BUS)
    row_start = lax.axis_index(CNEC) * rows
    acc_ref[...] = jnp.zeros_like(acc_ref)
    for copy in small:
        copy.wait()
    row, ends = find_picks(swt_ref[...], branch_ref)

    def ranks(owner, owners):
        count = owner.shape[1]
        inside = iota((owners, count), 0) == owner
        before = jnp.where(iota((count, count), 0) < iota((count, count), 1), 1.0, 0.0)
        place = dot(jnp.where(inside, 1.0, 0.0).astype(bf16), before.astype(bf16))
        return jnp.sum(jnp.where(inside, place, 0.0), axis=0, keepdims=True)

    bus = jnp.concatenate(ends, axis=1)
    count = 2 * picks
    held, place = bus // cols, ranks(bus // cols, lax.axis_size(BUS))
    owner, row_place = row // rows, ranks(row // rows, lax.axis_size(CNEC))
    most = jnp.maximum(
        jnp.max(place, axis=1, keepdims=True), jnp.max(row_place, axis=1, keepdims=True)
    )
    over = jnp.where(most >= SLOTS, 1.0, 0.0)
    meta_ref[0:1, :] = held.astype(jnp.float32)
    meta_ref[1:2, :] = place
    meta_ref[2:3, :] = jnp.broadcast_to(over, (1, count))
    meta_ref[3:4, :] = jnp.concatenate([owner.astype(jnp.float32), row_place], axis=1)
    meta_ref[4:, :] = jnp.zeros((SUB - 4, count), jnp.float32)
    place = place.astype(jnp.int32)
    mine = held == shard
    slot = jnp.where(mine, place, -1)
    local = bus - shard * cols

    def buses_of(group):
        match = iota((SLOTS, count), 0) + group * SLOTS == slot
        match = jnp.where(match, (local + 1).astype(jnp.float32), 0.0)
        return jnp.sum(match, axis=1, keepdims=True).astype(jnp.int32) - 1

    first_buses = buses_of(0)
    row_slot = jnp.where(owner == lax.axis_index(CNEC), row_place.astype(jnp.int32), -1)
    match = iota((SLOTS, picks), 0) == row_slot
    slot_row = jnp.where(match, (row - row_start + 1).astype(jnp.float32), 0.0)
    slot_row = jnp.sum(slot_row, axis=1, keepdims=True) - 1.0
    action_of = iota((SLOTS, picks), 1) // rank
    slot_action = jnp.where(match, action_of.astype(jnp.float32), 0.0)
    slot_action = jnp.sum(slot_action, axis=1, keepdims=True).astype(jnp.int32)

    weight = weight_ref[...]
    positive = weight > 0.0
    ones = jnp.where(positive, 1.0, 0.0).astype(bf16)
    lines = weight.shape[0]
    before = jnp.where(iota((LANES, LANES), 0) < iota((LANES, LANES), 1), 1.0, 0.0).astype(bf16)
    above = jnp.where(iota((lines, lines), 1) < iota((lines, lines), 0), 1.0, 0.0).astype(bf16)
    place = dot(ones, before) + jnp.sum(dot(above, ones), axis=1, keepdims=True)
    rank_ref[...] = jnp.where(positive, place, -1.0)
    most = jnp.max(jnp.max(rank_ref[...], axis=0, keepdims=True), axis=1, keepdims=True)
    over = over + jnp.where(most >= SLOTS, 1.0, 0.0)
    ids = iota((SLOTS, LANES), 0)
    slot_id = ids.astype(jnp.float32)
    slot_weight = jnp.zeros((SLOTS, LANES), jnp.float32)
    slot_zone = jnp.zeros((SLOTS, LANES), jnp.float32)
    for at in range(lines):
        match = rank_ref[at:at + 1, :] == slot_id
        slot_weight += jnp.where(match, weight_ref[at:at + 1, :], 0.0)
        slot_zone += jnp.where(match, zone_ref[at:at + 1, :].astype(jnp.float32), 0.0)
        chosen_ref[:, at * LANES:(at + 1) * LANES] = jnp.where(match, 1.0, 0.0).astype(bf16)
    eye = ids + HALF == iota((SLOTS, LANES), 1)
    slot_weight, slot_zone = [
        jnp.sum(
            jnp.where(eye, jnp.sum(x, axis=1, keepdims=True), 0.0), axis=0, keepdims=True
        )
        for x in (slot_weight, slot_zone)
    ]
    choose = iota((SLOTS, rows), 1) == slot_row.astype(jnp.int32)
    choose = jnp.where(choose, 1.0, 0.0).astype(bf16)
    lane = iota((SLOTS, BLOCK), 1)

    def select(buses, step):
        return jnp.where(lane == buses - step * BLOCK, 1.0, 0.0).astype(bf16)

    def step_body(step, carry):
        at = pl.ds(pl.multiple_of(step * BLOCK, BLOCK), BLOCK)
        chosen = jnp.concatenate([select(first_buses, step), chosen_ref[:, at]], axis=0)
        block_copy(step).wait()
        acc_ref[...] += dot_nt(sens_ref[:, at], chosen)
        return carry

    lax.fori_loop(0, steps, step_body, 0)

    def coupled_of(columns, group):
        slots = [slot[:, at * picks:(at + 1) * picks] - group * SLOTS for at in (0, 1)]
        chosen = dot(choose, columns.astype(bf16))
        return dot(chosen.astype(bf16), slot_matrix(slots, SLOTS))

    columns = acc_ref[:, 0:SLOTS]
    coupled_ref[...] = coupled_of(columns, 0)

    def group_body(group, carry):
        buses = buses_of(group)
        columns = jnp.zeros((rows, SLOTS), jnp.float32)
        for step in range(steps):
            at = pl.ds(step * BLOCK, BLOCK)
            columns += dot_nt(sens_ref[:, at], select(buses, step))
        coupled_ref[...] += coupled_of(columns, group)
        return carry

    groups = (jnp.sum(jnp.where(mine, 1.0, 0.0)).astype(jnp.int32) + SLOTS - 1) // SLOTS
    lax.fori_loop(1, groups, group_body, 0)

    coupled = jnp.where(action_of == slot_action, coupled_ref[...], 0.0)
    fold = jnp.where(iota((picks, LANES), 0) % rank == iota((picks, LANES), 1) % rank, 1.0, 0.0)
    high, low = [dot(part, fold.astype(bf16)) for part in two_parts(coupled)]
    shape = (SLOTS, LANES)
    coupled = jnp.where(iota(shape, 1) // rank == iota(shape, 0) // SUB, high + low, 0.0)
    coupled = jnp.sum(coupled.reshape(SLOTS // SUB, SUB, LANES), axis=0)
    line = iota(coupled.shape, 0)
    over = jnp.where(iota(coupled.shape, 1) < HALF, 0.0, over)
    for at, values in ((1, slot_weight), (2, slot_zone), (3, over)):
        coupled = coupled + jnp.where(line == at, values, 0.0)
    extra_ref[...] = coupled

    chunks = pay_ref.shape[0]
    weighted = acc_ref[:, SLOTS:]
    share = weighted.reshape(chunks, 2, 2, 2, SUB, SLOTS)
    share = jnp.where(lax.axis_index("act") == 0, share[:, :, 0], share[:, :, 1])
    share = jnp.concatenate([share[:, :, 0], share[:, :, 1]], axis=-1)
    half = SLOTS // 2
    switched = dot(choose, weighted.astype(bf16))
    switched = jnp.concatenate([switched[:half], switched[half:]], axis=1)
    pay_ref[:, 0:2 * SUB, :] = share.reshape(chunks, 2 * SUB, LANES)
    pay_ref[:, 2 * SUB:2 * SUB + half, :] = jnp.broadcast_to(switched[None], (chunks, half, LANES))
    pay_ref[:, 2 * SUB + half:SUMMED, :] = jnp.broadcast_to(coupled[None], (chunks, SUB, LANES))
    columns = columns.reshape(chunks, 2, rows // chunks // 2, SLOTS)
    pay_ref[:, SUMMED:, :] = jnp.concatenate([columns[:, 0], columns[:, 1]], axis=-1)


def place_kernel(parts_ref, meta_ref, mine_ref, send_ref, block_ref):
    chunks = parts_ref.shape[0]
    start = SUMMED - SUB
    extra = jnp.sum(parts_ref[:, start:SUMMED, :], axis=0)
    slot_weight, slot_zone = [
        jnp.concatenate([parts_ref[z, start + at:start + at + 1, :] for z in range(chunks)], axis=0)
        for at in (1, 2)
    ]
    upper = iota(slot_zone.shape, 1) >= HALF
    slot_zone = jnp.where(upper, slot_zone, 0.0)
    of_slot = jnp.take_along_axis(
        jnp.broadcast_to(extra[0:1], slot_zone.shape), slot_zone.astype(jnp.int32) + HALF, axis=1
    )
    key = (jnp.where(upper, slot_weight, 0.0) / of_slot).astype(jnp.bfloat16).astype(jnp.float32)
    key, slot_zone = [
        jnp.concatenate([x[z:z + 1, HALF:] for z in range(chunks)], axis=1)
        for x in (key, slot_zone)
    ]
    zone_id = iota((HALF, chunks * SLOTS), 0).astype(jnp.float32)
    key = jnp.where(slot_zone == zone_id, key, 0.0).astype(jnp.bfloat16)

    def across(first, count, lanes):
        lanes = slice(lanes * SLOTS, (lanes + 1) * SLOTS)
        return jnp.concatenate(
            [parts_ref[z, first:first + count, lanes] for z in range(chunks)], axis=1
        )

    rows = SLOTS // 2
    left = [across(at * SUB, SUB, side) for at in (0, 1) for side in (0, 1)]
    left += [across(2 * SUB, rows, side) for side in (0, 1)]
    zonal = dot_nt(jnp.concatenate(left, axis=0).astype(jnp.bfloat16), key)
    zonal, switched = zonal[0:4 * SUB], zonal[4 * SUB:]
    zonal = [
        jnp.concatenate([zonal[at:at + SUB], zonal[at + SUB:at + 2 * SUB]], axis=1)
        for at in (0, 2 * SUB)
    ]
    block_ref[0:rows, :] = jnp.concatenate([switched[:rows], switched[rows:]], axis=1)
    block_ref[rows:, :] = extra
    send_ref[0:BLOCK_ROWS, :] = block_ref[...]

    picks = meta_ref.shape[1] // 2
    half = parts_ref.shape[1] - SUMMED
    y_here, y_size = lax.axis_index("yh"), lax.axis_size("yh")
    held = meta_ref[0:1, :].astype(jnp.int32)
    place = meta_ref[1:2, :].astype(jnp.int32)
    known = (held % y_size == y_here) & (place < SLOTS)
    slot = jnp.where(known, held // y_size * SLOTS + place, -1)
    spread = slot_matrix([slot[:, at * picks:(at + 1) * picks] for at in (0, 1)], chunks * SLOTS)
    columns = [
        jnp.concatenate(
            [parts_ref[z, SUMMED:, at * SLOTS:(at + 1) * SLOTS] for z in range(chunks)], axis=1
        )
        for at in (0, 1)
    ]
    columns = jnp.concatenate(columns, axis=0).astype(jnp.bfloat16)
    diff = lax.dot_general(
        spread, columns, (((0,), (1,)), ((), ())), preferred_element_type=jnp.float32
    )
    diff = diff.reshape(2, picks // (2 * SUB), SUB, 2 * half)
    diff = jnp.concatenate([diff[0], diff[1]], axis=1).reshape(4, picks // 4, 2 * half)
    lower = y_here == 0
    packed = [
        jnp.concatenate([diff[g, :, at * half:(at + 1) * half] for g in range(4)], axis=1)
        for at in (0, 1)
    ]
    for ref, at, first in ((mine_ref, 0, lower), (send_ref, BLOCK_ROWS, ~lower)):
        ref[at:at + SUB, :] = jnp.where(first, zonal[0], zonal[1])
        ref[at + SUB:, :] = jnp.where(first, packed[0], packed[1])


def copy_kernel(*refs):
    count = len(refs) // 2
    copies = [
        pltpu.make_async_copy(refs[at], refs[count + at], refs[-1].at[at]) for at in range(count)
    ]
    for copy in copies:
        copy.start()
    for copy in copies:
        copy.wait()


def final_kernel(
    meta_ref, mine_ref, theirs_ref, other_ref, here_ref, x1_ref, x2_ref, x3_ref, position_ref,
    limit_ref, after_ref, loading_ref, margin_ref
):
    actions, share, zones = after_ref.shape
    pairs = actions // 2
    picks = actions * SUB
    bf16 = jnp.bfloat16

    size_x = lax.axis_size("x")
    owner = meta_ref[3:4, :picks].astype(jnp.int32)
    slot = meta_ref[3:4, picks:].astype(jnp.int32)
    back = (lax.axis_index("x") - owner % size_x + size_x) % size_x
    flip = jnp.where(owner // size_x == lax.axis_index("yl"), 0, 1)
    blocks = [
        ref[at * BLOCK_ROWS:(at + 1) * BLOCK_ROWS, :]
        for ref in (here_ref, x1_ref, x2_ref, x3_ref)
        for at in (0, 1)
    ]
    count = len(blocks) * SLOTS
    spread = iota((count, picks), 0) == (back * 2 + flip) * SLOTS + slot
    spread = jnp.where(spread, 1.0, 0.0).astype(bf16)
    half = SLOTS // 2
    switched, coupled = [], []
    lane = iota((half, LANES), 1)
    for block in blocks:
        rows = block[0:half]
        turned = pltpu.roll(rows, HALF, 1)
        switched += [jnp.where(lane < HALF, rows, turned), jnp.where(lane < HALF, turned, rows)]
        extra = block[half:]
        for g in range(SLOTS // SUB):
            coupled.append(jnp.where(iota(extra.shape, 1) // SUB == g, extra, 0.0))
    parts = two_parts(jnp.concatenate(switched, axis=0)) + two_parts(jnp.concatenate(coupled, axis=0))
    found = lax.dot_general(
        spread, jnp.concatenate(parts, axis=1), (((0,), (0,)), ((), ())),
        preferred_element_type=jnp.float32,
    )
    switched = found[:, 0:LANES] + found[:, LANES:2 * LANES]
    coupled = found[:, 2 * LANES:3 * LANES] + found[:, 3 * LANES:]
    shape = (LANES, LANES)
    repeat = (iota(shape, 0) < SLOTS) & (iota(shape, 0) % SUB == iota(shape, 1) % SUB)
    repeat = jnp.where(repeat, 1.0, 0.0).astype(bf16)
    high, low = [dot(part, repeat) for part in two_parts(coupled)]
    coupled = high + low

    shape = (pairs, SUB, LANES)
    row_id, lane = iota(shape, 1), iota(shape, 2)

    def side_by_side(x):
        return jnp.where(
            lane < HALF, x[:picks // 2].reshape(shape), x[picks // 2:].reshape(shape)
        )

    left = jnp.where(lane % SUB == row_id, 1.0, 0.0) - side_by_side(coupled)
    right = side_by_side(switched)
    for pivot in range(SUB):
        factor = jnp.where(
            lane < HALF, left[:, :, pivot:pivot + 1], left[:, :, HALF + pivot:HALF + pivot + 1]
        )
        diagonal = factor[:, pivot:pivot + 1]
        left_now = left[:, pivot:pivot + 1] / diagonal
        right_now = right[:, pivot:pivot + 1] / diagonal
        left = jnp.where(row_id == pivot, left_now, left - factor * left_now)
        right = jnp.where(row_id == pivot, right_now, right - factor * right_now)

    lower = lax.axis_index("act") == 0
    whole = mine_ref[...] + theirs_ref[BLOCK_ROWS:]
    mine, other = whole[0:SUB], other_ref[...]
    low, high = jnp.where(lower, mine, other), jnp.where(lower, other, mine)
    zonal = jnp.concatenate(
        [low[:, :HALF], low[:, HALF:], high[:, :HALF], high[:, HALF:]], axis=0
    )
    zonal_twice = jnp.concatenate([zonal, zonal], axis=1)
    groups = [whole[SUB:, g * share:(g + 1) * share] for g in range(LANES // share)]
    diff = jnp.concatenate(groups, axis=0)
    solved = jnp.concatenate(
        [jnp.where(lane < HALF, right, 0.0), jnp.where(lane < HALF, 0.0, right)], axis=1
    )
    diff_high, diff_low = two_parts(diff)
    solved_high, solved_low = two_parts(solved)

    def product(x, y):
        return lax.dot_general(
            x, y, (((0,), (0,)), ((), ())), preferred_element_type=jnp.float32
        )

    size = 2 * SUB
    for pair in range(pairs):
        at = slice(pair * size, (pair + 1) * size)
        left = jnp.concatenate([diff_high[at], diff_high[at], diff_low[at]], axis=0)
        right = jnp.concatenate(
            [solved_high[pair], solved_low[pair], solved_high[pair]], axis=0
        )
        total = zonal_twice + product(left, right)
        after_ref[2 * pair] = total[:, :HALF]
        after_ref[2 * pair + 1] = total[:, HALF:]
    position = position_ref[...]
    twice = jnp.concatenate([position, position], axis=1)
    moved = by_parts(dot_nt, twice, solved.reshape(pairs * size, LANES))
    shape = (actions, pairs * size)
    same = iota(shape, 1) // SUB == iota(shape, 0)
    flow = by_parts(dot_nt, position, zonal) + by_parts(dot, jnp.where(same, moved, 0.0), diff)
    limit = limit_ref[...]
    loading_ref[...] = flow / limit
    margin_ref[...] = limit - jnp.abs(flow)


def in_hbm(x):
    return pltpu.with_memory_space_constraint(x, pltpu.HBM)


def copied(arrays):
    hbm = pl.BlockSpec(memory_space=pltpu.HBM)
    return pl.pallas_call(
        copy_kernel,
        out_shape=[jax.ShapeDtypeStruct(x.shape, x.dtype) for x in arrays],
        in_specs=[hbm] * len(arrays),
        out_specs=[hbm] * len(arrays),
        scratch_shapes=[pltpu.SemaphoreType.DMA((len(arrays),))],
        name="copies",
    )(*[in_hbm(x) for x in arrays])


def params():
    return pltpu.CompilerParams(vmem_limit_bytes=48 * 1024 * 1024)


def body(
    nodal_sensitivity, shift_weight, bus_zone, branch_buses, switched_rows, net_position, flow_limit
):
    rows, cols = nodal_sensitivity.shape
    zones = net_position.shape[0]
    actions, rank = switched_rows.shape
    picks = actions * rank
    n_z, n_yh = lax.axis_size("z"), lax.axis_size("yh")
    share = rows // n_z // n_yh
    f32, i32 = jnp.float32, jnp.int32
    vmem = pl.BlockSpec(memory_space=pltpu.VMEM)
    hbm = pl.BlockSpec(memory_space=pltpu.HBM)

    weight, zone = [x.reshape(cols // LANES, LANES) for x in (shift_weight, bus_zone)]
    weight, zone = in_hbm(weight), in_hbm(zone)
    bus_scratch = [pltpu.VMEM((cols // LANES, LANES), kind) for kind in (f32, i32)]
    totals = pl.pallas_call(
        total_kernel,
        out_shape=jax.ShapeDtypeStruct((SUB, LANES), f32),
        in_specs=[hbm] * 2,
        out_specs=vmem,
        scratch_shapes=[*bus_scratch, pltpu.SemaphoreType.DMA((2,))],
        compiler_params=params(),
        name="totals",
    )(weight, zone)
    swap = [(0, 1), (1, 0)]
    turn = [(0, 3), (3, 0), (1, 2), (2, 1)]
    totals = totals + lax.ppermute(totals, ("yl", "yh"), turn)
    pay, meta, extra = pl.pallas_call(
        column_kernel,
        out_shape=(
            jax.ShapeDtypeStruct((n_z, SUMMED + share, LANES), f32),
            jax.ShapeDtypeStruct((SUB, 2 * picks), f32),
            jax.ShapeDtypeStruct((SUB, LANES), f32),
        ),
        in_specs=[hbm] * 5,
        out_specs=(vmem,) * 3,
        scratch_shapes=[
            pltpu.VMEM((rank, actions), i32),
            pltpu.VMEM(branch_buses.shape, i32),
            *bus_scratch,
            pltpu.VMEM((rows, cols), jnp.bfloat16),
            pltpu.VMEM((cols // LANES, LANES), f32),
            pltpu.VMEM((SLOTS, cols), jnp.bfloat16),
            pltpu.VMEM((rows, 2 * SLOTS), f32),
            pltpu.VMEM((SLOTS, picks), f32),
            pltpu.SemaphoreType.DMA((cols // BLOCK + 4,)),
        ],
        compiler_params=params(),
        name="columns",
    )(
        in_hbm(switched_rows.T), in_hbm(branch_buses), weight, zone, in_hbm(nodal_sensitivity)
    )
    extra = jnp.broadcast_to((extra + totals)[None], (n_z, SUB, LANES))
    pay = lax.dynamic_update_slice(pay, extra, (0, SUMMED - SUB, 0))
    parts = lax.all_to_all(pay, "z", 0, 0, tiled=True)
    mine, send, block = pl.pallas_call(
        place_kernel,
        out_shape=[
            jax.ShapeDtypeStruct((count, LANES), f32)
            for count in (SUB + 2 * share, BLOCK_ROWS + SUB + 2 * share, BLOCK_ROWS)
        ],
        in_specs=[vmem] * 2,
        out_specs=[vmem] * 3,
        compiler_params=params(),
        name="place",
    )(parts, meta)

    theirs = lax.ppermute(send, "yh", swap)
    beside = lax.ppermute(block, "yl", swap)
    across = lax.ppermute(block, ("yl", "yh"), turn)
    here = jnp.concatenate([block + theirs[:BLOCK_ROWS], beside + across], axis=0)
    n_x = lax.axis_size("x")
    others = [
        lax.ppermute(here, "x", [(at, (at + by) % n_x) for at in range(n_x)])
        for by in range(1, n_x)
    ]
    other = lax.ppermute(
        mine[:SUB] + theirs[BLOCK_ROWS:BLOCK_ROWS + SUB], "act", swap
    )

    def compact():
        outputs = pl.pallas_call(
            final_kernel,
            out_shape=(
                jax.ShapeDtypeStruct((actions, share, zones), f32),
                jax.ShapeDtypeStruct((actions, share), f32),
                jax.ShapeDtypeStruct((actions, share), f32),
            ),
            in_specs=[vmem] * 10,
            out_specs=(vmem, vmem, vmem),
            compiler_params=params(),
            name="update",
        )(
            meta, mine, theirs, other, here, *others,
            net_position.reshape(1, zones), flow_limit.reshape(1, share),
        )
        return tuple(outputs)

    def general():
        inputs = nodal_sensitivity, shift_weight, bus_zone, branch_buses, switched_rows
        return tuple(copied(plain(*copied(inputs), net_position, flow_limit)))

    return lax.cond(here[SLOTS // 2 + 3, HALF] > 0.5, general, compact)


def sum_over(x, axes):
    spread = jnp.broadcast_to(x[None], (lax.axis_size(axes), *x.shape))
    return jnp.sum(lax.all_to_all(spread, axes, 0, 0, tiled=True), axis=0)


def scattered_sum(x):
    shares = lax.axis_size(BUS)
    x = x.reshape(shares, x.shape[0] // shares, x.shape[1])
    return jnp.sum(lax.all_to_all(x, BUS, 0, 0, tiled=True), axis=0)


def plain(
    nodal_sensitivity, shift_weight, bus_zone, branch_buses, switched_rows, net_position, flow_limit
):
    rows, cols = nodal_sensitivity.shape
    zones = net_position.shape[0]
    actions, rank = switched_rows.shape
    onehot = (bus_zone[:, None] == jnp.arange(zones)[None, :]).astype(jnp.float32)
    total = sum_over(jnp.sum(onehot * shift_weight[:, None], axis=0), BUS)
    key = (onehot * shift_weight[:, None] / total[None, :]).astype(jnp.bfloat16)
    zonal = jnp.dot(nodal_sensitivity, key, preferred_element_type=jnp.float32)
    picks = switched_rows.reshape(-1)

    def columns(buses):
        local = buses - lax.axis_index(BUS) * cols
        owned = (local >= 0) & (local < cols)
        picked = jnp.take(nodal_sensitivity, jnp.clip(local, 0, cols - 1), axis=1)
        return jnp.where(owned[None, :], picked.astype(jnp.float32), 0.0)

    diff = columns(branch_buses[0][picks]) - columns(branch_buses[1][picks])
    zonal, diff = scattered_sum(zonal), scattered_sum(diff)
    share = rows // lax.axis_size(BUS)
    local = picks - lax.axis_index(CNEC) * rows - lax.axis_index(BUS) * share
    owned = ((local >= 0) & (local < share))[:, None]
    local = jnp.clip(local, 0, share - 1)
    switched = jnp.where(owned, jnp.take(zonal, local, axis=0), 0.0)
    coupled = jnp.where(owned, jnp.take(diff, local, axis=0), 0.0)
    coupled = jnp.einsum("aiaj->aij", coupled.reshape(actions, rank, actions, rank))
    both = jnp.concatenate([switched, coupled.reshape(actions * rank, rank)], axis=1)
    both = sum_over(sum_over(both, BUS), CNEC).reshape(actions, rank, zones + rank)
    left, right = jnp.eye(rank, dtype=jnp.float32)[None] - both[:, :, zones:], both[:, :, :zones]
    for pivot in range(rank):
        is_pivot = (jnp.arange(rank) == pivot)[None, :, None]
        factor = left[:, :, pivot:pivot + 1]
        diagonal = factor[:, pivot:pivot + 1]
        left_now, right_now = left[:, pivot:pivot + 1] / diagonal, right[:, pivot:pivot + 1] / diagonal
        left = jnp.where(is_pivot, left_now, left - factor * left_now)
        right = jnp.where(is_pivot, right_now, right - factor * right_now)
    after = zonal[None] + jnp.einsum(
        "caj,ajz->acz", diff.reshape(share, actions, rank), right, precision=HIGHEST
    )
    flow = jnp.einsum("acz,z->ac", after, net_position, precision=HIGHEST)
    return after, flow / flow_limit[None, :], flow_limit[None, :] - jnp.abs(flow)


def solution(mesh):
    n_cnec, n_bus, n_act = mesh.devices.shape
    split = Mesh(
        mesh.devices.reshape(2, n_cnec // 2, n_bus // 2, 2, n_act), ("yl", "x", "z", "yh", "act")
    )
    return jax.shard_map(
        body,
        mesh=split,
        in_specs=(
            P(CNEC, BUS),
            P(BUS),
            P(BUS),
            P(),
            P("act", None),
            P(),
            P(CNEC + BUS),
        ),
        out_specs=(
            P("act", CNEC + BUS, None),
            P("act", CNEC + BUS),
            P("act", CNEC + BUS),
        ),
        check_vma=False,
    )
```

```python
import jax
import jax.numpy as jnp
from jax import lax
from jax.experimental import pallas as pl
from jax.experimental.pallas import tpu as pltpu
from jax.sharding import Mesh
from jax.sharding import PartitionSpec as P

HIGHEST = lax.Precision.HIGHEST
LANES = 128
HALF = 64
SUB = 8
BLOCK = 2048
SLOTS = 64
BLOCK_ROWS = SLOTS // 2 + SUB
SUMMED = 2 * SUB + BLOCK_ROWS
CNEC, BUS = ("yl", "x"), ("z", "yh")


def iota(shape, dim):
    return lax.broadcasted_iota(jnp.int32, shape, dim)


def dot_nt(x, y, precision=None):
    return lax.dot_general(
        x, y, (((1,), (1,)), ((), ())), precision=precision, preferred_element_type=jnp.float32
    )


def dot(x, y, precision=None):
    return jnp.dot(x, y, precision=precision, preferred_element_type=jnp.float32)


def two_parts(values):
    high = values.astype(jnp.bfloat16)
    return high, (values - high.astype(jnp.float32)).astype(jnp.bfloat16)


def by_parts(product, x, y):
    x_high, x_low = two_parts(x)
    y_high, y_low = two_parts(y)
    return product(x_high, y_high) + product(x_high, y_low) + product(x_low, y_high)


def digits(values, base, count):
    return [((values >> (base * at)) & ((1 << base) - 1)).astype(jnp.float32).astype(jnp.bfloat16)
            for at in reversed(range(count))]


def find_picks(swt, branch_ref):
    rank, actions = swt.shape
    picks = rank * actions
    pick_id = iota((picks, actions), 0)
    of_action = pick_id % LANES // rank * 2 + pick_id // LANES == iota((picks, actions), 1)
    of_action = jnp.where(of_action, 1.0, 0.0).astype(jnp.bfloat16)
    high, low = digits(swt, 6, 2)
    row = dot_nt(high, of_action) * 64.0 + dot_nt(low, of_action)
    row = jnp.where(iota((rank, picks), 1) % rank == iota((rank, picks), 0), row, 0.0)
    row = jnp.sum(row, axis=0, keepdims=True).astype(jnp.int32)
    tiles = branch_ref.shape[1] // LANES
    table = jnp.concatenate(
        [branch_ref[:, at * LANES:(at + 1) * LANES] for at in range(tiles)], axis=0
    )
    onehot = jnp.where(iota((LANES, picks), 0) == row % LANES, 1.0, 0.0).astype(jnp.bfloat16)
    high, middle, low = [dot(part, onehot) for part in digits(table, 6, 3)]
    found = high * 4096.0 + middle * 64.0 + low
    line = iota((2 * tiles, picks), 0) - row // LANES * 2
    ends = [
        jnp.sum(jnp.where(line == end, found, 0.0), axis=0, keepdims=True).astype(jnp.int32)
        for end in (0, 1)
    ]
    return row, ends


def slot_matrix(slots, count):
    shape = (count, slots[0].shape[1])
    first, second = [jnp.where(iota(shape, 0) == slot, 1.0, 0.0) for slot in slots]
    return (first - second).astype(jnp.bfloat16)


def total_kernel(weight_hbm, zone_hbm, out_ref, weight_ref, zone_ref, sems):
    copies = [
        pltpu.make_async_copy(weight_hbm, weight_ref, sems.at[0]),
        pltpu.make_async_copy(zone_hbm, zone_ref, sems.at[1]),
    ]
    for copy in copies:
        copy.start()
    for copy in copies:
        copy.wait()
    ids = iota((HALF, LANES), 0)
    total = jnp.zeros((HALF, LANES), jnp.float32)
    for at in range(weight_ref.shape[0]):
        total += jnp.where(zone_ref[at:at + 1, :] == ids, weight_ref[at:at + 1, :], 0.0)
    total = jnp.sum(total, axis=1, keepdims=True)
    eye = ids + HALF == iota((HALF, LANES), 1)
    total = jnp.sum(jnp.where(eye, total, 0.0), axis=0, keepdims=True)
    out_ref[...] = jnp.where(iota(out_ref.shape, 0) == 0, total, 0.0)


def column_kernel(
    swt_hbm, branch_hbm, weight_hbm, zone_hbm, sens_hbm, pay_ref, meta_ref, extra_ref,
    swt_ref, branch_ref, weight_ref, zone_ref, sens_ref, rank_ref, acc_ref,
    coupled_ref, sems
):
    rows, cols = sens_ref.shape
    rank, actions = swt_ref.shape
    picks = rank * actions
    steps = cols // BLOCK
    bf16 = jnp.bfloat16
    small = [
        pltpu.make_async_copy(source, target, sems.at[steps + at])
        for at, (source, target) in enumerate(
            [(swt_hbm, swt_ref), (branch_hbm, branch_ref), (weight_hbm, weight_ref), (zone_hbm, zone_ref)]
        )
    ]
    for copy in small:
        copy.start()

    def block_copy(step):
        at = pl.ds(pl.multiple_of(step * BLOCK, BLOCK), BLOCK)
        return pltpu.make_async_copy(sens_hbm.at[:, at], sens_ref.at[:, at], sems.at[step])

    for step in range(steps):
        block_copy(step).start()

    shard = lax.axis_index(BUS)
    row_start = lax.axis_index(CNEC) * rows
    acc_ref[...] = jnp.zeros_like(acc_ref)
    for copy in small:
        copy.wait()
    row, ends = find_picks(swt_ref[...], branch_ref)

    def ranks(owner, owners):
        count = owner.shape[1]
        inside = iota((owners, count), 0) == owner
        before = jnp.where(iota((count, count), 0) < iota((count, count), 1), 1.0, 0.0)
        place = dot(jnp.where(inside, 1.0, 0.0).astype(bf16), before.astype(bf16))
        return jnp.sum(jnp.where(inside, place, 0.0), axis=0, keepdims=True)

    bus = jnp.concatenate(ends, axis=1)
    count = 2 * picks
    held, place = bus // cols, ranks(bus // cols, lax.axis_size(BUS))
    owner, row_place = row // rows, ranks(row // rows, lax.axis_size(CNEC))
    most = jnp.maximum(
        jnp.max(place, axis=1, keepdims=True), jnp.max(row_place, axis=1, keepdims=True)
    )
    over = jnp.where(most >= SLOTS, 1.0, 0.0)
    meta_ref[0:1, :] = held.astype(jnp.float32)
    meta_ref[1:2, :] = place
    meta_ref[2:3, :] = jnp.broadcast_to(over, (1, count))
    meta_ref[3:4, :] = jnp.concatenate([owner.astype(jnp.float32), row_place], axis=1)
    meta_ref[4:, :] = jnp.zeros((SUB - 4, count), jnp.float32)
    place = place.astype(jnp.int32)
    mine = held == shard
    slot = jnp.where(mine, place, -1)
    local = bus - shard * cols

    def buses_of(group):
        match = iota((SLOTS, count), 0) + group * SLOTS == slot
        match = jnp.where(match, (local + 1).astype(jnp.float32), 0.0)
        return jnp.sum(match, axis=1, keepdims=True).astype(jnp.int32) - 1

    first_buses = buses_of(0)
    row_slot = jnp.where(owner == lax.axis_index(CNEC), row_place.astype(jnp.int32), -1)
    match = iota((SLOTS, picks), 0) == row_slot
    slot_row = jnp.where(match, (row - row_start + 1).astype(jnp.float32), 0.0)
    slot_row = jnp.sum(slot_row, axis=1, keepdims=True) - 1.0
    action_of = iota((SLOTS, picks), 1) // rank
    slot_action = jnp.where(match, action_of.astype(jnp.float32), 0.0)
    slot_action = jnp.sum(slot_action, axis=1, keepdims=True).astype(jnp.int32)

    weight = weight_ref[...]
    positive = weight > 0.0
    ones = jnp.where(positive, 1.0, 0.0).astype(bf16)
    lines = weight.shape[0]
    before = jnp.where(iota((LANES, LANES), 0) < iota((LANES, LANES), 1), 1.0, 0.0).astype(bf16)
    above = jnp.where(iota((lines, lines), 1) < iota((lines, lines), 0), 1.0, 0.0).astype(bf16)
    place = dot(ones, before) + jnp.sum(dot(above, ones), axis=1, keepdims=True)
    rank_ref[...] = jnp.where(positive, place, -1.0)
    most = jnp.max(jnp.max(rank_ref[...], axis=0, keepdims=True), axis=1, keepdims=True)
    over = over + jnp.where(most >= SLOTS, 1.0, 0.0)
    ids = iota((SLOTS, LANES), 0)
    slot_id = ids.astype(jnp.float32)
    choose = iota((SLOTS, rows), 1) == slot_row.astype(jnp.int32)
    choose = jnp.where(choose, 1.0, 0.0).astype(bf16)
    lane = iota((SLOTS, BLOCK), 1)

    def select(buses, step):
        return jnp.where(lane == buses - step * BLOCK, 1.0, 0.0).astype(bf16)

    def step_body(step, sums):
        at = pl.ds(pl.multiple_of(step * BLOCK, BLOCK), BLOCK)
        slot_weight, slot_zone = sums
        chosen = []
        for part in range(BLOCK // LANES):
            line = pl.ds(step * (BLOCK // LANES) + part, 1)
            match = rank_ref[line, :] == slot_id
            slot_weight += jnp.where(match, weight_ref[line, :], 0.0)
            slot_zone += jnp.where(match, zone_ref[line, :].astype(jnp.float32), 0.0)
            chosen.append(jnp.where(match, 1.0, 0.0).astype(bf16))
        chosen = jnp.concatenate(chosen, axis=1)
        chosen = jnp.concatenate([select(first_buses, step), chosen], axis=0)
        block_copy(step).wait()
        acc_ref[...] += dot_nt(sens_ref[:, at], chosen)
        return slot_weight, slot_zone

    zeros = jnp.zeros((SLOTS, LANES), jnp.float32)
    slot_weight, slot_zone = lax.fori_loop(0, steps, step_body, (zeros, zeros))
    eye = ids + HALF == iota((SLOTS, LANES), 1)
    slot_weight, slot_zone = [
        jnp.sum(
            jnp.where(eye, jnp.sum(x, axis=1, keepdims=True), 0.0), axis=0, keepdims=True
        )
        for x in (slot_weight, slot_zone)
    ]

    def coupled_of(columns, group):
        slots = [slot[:, at * picks:(at + 1) * picks] - group * SLOTS for at in (0, 1)]
        chosen = dot(choose, columns.astype(bf16))
        return dot(chosen.astype(bf16), slot_matrix(slots, SLOTS))

    columns = acc_ref[:, 0:SLOTS]
    coupled_ref[...] = coupled_of(columns, 0)

    def group_body(group, carry):
        buses = buses_of(group)
        columns = jnp.zeros((rows, SLOTS), jnp.float32)
        for step in range(steps):
            at = pl.ds(step * BLOCK, BLOCK)
            columns += dot_nt(sens_ref[:, at], select(buses, step))
        coupled_ref[...] += coupled_of(columns, group)
        return carry

    groups = (jnp.sum(jnp.where(mine, 1.0, 0.0)).astype(jnp.int32) + SLOTS - 1) // SLOTS
    lax.fori_loop(1, groups, group_body, 0)

    coupled = jnp.where(action_of == slot_action, coupled_ref[...], 0.0)
    fold = jnp.where(iota((picks, LANES), 0) % rank == iota((picks, LANES), 1) % rank, 1.0, 0.0)
    high, low = [dot(part, fold.astype(bf16)) for part in two_parts(coupled)]
    shape = (SLOTS, LANES)
    coupled = jnp.where(iota(shape, 1) // rank == iota(shape, 0) // SUB, high + low, 0.0)
    coupled = jnp.sum(coupled.reshape(SLOTS // SUB, SUB, LANES), axis=0)
    line = iota(coupled.shape, 0)
    over = jnp.where(iota(coupled.shape, 1) < HALF, 0.0, over)
    for at, values in ((1, slot_weight), (2, slot_zone), (3, over)):
        coupled = coupled + jnp.where(line == at, values, 0.0)
    extra_ref[...] = coupled

    chunks = pay_ref.shape[0]
    weighted = acc_ref[:, SLOTS:]
    share = weighted.reshape(chunks, 2, 2, 2, SUB, SLOTS)
    share = jnp.where(lax.axis_index("act") == 0, share[:, :, 0], share[:, :, 1])
    share = jnp.concatenate([share[:, :, 0], share[:, :, 1]], axis=-1)
    half = SLOTS // 2
    switched = dot(choose, weighted.astype(bf16))
    switched = jnp.concatenate([switched[:half], switched[half:]], axis=1)
    pay_ref[:, 0:2 * SUB, :] = share.reshape(chunks, 2 * SUB, LANES)
    pay_ref[:, 2 * SUB:2 * SUB + half, :] = jnp.broadcast_to(switched[None], (chunks, half, LANES))
    pay_ref[:, 2 * SUB + half:SUMMED, :] = jnp.broadcast_to(coupled[None], (chunks, SUB, LANES))
    columns = columns.reshape(chunks, 2, rows // chunks // 2, SLOTS)
    pay_ref[:, SUMMED:, :] = jnp.concatenate([columns[:, 0], columns[:, 1]], axis=-1)


def place_kernel(parts_ref, meta_ref, mine_ref, send_ref, block_ref):
    chunks = parts_ref.shape[0]
    start = SUMMED - SUB
    extra = jnp.sum(parts_ref[:, start:SUMMED, :], axis=0)
    slot_weight, slot_zone = [
        jnp.concatenate([parts_ref[z, start + at:start + at + 1, :] for z in range(chunks)], axis=0)
        for at in (1, 2)
    ]
    upper = iota(slot_zone.shape, 1) >= HALF
    slot_zone = jnp.where(upper, slot_zone, 0.0)
    of_slot = jnp.take_along_axis(
        jnp.broadcast_to(extra[0:1], slot_zone.shape), slot_zone.astype(jnp.int32) + HALF, axis=1
    )
    key = (jnp.where(upper, slot_weight, 0.0) / of_slot).astype(jnp.bfloat16).astype(jnp.float32)
    key, slot_zone = [
        jnp.concatenate([x[z:z + 1, HALF:] for z in range(chunks)], axis=1)
        for x in (key, slot_zone)
    ]
    zone_id = iota((HALF, chunks * SLOTS), 0).astype(jnp.float32)
    key = jnp.where(slot_zone == zone_id, key, 0.0).astype(jnp.bfloat16)

    def across(first, count, lanes):
        lanes = slice(lanes * SLOTS, (lanes + 1) * SLOTS)
        return jnp.concatenate(
            [parts_ref[z, first:first + count, lanes] for z in range(chunks)], axis=1
        )

    rows = SLOTS // 2
    left = [across(at * SUB, SUB, side) for at in (0, 1) for side in (0, 1)]
    left += [across(2 * SUB, rows, side) for side in (0, 1)]
    zonal = dot_nt(jnp.concatenate(left, axis=0).astype(jnp.bfloat16), key)
    zonal, switched = zonal[0:4 * SUB], zonal[4 * SUB:]
    zonal = [
        jnp.concatenate([zonal[at:at + SUB], zonal[at + SUB:at + 2 * SUB]], axis=1)
        for at in (0, 2 * SUB)
    ]
    block_ref[0:rows, :] = jnp.concatenate([switched[:rows], switched[rows:]], axis=1)
    block_ref[rows:, :] = extra
    send_ref[0:BLOCK_ROWS, :] = block_ref[...]

    picks = meta_ref.shape[1] // 2
    half = parts_ref.shape[1] - SUMMED
    y_here, y_size = lax.axis_index("yh"), lax.axis_size("yh")
    held = meta_ref[0:1, :].astype(jnp.int32)
    place = meta_ref[1:2, :].astype(jnp.int32)
    known = (held % y_size == y_here) & (place < SLOTS)
    slot = jnp.where(known, held // y_size * SLOTS + place, -1)
    spread = slot_matrix([slot[:, at * picks:(at + 1) * picks] for at in (0, 1)], chunks * SLOTS)
    columns = [
        jnp.concatenate(
            [parts_ref[z, SUMMED:, at * SLOTS:(at + 1) * SLOTS] for z in range(chunks)], axis=1
        )
        for at in (0, 1)
    ]
    columns = jnp.concatenate(columns, axis=0).astype(jnp.bfloat16)
    diff = lax.dot_general(
        spread, columns, (((0,), (1,)), ((), ())), preferred_element_type=jnp.float32
    )
    diff = diff.reshape(2, picks // (2 * SUB), SUB, 2 * half)
    diff = jnp.concatenate([diff[0], diff[1]], axis=1).reshape(4, picks // 4, 2 * half)
    lower = y_here == 0
    packed = [
        jnp.concatenate([diff[g, :, at * half:(at + 1) * half] for g in range(4)], axis=1)
        for at in (0, 1)
    ]
    for ref, at, first in ((mine_ref, 0, lower), (send_ref, BLOCK_ROWS, ~lower)):
        ref[at:at + SUB, :] = jnp.where(first, zonal[0], zonal[1])
        ref[at + SUB:, :] = jnp.where(first, packed[0], packed[1])


def copy_kernel(*refs):
    count = len(refs) // 2
    copies = [
        pltpu.make_async_copy(refs[at], refs[count + at], refs[-1].at[at]) for at in range(count)
    ]
    for copy in copies:
        copy.start()
    for copy in copies:
        copy.wait()


def final_kernel(
    meta_ref, mine_ref, theirs_ref, other_ref, here_ref, x1_ref, x2_ref, x3_ref, position_ref,
    limit_ref, after_ref, loading_ref, margin_ref
):
    actions, share, zones = after_ref.shape
    pairs = actions // 2
    picks = actions * SUB
    bf16 = jnp.bfloat16

    size_x = lax.axis_size("x")
    owner = meta_ref[3:4, :picks].astype(jnp.int32)
    slot = meta_ref[3:4, picks:].astype(jnp.int32)
    back = (lax.axis_index("x") - owner % size_x + size_x) % size_x
    flip = jnp.where(owner // size_x == lax.axis_index("yl"), 0, 1)
    blocks = [
        ref[at * BLOCK_ROWS:(at + 1) * BLOCK_ROWS, :]
        for ref in (here_ref, x1_ref, x2_ref, x3_ref)
        for at in (0, 1)
    ]
    count = len(blocks) * SLOTS
    spread = iota((count, picks), 0) == (back * 2 + flip) * SLOTS + slot
    spread = jnp.where(spread, 1.0, 0.0).astype(bf16)
    half = SLOTS // 2
    switched, coupled = [], []
    lane = iota((half, LANES), 1)
    for block in blocks:
        rows = block[0:half]
        turned = pltpu.roll(rows, HALF, 1)
        switched += [jnp.where(lane < HALF, rows, turned), jnp.where(lane < HALF, turned, rows)]
        extra = block[half:]
        for g in range(SLOTS // SUB):
            coupled.append(jnp.where(iota(extra.shape, 1) // SUB == g, extra, 0.0))
    parts = two_parts(jnp.concatenate(switched, axis=0)) + two_parts(jnp.concatenate(coupled, axis=0))
    found = lax.dot_general(
        spread, jnp.concatenate(parts, axis=1), (((0,), (0,)), ((), ())),
        preferred_element_type=jnp.float32,
    )
    switched = found[:, 0:LANES] + found[:, LANES:2 * LANES]
    coupled = found[:, 2 * LANES:3 * LANES] + found[:, 3 * LANES:]
    shape = (LANES, LANES)
    repeat = (iota(shape, 0) < SLOTS) & (iota(shape, 0) % SUB == iota(shape, 1) % SUB)
    repeat = jnp.where(repeat, 1.0, 0.0).astype(bf16)
    high, low = [dot(part, repeat) for part in two_parts(coupled)]
    coupled = high + low

    shape = (pairs, SUB, LANES)
    row_id, lane = iota(shape, 1), iota(shape, 2)

    def side_by_side(x):
        return jnp.where(
            lane < HALF, x[:picks // 2].reshape(shape), x[picks // 2:].reshape(shape)
        )

    left = jnp.where(lane % SUB == row_id, 1.0, 0.0) - side_by_side(coupled)
    right = side_by_side(switched)
    for pivot in range(SUB):
        factor = jnp.where(
            lane < HALF, left[:, :, pivot:pivot + 1], left[:, :, HALF + pivot:HALF + pivot + 1]
        )
        diagonal = factor[:, pivot:pivot + 1]
        left_now = left[:, pivot:pivot + 1] / diagonal
        right_now = right[:, pivot:pivot + 1] / diagonal
        left = jnp.where(row_id == pivot, left_now, left - factor * left_now)
        right = jnp.where(row_id == pivot, right_now, right - factor * right_now)

    lower = lax.axis_index("act") == 0
    whole = mine_ref[...] + theirs_ref[BLOCK_ROWS:]
    mine, other = whole[0:SUB], other_ref[...]
    low, high = jnp.where(lower, mine, other), jnp.where(lower, other, mine)
    zonal = jnp.concatenate(
        [low[:, :HALF], low[:, HALF:], high[:, :HALF], high[:, HALF:]], axis=0
    )
    zonal_twice = jnp.concatenate([zonal, zonal], axis=1)
    groups = [whole[SUB:, g * share:(g + 1) * share] for g in range(LANES // share)]
    diff = jnp.concatenate(groups, axis=0)
    solved = jnp.concatenate(
        [jnp.where(lane < HALF, right, 0.0), jnp.where(lane < HALF, 0.0, right)], axis=1
    )
    diff_high, diff_low = two_parts(diff)
    solved_high, solved_low = two_parts(solved)

    def product(x, y):
        return lax.dot_general(
            x, y, (((0,), (0,)), ((), ())), preferred_element_type=jnp.float32
        )

    size = 2 * SUB
    for pair in range(pairs):
        at = slice(pair * size, (pair + 1) * size)
        left = jnp.concatenate([diff_high[at], diff_high[at], diff_low[at]], axis=0)
        right = jnp.concatenate(
            [solved_high[pair], solved_low[pair], solved_high[pair]], axis=0
        )
        total = zonal_twice + product(left, right)
        after_ref[2 * pair] = total[:, :HALF]
        after_ref[2 * pair + 1] = total[:, HALF:]
    position = position_ref[...]
    twice = jnp.concatenate([position, position], axis=1)
    moved = by_parts(dot_nt, twice, solved.reshape(pairs * size, LANES))
    shape = (actions, pairs * size)
    same = iota(shape, 1) // SUB == iota(shape, 0)
    flow = by_parts(dot_nt, position, zonal) + by_parts(dot, jnp.where(same, moved, 0.0), diff)
    limit = limit_ref[...]
    loading_ref[...] = flow / limit
    margin_ref[...] = limit - jnp.abs(flow)


def in_hbm(x):
    return pltpu.with_memory_space_constraint(x, pltpu.HBM)


def copied(arrays):
    hbm = pl.BlockSpec(memory_space=pltpu.HBM)
    return pl.pallas_call(
        copy_kernel,
        out_shape=[jax.ShapeDtypeStruct(x.shape, x.dtype) for x in arrays],
        in_specs=[hbm] * len(arrays),
        out_specs=[hbm] * len(arrays),
        scratch_shapes=[pltpu.SemaphoreType.DMA((len(arrays),))],
        name="copies",
    )(*[in_hbm(x) for x in arrays])


def params():
    return pltpu.CompilerParams(vmem_limit_bytes=48 * 1024 * 1024)


def body(
    nodal_sensitivity, shift_weight, bus_zone, branch_buses, switched_rows, net_position, flow_limit
):
    rows, cols = nodal_sensitivity.shape
    zones = net_position.shape[0]
    actions, rank = switched_rows.shape
    picks = actions * rank
    n_z, n_yh = lax.axis_size("z"), lax.axis_size("yh")
    share = rows // n_z // n_yh
    f32, i32 = jnp.float32, jnp.int32
    vmem = pl.BlockSpec(memory_space=pltpu.VMEM)
    hbm = pl.BlockSpec(memory_space=pltpu.HBM)

    weight, zone = [x.reshape(cols // LANES, LANES) for x in (shift_weight, bus_zone)]
    weight, zone = in_hbm(weight), in_hbm(zone)
    bus_scratch = [pltpu.VMEM((cols // LANES, LANES), kind) for kind in (f32, i32)]
    totals = pl.pallas_call(
        total_kernel,
        out_shape=jax.ShapeDtypeStruct((SUB, LANES), f32),
        in_specs=[hbm] * 2,
        out_specs=vmem,
        scratch_shapes=[*bus_scratch, pltpu.SemaphoreType.DMA((2,))],
        compiler_params=params(),
        name="totals",
    )(weight, zone)
    swap = [(0, 1), (1, 0)]
    turn = [(0, 3), (3, 0), (1, 2), (2, 1)]
    totals = totals + lax.ppermute(totals, ("yl", "yh"), turn)
    pay, meta, extra = pl.pallas_call(
        column_kernel,
        out_shape=(
            jax.ShapeDtypeStruct((n_z, SUMMED + share, LANES), f32),
            jax.ShapeDtypeStruct((SUB, 2 * picks), f32),
            jax.ShapeDtypeStruct((SUB, LANES), f32),
        ),
        in_specs=[hbm] * 5,
        out_specs=(vmem,) * 3,
        scratch_shapes=[
            pltpu.VMEM((rank, actions), i32),
            pltpu.VMEM(branch_buses.shape, i32),
            *bus_scratch,
            pltpu.VMEM((rows, cols), jnp.bfloat16),
            pltpu.VMEM((cols // LANES, LANES), f32),
            pltpu.VMEM((rows, 2 * SLOTS), f32),
            pltpu.VMEM((SLOTS, picks), f32),
            pltpu.SemaphoreType.DMA((cols // BLOCK + 4,)),
        ],
        compiler_params=params(),
        name="columns",
    )(
        in_hbm(switched_rows.T), in_hbm(branch_buses), weight, zone, in_hbm(nodal_sensitivity)
    )
    extra = jnp.broadcast_to((extra + totals)[None], (n_z, SUB, LANES))
    pay = lax.dynamic_update_slice(pay, extra, (0, SUMMED - SUB, 0))
    parts = lax.all_to_all(pay, "z", 0, 0, tiled=True)
    mine, send, block = pl.pallas_call(
        place_kernel,
        out_shape=[
            jax.ShapeDtypeStruct((count, LANES), f32)
            for count in (SUB + 2 * share, BLOCK_ROWS + SUB + 2 * share, BLOCK_ROWS)
        ],
        in_specs=[vmem] * 2,
        out_specs=[vmem] * 3,
        compiler_params=params(),
        name="place",
    )(parts, meta)

    theirs = lax.ppermute(send, "yh", swap)
    beside = lax.ppermute(block, "yl", swap)
    across = lax.ppermute(block, ("yl", "yh"), turn)
    here = jnp.concatenate([block + theirs[:BLOCK_ROWS], beside + across], axis=0)
    n_x = lax.axis_size("x")
    others = [
        lax.ppermute(here, "x", [(at, (at + by) % n_x) for at in range(n_x)])
        for by in range(1, n_x)
    ]
    other = lax.ppermute(
        mine[:SUB] + theirs[BLOCK_ROWS:BLOCK_ROWS + SUB], "act", swap
    )

    def compact():
        outputs = pl.pallas_call(
            final_kernel,
            out_shape=(
                jax.ShapeDtypeStruct((actions, share, zones), f32),
                jax.ShapeDtypeStruct((actions, share), f32),
                jax.ShapeDtypeStruct((actions, share), f32),
            ),
            in_specs=[vmem] * 10,
            out_specs=(vmem, vmem, vmem),
            compiler_params=params(),
            name="update",
        )(
            meta, mine, theirs, other, here, *others,
            net_position.reshape(1, zones), flow_limit.reshape(1, share),
        )
        return tuple(outputs)

    def general():
        inputs = nodal_sensitivity, shift_weight, bus_zone, branch_buses, switched_rows
        return tuple(copied(plain(*copied(inputs), net_position, flow_limit)))

    return lax.cond(here[SLOTS // 2 + 3, HALF] > 0.5, general, compact)


def sum_over(x, axes):
    spread = jnp.broadcast_to(x[None], (lax.axis_size(axes), *x.shape))
    return jnp.sum(lax.all_to_all(spread, axes, 0, 0, tiled=True), axis=0)


def scattered_sum(x):
    shares = lax.axis_size(BUS)
    x = x.reshape(shares, x.shape[0] // shares, x.shape[1])
    return jnp.sum(lax.all_to_all(x, BUS, 0, 0, tiled=True), axis=0)


def plain(
    nodal_sensitivity, shift_weight, bus_zone, branch_buses, switched_rows, net_position, flow_limit
):
    rows, cols = nodal_sensitivity.shape
    zones = net_position.shape[0]
    actions, rank = switched_rows.shape
    onehot = (bus_zone[:, None] == jnp.arange(zones)[None, :]).astype(jnp.float32)
    total = sum_over(jnp.sum(onehot * shift_weight[:, None], axis=0), BUS)
    key = (onehot * shift_weight[:, None] / total[None, :]).astype(jnp.bfloat16)
    zonal = jnp.dot(nodal_sensitivity, key, preferred_element_type=jnp.float32)
    picks = switched_rows.reshape(-1)

    def columns(buses):
        local = buses - lax.axis_index(BUS) * cols
        owned = (local >= 0) & (local < cols)
        picked = jnp.take(nodal_sensitivity, jnp.clip(local, 0, cols - 1), axis=1)
        return jnp.where(owned[None, :], picked.astype(jnp.float32), 0.0)

    diff = columns(branch_buses[0][picks]) - columns(branch_buses[1][picks])
    zonal, diff = scattered_sum(zonal), scattered_sum(diff)
    share = rows // lax.axis_size(BUS)
    local = picks - lax.axis_index(CNEC) * rows - lax.axis_index(BUS) * share
    owned = ((local >= 0) & (local < share))[:, None]
    local = jnp.clip(local, 0, share - 1)
    switched = jnp.where(owned, jnp.take(zonal, local, axis=0), 0.0)
    coupled = jnp.where(owned, jnp.take(diff, local, axis=0), 0.0)
    coupled = jnp.einsum("aiaj->aij", coupled.reshape(actions, rank, actions, rank))
    both = jnp.concatenate([switched, coupled.reshape(actions * rank, rank)], axis=1)
    both = sum_over(sum_over(both, BUS), CNEC).reshape(actions, rank, zones + rank)
    left, right = jnp.eye(rank, dtype=jnp.float32)[None] - both[:, :, zones:], both[:, :, :zones]
    for pivot in range(rank):
        is_pivot = (jnp.arange(rank) == pivot)[None, :, None]
        factor = left[:, :, pivot:pivot + 1]
        diagonal = factor[:, pivot:pivot + 1]
        left_now, right_now = left[:, pivot:pivot + 1] / diagonal, right[:, pivot:pivot + 1] / diagonal
        left = jnp.where(is_pivot, left_now, left - factor * left_now)
        right = jnp.where(is_pivot, right_now, right - factor * right_now)
    after = zonal[None] + jnp.einsum(
        "caj,ajz->acz", diff.reshape(share, actions, rank), right, precision=HIGHEST
    )
    flow = jnp.einsum("acz,z->ac", after, net_position, precision=HIGHEST)
    return after, flow / flow_limit[None, :], flow_limit[None, :] - jnp.abs(flow)


def solution(mesh):
    n_cnec, n_bus, n_act = mesh.devices.shape
    split = Mesh(
        mesh.devices.reshape(2, n_cnec // 2, n_bus // 2, 2, n_act), ("yl", "x", "z", "yh", "act")
    )
    return jax.shard_map(
        body,
        mesh=split,
        in_specs=(
            P(CNEC, BUS),
            P(BUS),
            P(BUS),
            P(),
            P("act", None),
            P(),
            P(CNEC + BUS),
        ),
        out_specs=(
            P("act", CNEC + BUS, None),
            P("act", CNEC + BUS),
            P("act", CNEC + BUS),
        ),
        check_vma=False,
    )
```

```python
import jax
import jax.numpy as jnp
from jax import lax
from jax.experimental import pallas as pl
from jax.experimental.pallas import tpu as pltpu
from jax.sharding import Mesh
from jax.sharding import PartitionSpec as P

HIGHEST = lax.Precision.HIGHEST
LANES = 128
HALF = 64
SUB = 8
BLOCK = 1024
SLOTS = 64
BLOCK_ROWS = SLOTS // 2 + SUB
SUMMED = 2 * SUB + BLOCK_ROWS
CNEC, BUS = ("yl", "x"), ("z", "yh")


def iota(shape, dim):
    return lax.broadcasted_iota(jnp.int32, shape, dim)


def dot_nt(x, y, precision=None):
    return lax.dot_general(
        x, y, (((1,), (1,)), ((), ())), precision=precision, preferred_element_type=jnp.float32
    )


def dot(x, y, precision=None):
    return jnp.dot(x, y, precision=precision, preferred_element_type=jnp.float32)


def two_parts(values):
    high = values.astype(jnp.bfloat16)
    return high, (values - high.astype(jnp.float32)).astype(jnp.bfloat16)


def by_parts(product, x, y):
    x_high, x_low = two_parts(x)
    y_high, y_low = two_parts(y)
    return product(x_high, y_high) + product(x_high, y_low) + product(x_low, y_high)


def digits(values, base, count):
    return [((values >> (base * at)) & ((1 << base) - 1)).astype(jnp.float32).astype(jnp.bfloat16)
            for at in reversed(range(count))]


def find_picks(swt, branch_ref):
    rank, actions = swt.shape
    picks = rank * actions
    pick_id = iota((picks, actions), 0)
    of_action = pick_id % LANES // rank * 2 + pick_id // LANES == iota((picks, actions), 1)
    of_action = jnp.where(of_action, 1.0, 0.0).astype(jnp.bfloat16)
    high, low = digits(swt, 6, 2)
    row = dot_nt(high, of_action) * 64.0 + dot_nt(low, of_action)
    row = jnp.where(iota((rank, picks), 1) % rank == iota((rank, picks), 0), row, 0.0)
    row = jnp.sum(row, axis=0, keepdims=True).astype(jnp.int32)
    tiles = branch_ref.shape[1] // LANES
    table = jnp.concatenate(
        [branch_ref[:, at * LANES:(at + 1) * LANES] for at in range(tiles)], axis=0
    )
    onehot = jnp.where(iota((LANES, picks), 0) == row % LANES, 1.0, 0.0).astype(jnp.bfloat16)
    high, middle, low = [dot(part, onehot) for part in digits(table, 6, 3)]
    found = high * 4096.0 + middle * 64.0 + low
    line = iota((2 * tiles, picks), 0) - row // LANES * 2
    ends = [
        jnp.sum(jnp.where(line == end, found, 0.0), axis=0, keepdims=True).astype(jnp.int32)
        for end in (0, 1)
    ]
    return row, ends


def slot_matrix(slots, count):
    shape = (count, slots[0].shape[1])
    first, second = [jnp.where(iota(shape, 0) == slot, 1.0, 0.0) for slot in slots]
    return (first - second).astype(jnp.bfloat16)


def total_kernel(weight_hbm, zone_hbm, out_ref, weight_ref, zone_ref, sems):
    copies = [
        pltpu.make_async_copy(weight_hbm, weight_ref, sems.at[0]),
        pltpu.make_async_copy(zone_hbm, zone_ref, sems.at[1]),
    ]
    for copy in copies:
        copy.start()
    for copy in copies:
        copy.wait()
    ids = iota((HALF, LANES), 0)
    total = jnp.zeros((HALF, LANES), jnp.float32)
    for at in range(weight_ref.shape[0]):
        total += jnp.where(zone_ref[at:at + 1, :] == ids, weight_ref[at:at + 1, :], 0.0)
    total = jnp.sum(total, axis=1, keepdims=True)
    eye = ids + HALF == iota((HALF, LANES), 1)
    total = jnp.sum(jnp.where(eye, total, 0.0), axis=0, keepdims=True)
    out_ref[...] = jnp.where(iota(out_ref.shape, 0) == 0, total, 0.0)


def column_kernel(
    swt_hbm, branch_hbm, weight_hbm, zone_hbm, sens_hbm, pay_ref, meta_ref, extra_ref,
    swt_ref, branch_ref, weight_ref, zone_ref, sens_ref, rank_ref, acc_ref,
    coupled_ref, sems
):
    rows, cols = sens_ref.shape
    rank, actions = swt_ref.shape
    picks = rank * actions
    steps = cols // BLOCK
    bf16 = jnp.bfloat16
    small = [
        pltpu.make_async_copy(source, target, sems.at[steps + at])
        for at, (source, target) in enumerate(
            [(swt_hbm, swt_ref), (branch_hbm, branch_ref), (weight_hbm, weight_ref), (zone_hbm, zone_ref)]
        )
    ]
    for copy in small:
        copy.start()

    def block_copy(step):
        at = pl.ds(pl.multiple_of(step * BLOCK, BLOCK), BLOCK)
        return pltpu.make_async_copy(sens_hbm.at[:, at], sens_ref.at[:, at], sems.at[step])

    for step in range(steps):
        block_copy(step).start()

    shard = lax.axis_index(BUS)
    row_start = lax.axis_index(CNEC) * rows
    acc_ref[...] = jnp.zeros_like(acc_ref)
    for copy in small:
        copy.wait()
    row, ends = find_picks(swt_ref[...], branch_ref)

    def ranks(owner, owners):
        count = owner.shape[1]
        inside = iota((owners, count), 0) == owner
        before = jnp.where(iota((count, count), 0) < iota((count, count), 1), 1.0, 0.0)
        place = dot(jnp.where(inside, 1.0, 0.0).astype(bf16), before.astype(bf16))
        return jnp.sum(jnp.where(inside, place, 0.0), axis=0, keepdims=True)

    bus = jnp.concatenate(ends, axis=1)
    count = 2 * picks
    held, place = bus // cols, ranks(bus // cols, lax.axis_size(BUS))
    owner, row_place = row // rows, ranks(row // rows, lax.axis_size(CNEC))
    most = jnp.maximum(
        jnp.max(place, axis=1, keepdims=True), jnp.max(row_place, axis=1, keepdims=True)
    )
    over = jnp.where(most >= SLOTS, 1.0, 0.0)
    meta_ref[0:1, :] = held.astype(jnp.float32)
    meta_ref[1:2, :] = place
    meta_ref[2:3, :] = jnp.broadcast_to(over, (1, count))
    meta_ref[3:4, :] = jnp.concatenate([owner.astype(jnp.float32), row_place], axis=1)
    meta_ref[4:, :] = jnp.zeros((SUB - 4, count), jnp.float32)
    place = place.astype(jnp.int32)
    mine = held == shard
    slot = jnp.where(mine, place, -1)
    local = bus - shard * cols

    def buses_of(group):
        match = iota((SLOTS, count), 0) + group * SLOTS == slot
        match = jnp.where(match, (local + 1).astype(jnp.float32), 0.0)
        return jnp.sum(match, axis=1, keepdims=True).astype(jnp.int32) - 1

    first_buses = buses_of(0)
    row_slot = jnp.where(owner == lax.axis_index(CNEC), row_place.astype(jnp.int32), -1)
    match = iota((SLOTS, picks), 0) == row_slot
    slot_row = jnp.where(match, (row - row_start + 1).astype(jnp.float32), 0.0)
    slot_row = jnp.sum(slot_row, axis=1, keepdims=True) - 1.0
    action_of = iota((SLOTS, picks), 1) // rank
    slot_action = jnp.where(match, action_of.astype(jnp.float32), 0.0)
    slot_action = jnp.sum(slot_action, axis=1, keepdims=True).astype(jnp.int32)

    weight = weight_ref[...]
    positive = weight > 0.0
    ones = jnp.where(positive, 1.0, 0.0).astype(bf16)
    lines = weight.shape[0]
    before = jnp.where(iota((LANES, LANES), 0) < iota((LANES, LANES), 1), 1.0, 0.0).astype(bf16)
    above = jnp.where(iota((lines, lines), 1) < iota((lines, lines), 0), 1.0, 0.0).astype(bf16)
    place = dot(ones, before) + jnp.sum(dot(above, ones), axis=1, keepdims=True)
    rank_ref[...] = jnp.where(positive, place, -1.0)
    most = jnp.max(jnp.max(rank_ref[...], axis=0, keepdims=True), axis=1, keepdims=True)
    over = over + jnp.where(most >= SLOTS, 1.0, 0.0)
    ids = iota((SLOTS, LANES), 0)
    slot_id = ids.astype(jnp.float32)
    choose = iota((SLOTS, rows), 1) == slot_row.astype(jnp.int32)
    choose = jnp.where(choose, 1.0, 0.0).astype(bf16)
    lane = iota((SLOTS, BLOCK), 1)

    def select(buses, step):
        return jnp.where(lane == buses - step * BLOCK, 1.0, 0.0).astype(bf16)

    def step_body(step, sums):
        at = pl.ds(pl.multiple_of(step * BLOCK, BLOCK), BLOCK)
        slot_weight, slot_zone = sums
        chosen = []
        for part in range(BLOCK // LANES):
            line = pl.ds(step * (BLOCK // LANES) + part, 1)
            match = rank_ref[line, :] == slot_id
            slot_weight += jnp.where(match, weight_ref[line, :], 0.0)
            slot_zone += jnp.where(match, zone_ref[line, :].astype(jnp.float32), 0.0)
            chosen.append(jnp.where(match, 1.0, 0.0).astype(bf16))
        chosen = jnp.concatenate(chosen, axis=1)
        chosen = jnp.concatenate([select(first_buses, step), chosen], axis=0)
        block_copy(step).wait()
        acc_ref[...] += dot_nt(sens_ref[:, at], chosen)
        return slot_weight, slot_zone

    zeros = jnp.zeros((SLOTS, LANES), jnp.float32)
    slot_weight, slot_zone = lax.fori_loop(0, steps, step_body, (zeros, zeros))
    eye = ids + HALF == iota((SLOTS, LANES), 1)
    slot_weight, slot_zone = [
        jnp.sum(
            jnp.where(eye, jnp.sum(x, axis=1, keepdims=True), 0.0), axis=0, keepdims=True
        )
        for x in (slot_weight, slot_zone)
    ]

    def coupled_of(columns, group):
        slots = [slot[:, at * picks:(at + 1) * picks] - group * SLOTS for at in (0, 1)]
        chosen = dot(choose, columns.astype(bf16))
        return dot(chosen.astype(bf16), slot_matrix(slots, SLOTS))

    columns = acc_ref[:, 0:SLOTS]
    coupled_ref[...] = coupled_of(columns, 0)

    def group_body(group, carry):
        buses = buses_of(group)
        columns = jnp.zeros((rows, SLOTS), jnp.float32)
        for step in range(steps):
            at = pl.ds(step * BLOCK, BLOCK)
            columns += dot_nt(sens_ref[:, at], select(buses, step))
        coupled_ref[...] += coupled_of(columns, group)
        return carry

    groups = (jnp.sum(jnp.where(mine, 1.0, 0.0)).astype(jnp.int32) + SLOTS - 1) // SLOTS
    lax.fori_loop(1, groups, group_body, 0)

    coupled = jnp.where(action_of == slot_action, coupled_ref[...], 0.0)
    fold = jnp.where(iota((picks, LANES), 0) % rank == iota((picks, LANES), 1) % rank, 1.0, 0.0)
    high, low = [dot(part, fold.astype(bf16)) for part in two_parts(coupled)]
    shape = (SLOTS, LANES)
    coupled = jnp.where(iota(shape, 1) // rank == iota(shape, 0) // SUB, high + low, 0.0)
    coupled = jnp.sum(coupled.reshape(SLOTS // SUB, SUB, LANES), axis=0)
    line = iota(coupled.shape, 0)
    over = jnp.where(iota(coupled.shape, 1) < HALF, 0.0, over)
    for at, values in ((1, slot_weight), (2, slot_zone), (3, over)):
        coupled = coupled + jnp.where(line == at, values, 0.0)
    extra_ref[...] = coupled

    chunks = pay_ref.shape[0]
    weighted = acc_ref[:, SLOTS:]
    share = weighted.reshape(chunks, 2, 2, 2, SUB, SLOTS)
    share = jnp.where(lax.axis_index("act") == 0, share[:, :, 0], share[:, :, 1])
    share = jnp.concatenate([share[:, :, 0], share[:, :, 1]], axis=-1)
    half = SLOTS // 2
    switched = dot(choose, weighted.astype(bf16))
    switched = jnp.concatenate([switched[:half], switched[half:]], axis=1)
    pay_ref[:, 0:2 * SUB, :] = share.reshape(chunks, 2 * SUB, LANES)
    pay_ref[:, 2 * SUB:2 * SUB + half, :] = jnp.broadcast_to(switched[None], (chunks, half, LANES))
    pay_ref[:, 2 * SUB + half:SUMMED, :] = jnp.broadcast_to(coupled[None], (chunks, SUB, LANES))
    columns = columns.reshape(chunks, 2, rows // chunks // 2, SLOTS)
    pay_ref[:, SUMMED:, :] = jnp.concatenate([columns[:, 0], columns[:, 1]], axis=-1)


def place_kernel(parts_ref, meta_ref, mine_ref, send_ref, block_ref):
    chunks = parts_ref.shape[0]
    start = SUMMED - SUB
    extra = jnp.sum(parts_ref[:, start:SUMMED, :], axis=0)
    slot_weight, slot_zone = [
        jnp.concatenate([parts_ref[z, start + at:start + at + 1, :] for z in range(chunks)], axis=0)
        for at in (1, 2)
    ]
    upper = iota(slot_zone.shape, 1) >= HALF
    slot_zone = jnp.where(upper, slot_zone, 0.0)
    of_slot = jnp.take_along_axis(
        jnp.broadcast_to(extra[0:1], slot_zone.shape), slot_zone.astype(jnp.int32) + HALF, axis=1
    )
    key = (jnp.where(upper, slot_weight, 0.0) / of_slot).astype(jnp.bfloat16).astype(jnp.float32)
    key, slot_zone = [
        jnp.concatenate([x[z:z + 1, HALF:] for z in range(chunks)], axis=1)
        for x in (key, slot_zone)
    ]
    zone_id = iota((HALF, chunks * SLOTS), 0).astype(jnp.float32)
    key = jnp.where(slot_zone == zone_id, key, 0.0).astype(jnp.bfloat16)

    def across(first, count, lanes):
        lanes = slice(lanes * SLOTS, (lanes + 1) * SLOTS)
        return jnp.concatenate(
            [parts_ref[z, first:first + count, lanes] for z in range(chunks)], axis=1
        )

    rows = SLOTS // 2
    left = [across(at * SUB, SUB, side) for at in (0, 1) for side in (0, 1)]
    left += [across(2 * SUB, rows, side) for side in (0, 1)]
    zonal = dot_nt(jnp.concatenate(left, axis=0).astype(jnp.bfloat16), key)
    zonal, switched = zonal[0:4 * SUB], zonal[4 * SUB:]
    zonal = [
        jnp.concatenate([zonal[at:at + SUB], zonal[at + SUB:at + 2 * SUB]], axis=1)
        for at in (0, 2 * SUB)
    ]
    block_ref[0:rows, :] = jnp.concatenate([switched[:rows], switched[rows:]], axis=1)
    block_ref[rows:, :] = extra
    send_ref[0:BLOCK_ROWS, :] = block_ref[...]

    picks = meta_ref.shape[1] // 2
    half = parts_ref.shape[1] - SUMMED
    y_here, y_size = lax.axis_index("yh"), lax.axis_size("yh")
    held = meta_ref[0:1, :].astype(jnp.int32)
    place = meta_ref[1:2, :].astype(jnp.int32)
    known = (held % y_size == y_here) & (place < SLOTS)
    slot = jnp.where(known, held // y_size * SLOTS + place, -1)
    spread = slot_matrix([slot[:, at * picks:(at + 1) * picks] for at in (0, 1)], chunks * SLOTS)
    columns = [
        jnp.concatenate(
            [parts_ref[z, SUMMED:, at * SLOTS:(at + 1) * SLOTS] for z in range(chunks)], axis=1
        )
        for at in (0, 1)
    ]
    columns = jnp.concatenate(columns, axis=0).astype(jnp.bfloat16)
    diff = lax.dot_general(
        spread, columns, (((0,), (1,)), ((), ())), preferred_element_type=jnp.float32
    )
    diff = diff.reshape(2, picks // (2 * SUB), SUB, 2 * half)
    diff = jnp.concatenate([diff[0], diff[1]], axis=1).reshape(4, picks // 4, 2 * half)
    lower = y_here == 0
    packed = [
        jnp.concatenate([diff[g, :, at * half:(at + 1) * half] for g in range(4)], axis=1)
        for at in (0, 1)
    ]
    for ref, at, first in ((mine_ref, 0, lower), (send_ref, BLOCK_ROWS, ~lower)):
        ref[at:at + SUB, :] = jnp.where(first, zonal[0], zonal[1])
        ref[at + SUB:, :] = jnp.where(first, packed[0], packed[1])


def copy_kernel(*refs):
    count = len(refs) // 2
    copies = [
        pltpu.make_async_copy(refs[at], refs[count + at], refs[-1].at[at]) for at in range(count)
    ]
    for copy in copies:
        copy.start()
    for copy in copies:
        copy.wait()


def final_kernel(
    meta_ref, mine_ref, theirs_ref, other_ref, here_ref, x1_ref, x2_ref, x3_ref, position_ref,
    limit_ref, after_ref, loading_ref, margin_ref
):
    actions, share, zones = after_ref.shape
    pairs = actions // 2
    picks = actions * SUB
    bf16 = jnp.bfloat16

    size_x = lax.axis_size("x")
    owner = meta_ref[3:4, :picks].astype(jnp.int32)
    slot = meta_ref[3:4, picks:].astype(jnp.int32)
    back = (lax.axis_index("x") - owner % size_x + size_x) % size_x
    flip = jnp.where(owner // size_x == lax.axis_index("yl"), 0, 1)
    blocks = [
        ref[at * BLOCK_ROWS:(at + 1) * BLOCK_ROWS, :]
        for ref in (here_ref, x1_ref, x2_ref, x3_ref)
        for at in (0, 1)
    ]
    count = len(blocks) * SLOTS
    spread = iota((count, picks), 0) == (back * 2 + flip) * SLOTS + slot
    spread = jnp.where(spread, 1.0, 0.0).astype(bf16)
    half = SLOTS // 2
    switched, coupled = [], []
    lane = iota((half, LANES), 1)
    for block in blocks:
        rows = block[0:half]
        turned = pltpu.roll(rows, HALF, 1)
        switched += [jnp.where(lane < HALF, rows, turned), jnp.where(lane < HALF, turned, rows)]
        extra = block[half:]
        for g in range(SLOTS // SUB):
            coupled.append(jnp.where(iota(extra.shape, 1) // SUB == g, extra, 0.0))
    parts = two_parts(jnp.concatenate(switched, axis=0)) + two_parts(jnp.concatenate(coupled, axis=0))
    found = lax.dot_general(
        spread, jnp.concatenate(parts, axis=1), (((0,), (0,)), ((), ())),
        preferred_element_type=jnp.float32,
    )
    switched = found[:, 0:LANES] + found[:, LANES:2 * LANES]
    coupled = found[:, 2 * LANES:3 * LANES] + found[:, 3 * LANES:]
    shape = (LANES, LANES)
    repeat = (iota(shape, 0) < SLOTS) & (iota(shape, 0) % SUB == iota(shape, 1) % SUB)
    repeat = jnp.where(repeat, 1.0, 0.0).astype(bf16)
    high, low = [dot(part, repeat) for part in two_parts(coupled)]
    coupled = high + low

    shape = (pairs, SUB, LANES)
    row_id, lane = iota(shape, 1), iota(shape, 2)

    def side_by_side(x):
        return jnp.where(
            lane < HALF, x[:picks // 2].reshape(shape), x[picks // 2:].reshape(shape)
        )

    left = jnp.where(lane % SUB == row_id, 1.0, 0.0) - side_by_side(coupled)
    right = side_by_side(switched)
    for pivot in range(SUB):
        factor = jnp.where(
            lane < HALF, left[:, :, pivot:pivot + 1], left[:, :, HALF + pivot:HALF + pivot + 1]
        )
        diagonal = factor[:, pivot:pivot + 1]
        left_now = left[:, pivot:pivot + 1] / diagonal
        right_now = right[:, pivot:pivot + 1] / diagonal
        left = jnp.where(row_id == pivot, left_now, left - factor * left_now)
        right = jnp.where(row_id == pivot, right_now, right - factor * right_now)

    lower = lax.axis_index("act") == 0
    whole = mine_ref[...] + theirs_ref[BLOCK_ROWS:]
    mine, other = whole[0:SUB], other_ref[...]
    low, high = jnp.where(lower, mine, other), jnp.where(lower, other, mine)
    zonal = jnp.concatenate(
        [low[:, :HALF], low[:, HALF:], high[:, :HALF], high[:, HALF:]], axis=0
    )
    zonal_twice = jnp.concatenate([zonal, zonal], axis=1)
    groups = [whole[SUB:, g * share:(g + 1) * share] for g in range(LANES // share)]
    diff = jnp.concatenate(groups, axis=0)
    solved = jnp.concatenate(
        [jnp.where(lane < HALF, right, 0.0), jnp.where(lane < HALF, 0.0, right)], axis=1
    )
    diff_high, diff_low = two_parts(diff)
    solved_high, solved_low = two_parts(solved)

    def product(x, y):
        return lax.dot_general(
            x, y, (((0,), (0,)), ((), ())), preferred_element_type=jnp.float32
        )

    size = 2 * SUB
    for pair in range(pairs):
        at = slice(pair * size, (pair + 1) * size)
        left = jnp.concatenate([diff_high[at], diff_high[at], diff_low[at]], axis=0)
        right = jnp.concatenate(
            [solved_high[pair], solved_low[pair], solved_high[pair]], axis=0
        )
        total = zonal_twice + product(left, right)
        after_ref[2 * pair] = total[:, :HALF]
        after_ref[2 * pair + 1] = total[:, HALF:]
    position = position_ref[...]
    twice = jnp.concatenate([position, position], axis=1)
    moved = by_parts(dot_nt, twice, solved.reshape(pairs * size, LANES))
    shape = (actions, pairs * size)
    same = iota(shape, 1) // SUB == iota(shape, 0)
    flow = by_parts(dot_nt, position, zonal) + by_parts(dot, jnp.where(same, moved, 0.0), diff)
    limit = limit_ref[...]
    loading_ref[...] = flow / limit
    margin_ref[...] = limit - jnp.abs(flow)


def in_hbm(x):
    return pltpu.with_memory_space_constraint(x, pltpu.HBM)


def copied(arrays):
    hbm = pl.BlockSpec(memory_space=pltpu.HBM)
    return pl.pallas_call(
        copy_kernel,
        out_shape=[jax.ShapeDtypeStruct(x.shape, x.dtype) for x in arrays],
        in_specs=[hbm] * len(arrays),
        out_specs=[hbm] * len(arrays),
        scratch_shapes=[pltpu.SemaphoreType.DMA((len(arrays),))],
        name="copies",
    )(*[in_hbm(x) for x in arrays])


def params():
    return pltpu.CompilerParams(vmem_limit_bytes=48 * 1024 * 1024)


def body(
    nodal_sensitivity, shift_weight, bus_zone, branch_buses, switched_rows, net_position, flow_limit
):
    rows, cols = nodal_sensitivity.shape
    zones = net_position.shape[0]
    actions, rank = switched_rows.shape
    picks = actions * rank
    n_z, n_yh = lax.axis_size("z"), lax.axis_size("yh")
    share = rows // n_z // n_yh
    f32, i32 = jnp.float32, jnp.int32
    vmem = pl.BlockSpec(memory_space=pltpu.VMEM)
    hbm = pl.BlockSpec(memory_space=pltpu.HBM)

    weight, zone = [x.reshape(cols // LANES, LANES) for x in (shift_weight, bus_zone)]
    weight, zone = in_hbm(weight), in_hbm(zone)
    bus_scratch = [pltpu.VMEM((cols // LANES, LANES), kind) for kind in (f32, i32)]
    totals = pl.pallas_call(
        total_kernel,
        out_shape=jax.ShapeDtypeStruct((SUB, LANES), f32),
        in_specs=[hbm] * 2,
        out_specs=vmem,
        scratch_shapes=[*bus_scratch, pltpu.SemaphoreType.DMA((2,))],
        compiler_params=params(),
        name="totals",
    )(weight, zone)
    swap = [(0, 1), (1, 0)]
    turn = [(0, 3), (3, 0), (1, 2), (2, 1)]
    totals = totals + lax.ppermute(totals, ("yl", "yh"), turn)
    pay, meta, extra = pl.pallas_call(
        column_kernel,
        out_shape=(
            jax.ShapeDtypeStruct((n_z, SUMMED + share, LANES), f32),
            jax.ShapeDtypeStruct((SUB, 2 * picks), f32),
            jax.ShapeDtypeStruct((SUB, LANES), f32),
        ),
        in_specs=[hbm] * 5,
        out_specs=(vmem,) * 3,
        scratch_shapes=[
            pltpu.VMEM((rank, actions), i32),
            pltpu.VMEM(branch_buses.shape, i32),
            *bus_scratch,
            pltpu.VMEM((rows, cols), jnp.bfloat16),
            pltpu.VMEM((cols // LANES, LANES), f32),
            pltpu.VMEM((rows, 2 * SLOTS), f32),
            pltpu.VMEM((SLOTS, picks), f32),
            pltpu.SemaphoreType.DMA((cols // BLOCK + 4,)),
        ],
        compiler_params=params(),
        name="columns",
    )(
        in_hbm(switched_rows.T), in_hbm(branch_buses), weight, zone, in_hbm(nodal_sensitivity)
    )
    extra = jnp.broadcast_to((extra + totals)[None], (n_z, SUB, LANES))
    pay = lax.dynamic_update_slice(pay, extra, (0, SUMMED - SUB, 0))
    parts = lax.all_to_all(pay, "z", 0, 0, tiled=True)
    mine, send, block = pl.pallas_call(
        place_kernel,
        out_shape=[
            jax.ShapeDtypeStruct((count, LANES), f32)
            for count in (SUB + 2 * share, BLOCK_ROWS + SUB + 2 * share, BLOCK_ROWS)
        ],
        in_specs=[vmem] * 2,
        out_specs=[vmem] * 3,
        compiler_params=params(),
        name="place",
    )(parts, meta)

    theirs = lax.ppermute(send, "yh", swap)
    beside = lax.ppermute(block, "yl", swap)
    across = lax.ppermute(block, ("yl", "yh"), turn)
    here = jnp.concatenate([block + theirs[:BLOCK_ROWS], beside + across], axis=0)
    n_x = lax.axis_size("x")
    others = [
        lax.ppermute(here, "x", [(at, (at + by) % n_x) for at in range(n_x)])
        for by in range(1, n_x)
    ]
    other = lax.ppermute(
        mine[:SUB] + theirs[BLOCK_ROWS:BLOCK_ROWS + SUB], "act", swap
    )

    def compact():
        outputs = pl.pallas_call(
            final_kernel,
            out_shape=(
                jax.ShapeDtypeStruct((actions, share, zones), f32),
                jax.ShapeDtypeStruct((actions, share), f32),
                jax.ShapeDtypeStruct((actions, share), f32),
            ),
            in_specs=[vmem] * 10,
            out_specs=(vmem, vmem, vmem),
            compiler_params=params(),
            name="update",
        )(
            meta, mine, theirs, other, here, *others,
            net_position.reshape(1, zones), flow_limit.reshape(1, share),
        )
        return tuple(outputs)

    def general():
        inputs = nodal_sensitivity, shift_weight, bus_zone, branch_buses, switched_rows
        return tuple(copied(plain(*copied(inputs), net_position, flow_limit)))

    return lax.cond(here[SLOTS // 2 + 3, HALF] > 0.5, general, compact)


def sum_over(x, axes):
    spread = jnp.broadcast_to(x[None], (lax.axis_size(axes), *x.shape))
    return jnp.sum(lax.all_to_all(spread, axes, 0, 0, tiled=True), axis=0)


def scattered_sum(x):
    shares = lax.axis_size(BUS)
    x = x.reshape(shares, x.shape[0] // shares, x.shape[1])
    return jnp.sum(lax.all_to_all(x, BUS, 0, 0, tiled=True), axis=0)


def plain(
    nodal_sensitivity, shift_weight, bus_zone, branch_buses, switched_rows, net_position, flow_limit
):
    rows, cols = nodal_sensitivity.shape
    zones = net_position.shape[0]
    actions, rank = switched_rows.shape
    onehot = (bus_zone[:, None] == jnp.arange(zones)[None, :]).astype(jnp.float32)
    total = sum_over(jnp.sum(onehot * shift_weight[:, None], axis=0), BUS)
    key = (onehot * shift_weight[:, None] / total[None, :]).astype(jnp.bfloat16)
    zonal = jnp.dot(nodal_sensitivity, key, preferred_element_type=jnp.float32)
    picks = switched_rows.reshape(-1)

    def columns(buses):
        local = buses - lax.axis_index(BUS) * cols
        owned = (local >= 0) & (local < cols)
        picked = jnp.take(nodal_sensitivity, jnp.clip(local, 0, cols - 1), axis=1)
        return jnp.where(owned[None, :], picked.astype(jnp.float32), 0.0)

    diff = columns(branch_buses[0][picks]) - columns(branch_buses[1][picks])
    zonal, diff = scattered_sum(zonal), scattered_sum(diff)
    share = rows // lax.axis_size(BUS)
    local = picks - lax.axis_index(CNEC) * rows - lax.axis_index(BUS) * share
    owned = ((local >= 0) & (local < share))[:, None]
    local = jnp.clip(local, 0, share - 1)
    switched = jnp.where(owned, jnp.take(zonal, local, axis=0), 0.0)
    coupled = jnp.where(owned, jnp.take(diff, local, axis=0), 0.0)
    coupled = jnp.einsum("aiaj->aij", coupled.reshape(actions, rank, actions, rank))
    both = jnp.concatenate([switched, coupled.reshape(actions * rank, rank)], axis=1)
    both = sum_over(sum_over(both, BUS), CNEC).reshape(actions, rank, zones + rank)
    left, right = jnp.eye(rank, dtype=jnp.float32)[None] - both[:, :, zones:], both[:, :, :zones]
    for pivot in range(rank):
        is_pivot = (jnp.arange(rank) == pivot)[None, :, None]
        factor = left[:, :, pivot:pivot + 1]
        diagonal = factor[:, pivot:pivot + 1]
        left_now, right_now = left[:, pivot:pivot + 1] / diagonal, right[:, pivot:pivot + 1] / diagonal
        left = jnp.where(is_pivot, left_now, left - factor * left_now)
        right = jnp.where(is_pivot, right_now, right - factor * right_now)
    after = zonal[None] + jnp.einsum(
        "caj,ajz->acz", diff.reshape(share, actions, rank), right, precision=HIGHEST
    )
    flow = jnp.einsum("acz,z->ac", after, net_position, precision=HIGHEST)
    return after, flow / flow_limit[None, :], flow_limit[None, :] - jnp.abs(flow)


def solution(mesh):
    n_cnec, n_bus, n_act = mesh.devices.shape
    split = Mesh(
        mesh.devices.reshape(2, n_cnec // 2, n_bus // 2, 2, n_act), ("yl", "x", "z", "yh", "act")
    )
    return jax.shard_map(
        body,
        mesh=split,
        in_specs=(
            P(CNEC, BUS),
            P(BUS),
            P(BUS),
            P(),
            P("act", None),
            P(),
            P(CNEC + BUS),
        ),
        out_specs=(
            P("act", CNEC + BUS, None),
            P("act", CNEC + BUS),
            P("act", CNEC + BUS),
        ),
        check_vma=False,
    )
```
